128 devices in a mesh: ctx: 16 (over y, x), exp: 8 (over z, core).
Axes of the slice: x: 4, y: 4, z: 4, core: 2. Of those that a mesh axis runs over, the one named last changes fastest.
Arguments:
- tokens: bfloat16 [8, 2048, 768], P('exp', 'ctx'), may hold values from -6 to 6
- segment_ids: int32 [8, 2048], P('exp', 'ctx'), may hold values from 0 to 1, never falling along the last dimension, each value on 1 to 1792 neighbouring positions
- buckets: int32 [2048], replicated, may hold values from 0 to 31, as said below
- routes: int32 [8, 2048, 2], P('exp', 'ctx'), may hold values from 0 to 7, all different within a row; in each aligned block of 128 rows (0 to 127, 128 to 255, ..., all dimensions but the last counted through in order) at most 40 rows name the same one
- attention_gain: float32 [768], replicated, may hold values from 0.5 to 1.5
- query_weight: bfloat16 [768, 768], replicated, may hold values from -0.21875 to 0.21875
- key_weight: bfloat16 [768, 768], replicated, may hold values from -0.21875 to 0.21875
- value_weight: bfloat16 [768, 768], replicated, may hold values from -0.21875 to 0.21875
- output_weight: bfloat16 [768, 768], replicated, may hold values from -1.75 to 1.75
- bias_table: float32 [32, 12], replicated, may hold values from -4 to 4
- expert_gain: float32 [768], replicated, may hold values from 0.5 to 1.5
- router_weight: bfloat16 [768, 8], replicated, may hold values from -0.21875 to 0.21875
- expert_up: bfloat16 [768, 8, 3072], P('ctx', 'exp'), may hold values from -0.21875 to 0.21875
- expert_down: bfloat16 [768, 8, 3072], P('ctx', 'exp'), may hold values from -0.109375 to 0.109375
- out_grad: bfloat16 [8, 2048, 768], P('exp', 'ctx'), may hold values from -6 to 6
Outputs:
- layer_out: bfloat16 [8, 2048, 768], P('exp', 'ctx')
- tokens_grad: float32 [8, 2048, 768], P('exp', 'ctx')
- attention_gain_grad: float32 [768], replicated
- query_weight_grad: float32 [768, 768], replicated
- key_weight_grad: float32 [768, 768], replicated
- value_weight_grad: float32 [768, 768], replicated
- output_weight_grad: float32 [768, 768], replicated
- bias_table_grad: float32 [32, 12], replicated
- expert_gain_grad: float32 [768], replicated
- router_weight_grad: float32 [768, 8], replicated
- expert_up_grad: float32 [768, 8, 3072], P('ctx', 'exp')
- expert_down_grad: float32 [768, 8, 3072], P('ctx', 'exp')
The draws below stay inside these ranges and needn't reach their ends.
Inputs may be any that keep to these rules, and one draw needn't show every extreme that they name: buckets[r] is the bucket of relative distance r: 0 at r = 0, never falling as r grows, 31 at r = 2047. `routes`: a token's two experts differ; among the 256 choices of the tokens of one device (aligned blocks of 128 tokens) no expert is named more than 40 times, and in some such blocks one expert is named exactly 40 times. `segment_ids`: within a sequence the numbers never fall; each of the 2 documents holds 1 to 1792 tokens.
All inputs are finite; a program needn't handle non-finite values.
Results may differ from the reference program's by a relative error of at most 0.025.
Values may be sent and summed in bfloat16 or wider, within the bound.
No kernel may reach another device: no remote copies, remote signals or barrier semaphores. Data moves between devices by JAX's collectives and lax.ppermute only.
A program may use at most 128 MiB of HBM per device.

```python
import math
import jax
import jax.numpy as jnp
import numpy as np
from jax import lax

D = 768
HEADS = 12
HEAD_DIM = 64
FF = 3072
NB = 32
DOCS = 2
BLOCK = 128
LENGTH = 2048
SEQS = 8
EXPERTS = 8
CAP = 40
DOC_MOST = 1792
N_CTX = 16


def draw_buckets(key, part):
    stride = LENGTH // NB
    jitter = jax.random.randint(key, (NB - 1,), 0, max(stride // 2, 1))
    edges = (jnp.arange(1, NB, dtype=jnp.int32) * stride + jitter).astype(jnp.int32)
    places = jnp.arange(LENGTH, dtype=jnp.int32)
    level = jnp.sum((places[:, None] >= edges[None, :]).astype(jnp.int32), axis=1)
    return jnp.minimum(level, NB - 1).astype(jnp.int32)


def shard_levels(rng, extent, cuts, low, high):
    factor_of, own = 1.0, jax.random.fold_in(rng, 6)
    for position, blocks in cuts:
        draws = jnp.exp(jax.random.uniform(jax.random.fold_in(own, position), (blocks,), jnp.float32, low / len(cuts), high / len(cuts)))
        factor_of = factor_of * jnp.repeat(draws, extent[position] // blocks).reshape([-1 if axis == position else 1 for axis in range(len(extent))])
    return factor_of


def length_profile(amount, total, reach, lean):
    loads = [(1 << 20) // math.isqrt(standing ** lean) + 1 for standing in range(2, amount + 1)]
    spare, counts = total - reach - (amount - 1), [1] * (amount - 1)
    while spare > 0:
        free = [i for i in range(amount - 1) if counts[i] < reach]
        pool, remaining = sum([loads[i] for i in free]), spare
        for i in free:
            extra = min(reach - counts[i], max(1, remaining * loads[i] // pool), spare)
            counts[i] = counts[i] + extra
            spare = spare - extra
    return np.array([reach] + counts)


def ragged_sizes(key, number_of, total, bound, slope):
    if number_of == 2:
        one = jax.random.randint(key, (), max(1, total - bound), min(bound, total - 1) + 1)
        return jnp.stack([one, total - one])
    lengths = jnp.asarray(length_profile(number_of, total, bound, slope), jnp.int32)
    twos = (number_of - 1) // 2
    giver, receiver = lengths[1:1 + 2 * twos:2], lengths[2:2 + 2 * twos:2]
    margin = jnp.minimum(giver - 1, bound - receiver)
    moved = jax.random.randint(jax.random.fold_in(key, 1), (twos,), 0, 1 << 20) % (margin + 1)
    lengths = lengths.at[1:1 + 2 * twos:2].set(giver - moved).at[2:2 + 2 * twos:2].set(receiver + moved)
    return lengths[jax.random.permutation(jax.random.fold_in(key, 2), number_of)]


def routed_block(key, own, number, rows, count, top, bound, skew):
    ranking = jax.random.permutation(key, count)
    crowded, common = portions_of(count, rows * top, bound, skew, True), portions_of(count, rows * top, bound, skew, False)
    places = jnp.arange(count)

    def named(sizes, offset_by):
        used = int((sizes > 0).sum())
        fixed = max(1, used // 4)
        passed = fixed + (places - fixed + offset_by * (used - fixed)) % max(1, count - fixed)
        return jnp.zeros((count,), jnp.int32).at[ranking[jnp.where(places < fixed, places, passed)]].set(jnp.asarray(sizes, jnp.int32))

    sizes = jnp.where(number % 4 == 0, named(crowded, number // 4), named(common, number - number // 4 - 1))
    mixed = jax.random.permutation(jax.random.fold_in(own, 3), count)
    source_of, sink = mixed[0:count // 2 * 2:2], mixed[1:count // 2 * 2:2]
    room = jnp.minimum(sizes[source_of] - 1, bound - sizes[sink]) // 2
    room = jnp.where((source_of == ranking[0]) | (sink == ranking[0]) | (sizes[sink] == 0), 0, jnp.maximum(room, 0))
    passed = jax.random.randint(jax.random.fold_in(own, 4), (count // 2,), 0, 1 << 20) % (room + 1)
    sizes = sizes.at[source_of].add(-passed).at[sink].add(passed)
    labels = jnp.searchsorted(jnp.cumsum(sizes), jnp.arange(rows * top), side="right").astype(jnp.int32)
    listing = labels.reshape(top, rows).T
    listing = listing[jax.random.permutation(jax.random.fold_in(own, 1), rows)]
    offset_by = jax.random.randint(jax.random.fold_in(own, 2), (rows, 1), 0, top)
    return jnp.take_along_axis(listing, (jnp.arange(top)[None, :] + offset_by) % top, axis=1)


def portions_of(count, total, most, skew, full):
    loads = [(1 << 20) // math.isqrt(standing ** skew) + 1 for standing in range(1, count + 1)]
    largest = most if full else min(most, max(-(-total // count), total * loads[0] // sum(loads)))
    least = 1 if total - largest >= count - 1 else 0
    given, rest = [largest] + [least] * (count - 1), total - largest - least * (count - 1)
    while rest > 0:
        candidates = [i for i in range(1, count) if given[i] < largest] or [i for i in range(1, count) if given[i] < most]
        mass, budget = sum([loads[i] for i in candidates]), rest
        for i in candidates:
            extra = min(most - given[i], max(1, budget * loads[i] // mass), rest)
            given[i] = given[i] + extra
            rest = rest - extra
    return np.array(given)


def noise(rng, extent, spread, reach, shards=(), held_as=jnp.bfloat16):
    drawn = jax.random.normal(rng, extent, jnp.float32) * spread
    if len(shards) > 0:
        drawn = shard_levels(rng, extent, shards, -0.22, 0.18) * drawn
    return jnp.clip(drawn, min=-reach, max=reach).astype(held_as)


def setup_inputs(seed: int = 0) -> dict:
    splits = jax.random.split(jax.random.key(seed), 16)
    tokens = noise(splits[0], (SEQS, LENGTH, D), 1.0, 6.0, ((0, 8), (1, 16)))
    segment_ids = jax.vmap(lambda own: jnp.searchsorted(jnp.cumsum(ragged_sizes(own, DOCS, LENGTH, DOC_MOST, 1)), jnp.arange(LENGTH), side="right"))(jax.random.split(splits[1], SEQS)).reshape((SEQS, LENGTH)).astype(jnp.int32)
    buckets = draw_buckets(jax.random.fold_in(splits[15], 71), 0)
    routes_keys = jax.random.split(jax.random.fold_in(splits[3], 1), SEQS * LENGTH // BLOCK)
    routes_turns = jax.random.permutation(jax.random.fold_in(splits[3], 3), SEQS * LENGTH // BLOCK)
    routes = jax.vmap(lambda own, number: routed_block(jax.random.fold_in(splits[3], 2), own, number, BLOCK, EXPERTS, 2, CAP, 0))(routes_keys, routes_turns).reshape((SEQS, LENGTH, 2))
    attention_gain = jnp.clip(1.0 + 0.1 * jax.random.normal(splits[4], (D,), jnp.float32), 0.5, 1.5)
    query_weight = noise(splits[5], (D, D), D ** -0.5, 0.21875)
    key_weight = noise(splits[6], (D, D), D ** -0.5, 0.21875)
    value_weight = noise(splits[7], (D, D), D ** -0.5, 0.21875)
    output_weight = noise(splits[8], (D, D), (D // 64) ** -0.5, 1.75)
    bias_table = noise(splits[9], (NB, HEADS), 1.0, 4.0, (), jnp.float32)
    expert_gain = jnp.clip(1.0 + 0.1 * jax.random.normal(splits[10], (D,), jnp.float32), 0.5, 1.5)
    router_weight = noise(splits[11], (D, EXPERTS), D ** -0.5, 0.21875)
    expert_up = noise(splits[12], (D, EXPERTS, FF), D ** -0.5, 0.21875, ((0, 16), (1, 8)))
    expert_down = noise(splits[13], (D, EXPERTS, FF), FF ** -0.5, 0.109375, ((0, 16), (1, 8)))
    out_grad = noise(splits[14], (SEQS, LENGTH, D), 1.0, 6.0, ((0, 8), (1, 16)))
    return dict(tokens=tokens, segment_ids=segment_ids, buckets=buckets, routes=routes, attention_gain=attention_gain, query_weight=query_weight, key_weight=key_weight, value_weight=value_weight, output_weight=output_weight, bias_table=bias_table, expert_gain=expert_gain, router_weight=router_weight, expert_up=expert_up, expert_down=expert_down, out_grad=out_grad)


@jax.custom_vjp
def low(v):
    return lax.optimization_barrier(v.astype(jnp.bfloat16)).astype(jnp.float32)

@jax.custom_vjp
def low_back(v):
    return v

def low_keep(v):
    return (low(v), None)

def low_pass(kept, grad):
    return (grad,)

def back_keep(v):
    return (v, None)

def back_low(kept, grad):
    return (low(grad),)
low.defvjp(low_keep, low_pass)
low_back.defvjp(back_keep, back_low)
EPS = 1e-06
NEG = -1e+30
HIGH = lax.Precision.HIGHEST

def matmul(left, right):
    return jnp.dot(left, right, precision=HIGH, preferred_element_type=jnp.float32)

def rms_norm(value, gain):
    return value * lax.rsqrt(lax.optimization_barrier(jnp.mean(value * value, axis=-1, keepdims=True)) + EPS) * gain

def attend_sequence(queries, keys, values, segment, bias_dist):
    span = math.gcd(LENGTH, 512)
    count = LENGTH // span
    key_heads = keys.reshape(LENGTH, HEADS, HEAD_DIM)
    value_heads = values.reshape(LENGTH, HEADS, HEAD_DIM)
    positions = jnp.arange(LENGTH, dtype=jnp.int32)

    def one_block(inputs):
        query_block, seg_block, pos_block = inputs
        distance = pos_block[:, None] - positions[None, :]
        allowed = (distance >= 0) & (seg_block[:, None] == segment[None, :])
        bias = jnp.take(bias_dist, jnp.clip(distance, 0, LENGTH - 1).astype(jnp.int32), axis=1)
        query_heads = query_block.reshape(span, HEADS, HEAD_DIM)
        scores = jnp.einsum('qhd,khd->hqk', query_heads, key_heads, precision=HIGH) * HEAD_DIM ** (-0.5) + bias
        scores = low_back(scores)
        scores = jnp.where(allowed[None], scores, NEG)
        probs = low(jax.nn.softmax(scores, axis=-1))
        result = jnp.einsum('hqk,khd->qhd', probs, value_heads, precision=HIGH)
        return result.reshape(span, HEADS * HEAD_DIM)
    blocks = (queries.reshape(count, span, HEADS * HEAD_DIM), segment.reshape(count, span), positions.reshape(count, span))
    return lax.map(jax.checkpoint(one_block), blocks).reshape(LENGTH, HEADS * HEAD_DIM)

def reference(tokens, segment_ids, buckets, routes, attention_gain, query_weight, key_weight, value_weight, output_weight, bias_table, expert_gain, router_weight, expert_up, expert_down, out_grad):
    total = SEQS * LENGTH
    blocks = SEQS * N_CTX
    pairs = routes.reshape(blocks, 2 * BLOCK).astype(jnp.int32)
    hot = (pairs[:, :, None] == jnp.arange(EXPERTS, dtype=jnp.int32)[None, None, :]).astype(jnp.int32)
    earlier = jnp.cumsum(hot, axis=1) - hot
    slots = lax.optimization_barrier(jnp.sum(hot * earlier, axis=2)).reshape(-1).astype(jnp.int32)
    pair_expert = pairs.reshape(-1)
    pair_block = (jnp.arange(blocks * 2 * BLOCK, dtype=jnp.int32) // (2 * BLOCK)).astype(jnp.int32)
    owners = (jnp.arange(total * 2, dtype=jnp.int32) // 2).astype(jnp.int32)
    routed = routes.reshape(total, 2).astype(jnp.int32)

    def forward(inputs, gain_one, wq_full, wk_full, wv_full, wo_full, table, gain_two, router, up_full, down_full):
        flat = inputs.reshape(total, D)
        hidden_one = low(rms_norm(flat, gain_one))
        queries = low_back(low(matmul(hidden_one, wq_full)))
        keys = low_back(low(matmul(hidden_one, wk_full)))
        values = low_back(low(matmul(hidden_one, wv_full)))
        bias_dist = jnp.take(table, buckets, axis=0).T

        def per_sequence(items):
            return attend_sequence(items[0], items[1], items[2], items[3], bias_dist)
        attended = lax.map(per_sequence, (queries.reshape(SEQS, LENGTH, D), keys.reshape(SEQS, LENGTH, D), values.reshape(SEQS, LENGTH, D), segment_ids))
        attended = low_back(low(attended.reshape(total, D)))
        residual = flat + low_back(matmul(attended, wo_full))
        hidden_two = low(rms_norm(residual, gain_two))
        logits = matmul(hidden_two, router)
        picked_logits = jnp.take_along_axis(logits, routed, axis=1)
        gates = jax.nn.softmax(picked_logits, axis=-1)
        buffer = jnp.zeros((EXPERTS, blocks, CAP, D), jnp.float32)
        buffer = buffer.at[pair_expert, pair_block, slots].set(hidden_two[owners])
        buffer = low_back(buffer)

        def run_expert(items):
            rows, weight_up, weight_down = items
            pre_act = low_back(matmul(rows, weight_up))
            hidden_act = low(jax.nn.gelu(pre_act))
            return low_back(low(matmul(hidden_act, weight_down.T)))
        outputs = lax.map(jax.checkpoint(run_expert), (buffer.reshape(EXPERTS, blocks * CAP, D), jnp.transpose(up_full, (1, 0, 2)), jnp.transpose(down_full, (1, 0, 2))))
        outputs = outputs.reshape(EXPERTS, blocks, CAP, D)
        pair_out = outputs[pair_expert, pair_block, slots].reshape(total, 2, D)
        mixed = lax.optimization_barrier(jnp.sum(gates[:, :, None] * pair_out, axis=1))
        return (residual + mixed).reshape(SEQS, LENGTH, D)
    floats = (tokens.astype(jnp.float32), attention_gain.astype(jnp.float32), query_weight.astype(jnp.float32), key_weight.astype(jnp.float32), value_weight.astype(jnp.float32), output_weight.astype(jnp.float32), bias_table.astype(jnp.float32), expert_gain.astype(jnp.float32), router_weight.astype(jnp.float32), expert_up.astype(jnp.float32), expert_down.astype(jnp.float32))
    result, pullback = jax.vjp(forward, *floats)
    grads = pullback(out_grad.astype(jnp.float32))
    return (result.astype(jnp.bfloat16), grads[0], grads[1], grads[2], grads[3], grads[4], grads[5], grads[6], grads[7], grads[8], grads[9], grads[10])
```

```python
import jax
import jax.numpy as jnp
from jax import lax
from jax.experimental import pallas as pl
from jax.experimental.pallas import tpu as pltpu
from jax.sharding import PartitionSpec as P

HEADS = 12
HEAD_DIM = 64
EPS = 1e-06
NEG = -1e30
BIG = 2.0**99
SCALE = HEAD_DIM ** (-0.5)
AUG = 16
ROWS = 256
f32 = jnp.float32
bf16 = jnp.bfloat16
MB = 1024 * 1024


def nn(a, b):
    return lax.dot_general(a, b, (((1,), (0,)), ((), ())), preferred_element_type=f32)


def nt(a, b):
    return lax.dot_general(a, b, (((1,), (1,)), ((), ())), preferred_element_type=f32)


def tn(a, b):
    return lax.dot_general(a, b, (((0,), (0,)), ((), ())), preferred_element_type=f32)


def call(kernel, out_shape, vmem=48, flops=0, moved=0, **kw):
    return pl.pallas_call(
        kernel,
        out_shape=out_shape,
        compiler_params=pltpu.CompilerParams(vmem_limit_bytes=vmem * MB),
        cost_estimate=pl.CostEstimate(flops=flops, bytes_accessed=moved, transcendentals=0),
        **kw,
    )


def sds(shape, dtype):
    return jax.ShapeDtypeStruct(shape, dtype)


def inv_rms(value):
    return lax.rsqrt(jnp.mean(value * value, axis=-1, keepdims=True) + EPS)


def project_kernel(tok_ref, gain_ref, seg_ref, wq_ref, wk_ref, wv_ref, out_ref, hid_ref):
    x = tok_ref[...].astype(f32)
    hidden = (x * inv_rms(x) * gain_ref[...]).astype(bf16)
    hid_ref[...] = hidden
    tokens = x.shape[0]
    heads = out_ref.shape[0]

    def put(weight_ref, at, factor):
        t = (nn(hidden, weight_ref[...]).astype(bf16).astype(f32) * factor).T.astype(bf16)
        out_ref[0:HEADS, at : at + HEAD_DIM, :] = t.reshape(HEADS, HEAD_DIM, tokens)
        out_ref[HEADS:, at : at + HEAD_DIM, :] = jnp.zeros((heads - HEADS, HEAD_DIM, tokens), bf16)

    put(wq_ref, 0, SCALE)
    put(wk_ref, HEAD_DIM + AUG, 1.0)
    put(wv_ref, 2 * (HEAD_DIM + AUG), 1.0)
    s = jnp.broadcast_to(seg_ref[...].astype(f32), (AUG, tokens))
    row = lax.broadcasted_iota(jnp.int32, (AUG, tokens), 0)
    q_rows = jnp.where(row == 0, s * BIG, jnp.where(row == 1, (1.0 - s) * BIG, 0.0)).astype(bf16)
    k_rows = jnp.where(
        row == 0, s - 1.0, jnp.where(row == 1, -s, jnp.where(row < 5, 1.0, 0.0))
    ).astype(bf16)
    full = (heads, AUG, tokens)
    out_ref[:, HEAD_DIM : HEAD_DIM + AUG, :] = jnp.broadcast_to(q_rows[None], full)
    out_ref[:, 2 * HEAD_DIM + AUG : 2 * (HEAD_DIM + AUG), :] = jnp.broadcast_to(k_rows[None], full)


QA = HEAD_DIM + AUG
TQ = 256


def bias_tiles(bucket_ref, tab_ref, tile_ref):
    length = bucket_ref.shape[1]
    buckets = bucket_ref[...]
    nb = tab_ref.shape[0]
    hot = jnp.broadcast_to(buckets, (nb, length)) == lax.broadcasted_iota(
        jnp.int32, (nb, length), 0
    )
    b = jnp.sum(jnp.where(hot, tab_ref[...], 0.0), axis=0, keepdims=True)
    w = jnp.concatenate([jnp.full((1, TQ), NEG, f32), b], axis=1)
    x = jnp.broadcast_to(w, (8, length + TQ))
    row = lax.broadcasted_iota(jnp.int32, x.shape, 0)
    for bit in (1, 2, 4):
        x = jnp.where((row & bit) > 0, pltpu.roll(x, bit, axis=1), x)
    for bit in (8, 16, 32, 64):
        x = jnp.concatenate([x, pltpu.roll(x, bit, axis=1)], axis=0)
    for d in range(length // TQ):
        at = (d + 1) * TQ
        tile_ref[d, 0:128, :] = x[:, at : at + TQ]
        tile_ref[d, 128:256, :] = x[:, at - 128 : at - 128 + TQ]


def transposed(block):
    return block.astype(f32).T.astype(bf16)


def pair(ref, index, at, size):
    return jnp.concatenate(
        [ref[2 * index, at : at + size, :], ref[2 * index + 1, at : at + size, :]], axis=1
    )


def boundary(recv_ref):
    ones = recv_ref[:, QA + HEAD_DIM : QA + HEAD_DIM + AUG, :].astype(f32)
    row = lax.broadcasted_iota(jnp.int32, ones.shape, 1)
    total = jnp.sum(jnp.where(row == 1, ones, 0.0))
    return recv_ref.shape[0] * recv_ref.shape[2] + total.astype(jnp.int32)


def first_tile(qb, edge):
    return jnp.where(qb * TQ >= edge, edge // TQ, 0)


def attend_kernel(recv_ref, bucket_ref, tab_ref, ot_ref, otf_ref, lse_ref, kn_ref, tile_ref):
    blocks = recv_ref.shape[0]
    bias_tiles(bucket_ref, tab_ref, tile_ref)
    for c in range(blocks):
        kn_ref[c // 2, (c % 2) * 128 : (c % 2) * 128 + 128, :] = transposed(
            recv_ref[c, QA : 2 * QA, :]
        )
    edge = boundary(recv_ref)

    def one_query_tile(qb, carry):
        qt = pair(recv_ref, qb, 0, QA)

        def one_key_tile(i, state):
            top, total, acc = state
            kb = qb - i
            s = nn(kn_ref[kb], qt) + tile_ref[i]
            new_top = jnp.maximum(top, jnp.max(s, axis=0, keepdims=True))
            p = jnp.exp(s - new_top)
            factor = jnp.exp(top - new_top)
            total = total * factor + jnp.sum(p, axis=0, keepdims=True)
            acc = acc * factor + nn(pair(recv_ref, kb, 2 * QA, HEAD_DIM), p.astype(bf16))
            return new_top, total, acc

        start = (jnp.full((1, TQ), NEG, f32), jnp.zeros((1, TQ), f32), jnp.zeros((HEAD_DIM, TQ), f32))
        top, total, acc = lax.fori_loop(0, qb - first_tile(qb, edge) + 1, one_key_tile, start)
        o = acc / total
        otf_ref[qb] = o
        lse_ref[qb] = top + jnp.log(total)
        low = o.astype(bf16)
        ot_ref[2 * qb] = low[:, :128]
        ot_ref[2 * qb + 1] = low[:, 128:]
        return carry

    lax.fori_loop(0, blocks // 2, one_query_tile, 0)


def attend_back_kernel(
    recv_ref, gt_ref, otf_ref, lse_ref, bucket_ref, tab_ref,
    out_ref, flat_ref, bias_ref,
    kn_ref, vn_ref, tile_ref, dtile_ref, dk_ref, dv_ref,
):
    blocks = recv_ref.shape[0]
    tiles = blocks // 2
    bias_tiles(bucket_ref, tab_ref, tile_ref)
    for c in range(blocks):
        at = (c % 2) * 128
        kn_ref[c // 2, at : at + 128, :] = transposed(recv_ref[c, QA : 2 * QA, :])
        vn_ref[c // 2, at : at + 128, :] = transposed(recv_ref[c, 2 * QA : 2 * QA + HEAD_DIM, :])
    edge = boundary(recv_ref)
    dtile_ref[...] = jnp.zeros_like(dtile_ref)
    dk_ref[...] = jnp.zeros_like(dk_ref)
    dv_ref[...] = jnp.zeros_like(dv_ref)

    def one_query_tile(qb, carry):
        qt = pair(recv_ref, qb, 0, QA)
        gt = pair(gt_ref, qb, 0, HEAD_DIM)
        lse = lse_ref[qb]
        delta = jnp.sum(gt.astype(f32) * otf_ref[qb], axis=0, keepdims=True)

        def one_key_tile(i, acc):
            kb = qb - i
            p = jnp.exp(nn(kn_ref[kb], qt) + tile_ref[i] - lse)
            dp = nn(vn_ref[kb], gt)
            ds = (p * (dp - delta)).astype(bf16)
            dtile_ref[i] += ds.astype(f32)
            dv_ref[kb] += nt(gt, p.astype(bf16))
            dk_ref[kb] += nt(qt[:HEAD_DIM], ds)
            return acc + nn(pair(recv_ref, kb, QA, HEAD_DIM), ds)

        acc = lax.fori_loop(
            0, qb - first_tile(qb, edge) + 1, one_key_tile, jnp.zeros((HEAD_DIM, TQ), f32)
        )
        low = (acc * SCALE).astype(bf16)
        out_ref[2 * qb, 0:HEAD_DIM, :] = low[:, :128]
        out_ref[2 * qb + 1, 0:HEAD_DIM, :] = low[:, 128:]
        return carry

    lax.fori_loop(0, tiles, one_query_tile, 0)
    for kb in range(tiles):
        for ref, at in ((dk_ref, HEAD_DIM), (dv_ref, 2 * HEAD_DIM)):
            low = ref[kb].astype(bf16)
            out_ref[2 * kb, at : at + HEAD_DIM, :] = low[:, :128]
            out_ref[2 * kb + 1, at : at + HEAD_DIM, :] = low[:, 128:]
    for c in range(blocks):
        flat_ref[:, c * 128 : (c + 1) * 128] = out_ref[c]
    upper = jnp.concatenate([dtile_ref[d, 0:128, :] for d in range(tiles)], axis=1)
    lower = jnp.concatenate([dtile_ref[d, 128:256, :] for d in range(tiles)], axis=1)
    pad = jnp.zeros((128, 128), f32)
    x = jnp.concatenate([pad, pad, upper], axis=1) + jnp.concatenate([pad, lower, pad], axis=1)
    wide = x.shape[1]
    for half in (64, 32, 16, 8, 4, 2, 1):
        x = x[0:half] + pltpu.roll(x[half : 2 * half], wide - half, axis=1)
    g = x[:, TQ:]
    nb, length = tab_ref.shape[0], bucket_ref.shape[1]
    hot = jnp.broadcast_to(bucket_ref[...], (nb, length)) == lax.broadcasted_iota(
        jnp.int32, (nb, length), 0
    )
    sums = jnp.sum(jnp.where(hot, jnp.broadcast_to(g, (nb, length)), 0.0), axis=1, keepdims=True)
    column = jnp.concatenate([jnp.broadcast_to(sums, (nb, 128)), jnp.zeros((128 - nb, 128), f32)], axis=0)
    bias_ref[...] = column.T[0:8, :]


def route_kernel(
    ot_ref, tok_ref, wo_ref, gain_ref, router_ref, rt_ref, rcol_ref, grad_ref,
    send_ref, res_ref, gate_ref, hid_ref,
):
    tokens, width = tok_ref.shape
    experts = router_ref.shape[1]
    slots_all = send_ref.shape[0]
    capacity = slots_all // experts
    att = ot_ref[0:HEADS].reshape(width, tokens)
    residual = tok_ref[...].astype(f32) + tn(att, wo_ref[...])
    res_ref[...] = residual
    hidden = (residual * inv_rms(residual) * gain_ref[...]).astype(bf16)
    hid_ref[...] = hidden
    logits = nn(hidden, router_ref[...])
    expert_lane = lax.broadcasted_iota(jnp.int32, (tokens, experts), 1)
    picked = [
        jnp.sum(jnp.where(expert_lane == rcol_ref[:, c : c + 1], logits, 0.0), axis=1, keepdims=True)
        for c in (0, 1)
    ]
    top = jnp.maximum(picked[0], picked[1])
    e0, e1 = jnp.exp(picked[0] - top), jnp.exp(picked[1] - top)
    gates = [e0 / (e0 + e1), e1 / (e0 + e1)]
    gate_ref[...] = jnp.concatenate(
        [jnp.broadcast_to(g, (tokens, 128)) for g in gates], axis=1
    )
    expert_row = lax.broadcasted_iota(jnp.int32, (experts, tokens), 0)
    before = (
        lax.broadcasted_iota(jnp.int32, (tokens, tokens), 0)
        < lax.broadcasted_iota(jnp.int32, (tokens, tokens), 1)
    ).astype(bf16)
    slot_row = lax.broadcasted_iota(jnp.int32, (slots_all, tokens), 0)
    hots = [(expert_row == rt_ref[c : c + 1, :]).astype(f32) for c in (0, 1)]
    counts = jnp.sum(hots[0], axis=1, keepdims=True)
    taken = [nn(hots[0].astype(bf16), before), nn(hots[1].astype(bf16), before) + counts]
    to_slot = []
    for c in (0, 1):
        slot = jnp.sum(hots[c] * taken[c], axis=0, keepdims=True).astype(jnp.int32)
        place = rt_ref[c : c + 1, :] * capacity + slot
        to_slot.append((slot_row == place).astype(bf16))
    send_ref[:, 0:width] = nn(to_slot[0] + to_slot[1], hidden).astype(bf16)
    upstream = grad_ref[...].astype(f32)
    weighted = jnp.concatenate([(g * upstream).astype(bf16) for g in gates], axis=0)
    send_ref[:, width:] = nn(jnp.concatenate(to_slot, axis=1), weighted).astype(bf16)


def combine_kernel(
    ret_ref, res_ref, grad_ref, gate_ref, hid_ref, rcol_ref, gain_ref, router_t_ref, wo_ref, ot_ref,
    layer_ref, rgrad_ref, gt_ref, wo_grad_ref, small_ref,
):
    tokens, width = res_ref.shape
    experts = router_t_ref.shape[0]
    slots_all = ret_ref.shape[0]
    capacity = slots_all // experts
    lane = lax.broadcasted_iota(jnp.int32, (tokens, 128), 1)
    earlier = (
        lax.broadcasted_iota(jnp.int32, (tokens, tokens), 1)
        < lax.broadcasted_iota(jnp.int32, (tokens, tokens), 0)
    ).astype(bf16)
    hots = [(lane == rcol_ref[:, c : c + 1]).astype(f32) for c in (0, 1)]
    counts = jnp.sum(hots[0], axis=0, keepdims=True)
    taken = [nn(earlier, hots[0].astype(bf16)), nn(earlier, hots[1].astype(bf16)) + counts]
    slot_lane = lax.broadcasted_iota(jnp.int32, (tokens, slots_all), 1)
    from_slot = []
    for c in (0, 1):
        slot = jnp.sum(hots[c] * taken[c], axis=1, keepdims=True).astype(jnp.int32)
        place = rcol_ref[:, c : c + 1] * capacity + slot
        from_slot.append((slot_lane == place).astype(bf16))
    outs = [nn(m, ret_ref[:, 0:width]) for m in from_slot]
    row_sum = nn(from_slot[0] + from_slot[1], ret_ref[:, width:])
    gates = [gate_ref[:, 0:1], gate_ref[:, 128:129]]
    residual = res_ref[...]
    layer_ref[...] = (residual + (gates[0] * outs[0] + gates[1] * outs[1])).astype(bf16)
    upstream = grad_ref[...].astype(f32)
    gate_grads = [jnp.sum(upstream * o, axis=1, keepdims=True) for o in outs]
    mixed = gates[0] * gate_grads[0] + gates[1] * gate_grads[1]
    logit_grad = (
        gates[0] * (gate_grads[0] - mixed) * hots[0] + gates[1] * (gate_grads[1] - mixed) * hots[1]
    )
    h2g = row_sum
    for e in range(experts):
        h2g = h2g + logit_grad[:, e : e + 1] * router_t_ref[e : e + 1, :]
    inverse = inv_rms(residual)
    normed = residual * inverse
    logit_t = logit_grad.T
    high = logit_t.astype(bf16)
    rest = (logit_t - high.astype(f32)).astype(bf16)
    router_grad = nn(high, hid_ref[...]) + nn(rest, hid_ref[...])
    small_ref[0:8, :] = jnp.broadcast_to(jnp.sum(h2g * normed, axis=0, keepdims=True), (8, width))
    small_ref[8:16, :] = router_grad[0:experts]
    scaled = h2g * gain_ref[...]
    average = jnp.mean(scaled * normed, axis=-1, keepdims=True)
    residual_grad = upstream + inverse * (scaled - normed * average)
    rgrad_ref[...] = residual_grad
    branch = residual_grad.astype(bf16)
    gt = nt(wo_ref[...], branch).astype(bf16)
    gt_ref[0:HEADS] = gt.reshape(HEADS, HEAD_DIM, tokens)
    gt_ref[HEADS:] = jnp.zeros((gt_ref.shape[0] - HEADS, HEAD_DIM, tokens), bf16)
    att = ot_ref[0:HEADS].reshape(width, tokens)
    wo_grad_ref[...] = nn(att, branch).astype(bf16)


def expert_kernel(rows_ref, up_ref, down_ref, ret_ref, pre_ref, act_ref, out_acc, row_acc):
    step = pl.program_id(0)
    width = up_ref.shape[0]
    rows = rows_ref[:, 0:width]
    grads = rows_ref[:, width:]
    up, down = up_ref[...], down_ref[...]
    x = nn(rows, up)
    c = 0.7978845608028654
    t = jnp.tanh(c * (x + 0.044715 * (x * x * x)))
    hidden = (0.5 * x * (1.0 + t)).astype(bf16)
    slope = 0.5 * (1.0 + t) + 0.5 * x * (1.0 - t * t) * (c * (1.0 + 3 * 0.044715 * (x * x)))
    pre = (nn(grads, down) * slope).astype(bf16)
    act_ref[...] = hidden
    pre_ref[...] = pre
    out_part, row_part = nt(hidden, down), nt(pre, up)

    @pl.when(step == 0)
    def _():
        out_acc[...] = out_part
        row_acc[...] = row_part

    @pl.when(step > 0)
    def _():
        out_acc[...] += out_part
        row_acc[...] += row_part

    @pl.when(step == pl.num_programs(0) - 1)
    def _():
        ret_ref[:, 0:width] = out_acc[...].astype(bf16)
        ret_ref[:, width:] = row_acc[...].astype(bf16)


def expert_grad_kernel(rows_ref, pre_ref, act_ref, out_ref, left_ref):
    step = pl.program_id(0)
    steps = pl.num_programs(0)
    width = out_ref.shape[0]

    @pl.when(step == 0)
    def _():
        left_ref[...] = rows_ref[:, 0:width].astype(f32).T.astype(bf16)

    @pl.when(step == steps // 2)
    def _():
        left_ref[...] = rows_ref[:, width:].astype(f32).T.astype(bf16)

    @pl.when(step < steps // 2)
    def _():
        out_ref[...] = nn(left_ref[...], pre_ref[...]).astype(bf16)

    @pl.when(step >= steps // 2)
    def _():
        out_ref[...] = nn(left_ref[...], act_ref[...]).astype(bf16)


def pack_kernel(flat_ref, hid_ref, wt_ref, gain_ref, wo_ref, small_ref, bias_ref, out_ref):
    width = hid_ref.shape[1]
    grad = nn(flat_ref[...], hid_ref[...])
    part = jnp.sum(grad * wt_ref[...].astype(f32), axis=0, keepdims=True) / gain_ref[...]
    out_ref[0:192, :] = grad.astype(bf16)
    wo = wo_ref[0].astype(f32)
    for c in range(1, wo_ref.shape[0]):
        wo = wo + wo_ref[c].astype(f32)
    out_ref[192:240, :] = wo.astype(bf16)
    bias = jnp.concatenate([bias_ref[...], jnp.zeros((8, width - 128), f32)], axis=1)
    row = lax.broadcasted_iota(jnp.int32, (8, width), 0)
    first = jnp.where(
        row == 0, jnp.broadcast_to(part, (8, width)), jnp.where(row == 1, small_ref[0:8, :], bias)
    )
    out_ref[240:256, :] = jnp.concatenate([first, small_ref[8:16, :]], axis=0).astype(bf16)


def tokens_kernel(recv_ref, tok_ref, gain_ref, rgrad_ref, wq_ref, wk_ref, wv_ref, out_ref):
    tokens, width = tok_ref.shape
    acc = None
    for weight_ref, at in ((wq_ref, 0), (wk_ref, HEAD_DIM), (wv_ref, 2 * HEAD_DIM)):
        grad = recv_ref[0:HEADS, at : at + HEAD_DIM, :].reshape(width, tokens)
        part = nn(weight_ref[...], grad)
        acc = part if acc is None else acc + part
    hidden_grad = acc.T
    x = tok_ref[...].astype(f32)
    inverse = inv_rms(x)
    normed = x * inverse
    scaled = hidden_grad * gain_ref[...]
    average = jnp.mean(scaled * normed, axis=-1, keepdims=True)
    out_ref[...] = rgrad_ref[...] + inverse * (scaled - normed * average)


def unpack_kernel(all_ref, q_ref, k_ref, v_ref):
    for ref, at in ((q_ref, 0), (k_ref, HEAD_DIM), (v_ref, 2 * HEAD_DIM)):
        both = jnp.concatenate(
            [all_ref[0, at : at + HEAD_DIM, :], all_ref[1, at : at + HEAD_DIM, :]], axis=0
        )
        ref[...] = both.astype(f32).T


def on_device(
    tokens, segment_ids, buckets, routes, attention_gain, query_weight, key_weight, value_weight,
    output_weight, bias_table, expert_gain, router_weight, expert_up, expert_down, out_grad,
):
    n_ctx, n_exp = lax.axis_size("ctx"), lax.axis_size("exp")
    rows, width = tokens.shape[1:]
    length = buckets.shape[0]
    experts = router_weight.shape[1]
    capacity = 5 * rows // (2 * experts)
    slots = experts * capacity
    hidden_units = expert_up.shape[2]
    head = lax.axis_index("ctx")
    gain_one = attention_gain.reshape(1, width)
    gain_two = expert_gain.reshape(1, width)
    bucket_row = buckets.reshape(1, length)
    table = jnp.pad(bias_table, ((0, 0), (0, n_ctx - HEADS)))
    tab = lax.dynamic_slice_in_dim(table, head, 1, axis=1)

    up_down = jnp.concatenate([expert_up[:, 0], expert_down[:, 0]], axis=1)
    weights = lax.all_gather(up_down, "ctx", axis=0, tiled=True)

    x = tokens[0]
    qkv, hidden = call(
        project_kernel,
        (sds((n_ctx, 2 * QA + HEAD_DIM, rows), bf16), sds((rows, width), bf16)),
        flops=6 * rows * width * width,
        moved=4 * MB,
    )(x, gain_one, segment_ids, query_weight, key_weight, value_weight)
    qkv = lax.all_to_all(qkv, "ctx", split_axis=0, concat_axis=0, tiled=True)
    hidden_all = lax.all_gather(hidden, "ctx", axis=0, tiled=True)

    tiles = length // TQ
    ot, otf, lse = call(
        attend_kernel,
        (
            sds((n_ctx, HEAD_DIM, rows), bf16),
            sds((tiles, HEAD_DIM, TQ), f32),
            sds((tiles, 1, TQ), f32),
        ),
        scratch_shapes=[pltpu.VMEM((tiles, TQ, QA), bf16), pltpu.VMEM((tiles, TQ, TQ), f32)],
        flops=8 * 10**9,
        moved=10 * MB,
    )(qkv, bucket_row, tab)
    ot = lax.all_to_all(ot, "ctx", split_axis=0, concat_axis=0, tiled=True)

    routed = routes[0]
    grads_in = out_grad[0]
    send, residual, gates, hidden_two = call(
        route_kernel,
        (
            sds((slots, 2 * width), bf16),
            sds((rows, width), f32),
            sds((rows, 256), f32),
            sds((rows, width), bf16),
        ),
        flops=10**9,
        moved=4 * MB,
    )(ot, x, output_weight, gain_two, router_weight, routed.T, routed, grads_in)
    received = lax.all_to_all(send, "exp", split_axis=0, concat_axis=0, tiled=True)

    chunk = 512
    steps = hidden_units // chunk
    whole = lambda shape: pl.BlockSpec(shape, lambda i: (0, 0))
    result, pre, act = call(
        expert_kernel,
        (
            sds((slots, 2 * width), bf16),
            sds((slots, hidden_units), bf16),
            sds((slots, hidden_units), bf16),
        ),
        grid=(steps,),
        in_specs=[
            whole((slots, 2 * width)),
            pl.BlockSpec((width, chunk), lambda i: (0, i)),
            pl.BlockSpec((width, chunk), lambda i: (0, steps + i)),
        ],
        out_specs=[
            whole((slots, 2 * width)),
            pl.BlockSpec((slots, chunk), lambda i: (0, i)),
            pl.BlockSpec((slots, chunk), lambda i: (0, i)),
        ],
        scratch_shapes=[pltpu.VMEM((slots, width), f32), pltpu.VMEM((slots, width), f32)],
        flops=8 * slots * width * hidden_units,
        moved=16 * MB,
    )(received, weights, weights)
    returned = lax.all_to_all(result, "exp", split_axis=0, concat_axis=0, tiled=True)
    weight_grads = call(
        expert_grad_kernel,
        sds((width, 2 * hidden_units), bf16),
        grid=(2 * steps,),
        in_specs=[
            whole((slots, 2 * width)),
            pl.BlockSpec((slots, chunk), lambda i: (0, jnp.minimum(i, steps - 1))),
            pl.BlockSpec((slots, chunk), lambda i: (0, jnp.maximum(i - steps, 0))),
        ],
        out_specs=pl.BlockSpec((width, chunk), lambda i: (0, i)),
        scratch_shapes=[pltpu.VMEM((width, slots), bf16)],
        flops=4 * slots * width * hidden_units,
        moved=16 * MB,
    )(received, pre, act)
    returned, weight_grads = lax.optimization_barrier((returned, weight_grads))
    summed = lax.psum_scatter(weight_grads, "ctx", scatter_dimension=0, tiled=True)

    layer_out, residual_grad, gt, wo_grad, small = call(
        combine_kernel,
        (
            sds((rows, width), bf16),
            sds((rows, width), f32),
            sds((n_ctx, HEAD_DIM, rows), bf16),
            sds((width, width), bf16),
            sds((16, width), f32),
        ),
        flops=10**9,
        moved=6 * MB,
    )(
        returned, residual, grads_in, gates, hidden_two, routed, gain_two,
        router_weight.astype(f32).T, output_weight, ot,
    )
    gt = lax.all_to_all(gt, "ctx", split_axis=0, concat_axis=0, tiled=True)
    wo_parts = lax.all_to_all(
        wo_grad.reshape(n_ctx, width // n_ctx, width), "ctx", split_axis=0, concat_axis=0, tiled=True
    )

    dqkv, flat, bias_grad = call(
        attend_back_kernel,
        (
            sds((n_ctx, 3 * HEAD_DIM, rows), bf16),
            sds((3 * HEAD_DIM, length), bf16),
            sds((8, 128), f32),
        ),
        scratch_shapes=[
            pltpu.VMEM((tiles, TQ, QA), bf16),
            pltpu.VMEM((tiles, TQ, HEAD_DIM), bf16),
            pltpu.VMEM((tiles, TQ, TQ), f32),
            pltpu.VMEM((tiles, TQ, TQ), f32),
            pltpu.VMEM((tiles, HEAD_DIM, TQ), f32),
            pltpu.VMEM((tiles, HEAD_DIM, TQ), f32),
        ],
        flops=20 * 10**9,
        moved=20 * MB,
    )(qkv, gt, otf, lse, bucket_row, tab)

    at = jnp.minimum(head, HEADS - 1) * HEAD_DIM
    own_weights = jnp.concatenate(
        [
            lax.dynamic_slice_in_dim(w, at, HEAD_DIM, axis=1).T
            for w in (query_weight, key_weight, value_weight)
        ],
        axis=0,
    )
    packed = call(
        pack_kernel,
        sds((ROWS, width), bf16),
        flops=6 * length * width * HEAD_DIM,
        moved=6 * MB,
    )(flat, hidden_all, own_weights, gain_one, wo_parts, small, bias_grad)
    parts = lax.all_to_all(
        packed.reshape(n_exp, ROWS // n_exp, width), "exp", split_axis=0, concat_axis=0, tiled=True
    )
    share = jnp.sum(parts.astype(f32), axis=0).astype(bf16)
    everything = lax.all_gather(share, ("ctx", "exp"), axis=0, tiled=True)
    everything = everything.reshape(n_ctx, ROWS, width)

    back = lax.all_to_all(dqkv, "ctx", split_axis=0, concat_axis=0, tiled=True)
    tokens_grad = call(
        tokens_kernel,
        sds((rows, width), f32),
        flops=6 * rows * width * width,
        moved=6 * MB,
    )(back, x, gain_one, residual_grad, query_weight, key_weight, value_weight)

    full = sds((width, width), f32)
    column = pl.BlockSpec((width, 128), lambda i: (0, i))
    query_grad, key_grad, value_grad = call(
        unpack_kernel,
        (full, full, full),
        grid=(HEADS // 2,),
        in_specs=[pl.BlockSpec((2, ROWS, width), lambda i: (i, 0, 0))],
        out_specs=[column, column, column],
        moved=16 * MB,
    )(everything)
    output_grad = everything[:, 192:240].reshape(width, width).astype(f32)
    tails = jnp.sum(everything[:, 240:256].astype(f32), axis=0)
    table_grad = everything[:HEADS, 242, : bias_table.shape[0]].astype(f32).T
    return (
        layer_out[None],
        tokens_grad[None],
        tails[0],
        query_grad,
        key_grad,
        value_grad,
        output_grad,
        table_grad,
        tails[1],
        tails[8:].T,
        summed[:, :hidden_units].astype(f32)[:, None],
        summed[:, hidden_units:].astype(f32)[:, None],
    )


def solution(mesh):
    placed = (
        P("exp", "ctx", None),
        P("exp", "ctx"),
        P(),
        P("exp", "ctx", None),
        P(),
        P(),
        P(),
        P(),
        P(),
        P(),
        P(),
        P(),
        P("ctx", "exp", None),
        P("ctx", "exp", None),
        P("exp", "ctx", None),
    )
    return jax.shard_map(
        on_device,
        mesh=mesh,
        in_specs=placed,
        out_specs=(
            P("exp", "ctx", None),
            P("exp", "ctx", None),
            P(),
            P(),
            P(),
            P(),
            P(),
            P(),
            P(),
            P(),
            P("ctx", "exp", None),
            P("ctx", "exp", None),
        ),
        check_vma=False,
    )
```

```python
import jax
import jax.numpy as jnp
from jax import lax
from jax.experimental import pallas as pl
from jax.experimental.pallas import tpu as pltpu
from jax.sharding import PartitionSpec as P

HEADS = 12
HEAD_DIM = 64
EPS = 1e-06
NEG = -1e30
BIG = 2.0**99
SCALE = HEAD_DIM ** (-0.5)
AUG = 16
ROWS = 256
f32 = jnp.float32
bf16 = jnp.bfloat16
MB = 1024 * 1024


def nn(a, b):
    return lax.dot_general(a, b, (((1,), (0,)), ((), ())), preferred_element_type=f32)


def nt(a, b):
    return lax.dot_general(a, b, (((1,), (1,)), ((), ())), preferred_element_type=f32)


def tn(a, b):
    return lax.dot_general(a, b, (((0,), (0,)), ((), ())), preferred_element_type=f32)


def call(kernel, out_shape, vmem=60, flops=0, moved=0, **kw):
    return pl.pallas_call(
        kernel,
        out_shape=out_shape,
        compiler_params=pltpu.CompilerParams(vmem_limit_bytes=vmem * MB),
        cost_estimate=pl.CostEstimate(flops=flops, bytes_accessed=moved, transcendentals=0),
        **kw,
    )


def sds(shape, dtype):
    return jax.ShapeDtypeStruct(shape, dtype)


def inv_rms(value):
    return lax.rsqrt(jnp.mean(value * value, axis=-1, keepdims=True) + EPS)


def project_kernel(tok_ref, gain_ref, seg_ref, wq_ref, wk_ref, wv_ref, out_ref, hid_ref):
    x = tok_ref[...].astype(f32)
    hidden = (x * inv_rms(x) * gain_ref[...]).astype(bf16)
    hid_ref[...] = hidden
    tokens = x.shape[0]
    heads = out_ref.shape[0]

    def put(weight_ref, at, factor):
        t = (nn(hidden, weight_ref[...]).astype(bf16).astype(f32) * factor).T.astype(bf16)
        out_ref[0:HEADS, at : at + HEAD_DIM, :] = t.reshape(HEADS, HEAD_DIM, tokens)
        out_ref[HEADS:, at : at + HEAD_DIM, :] = jnp.zeros((heads - HEADS, HEAD_DIM, tokens), bf16)

    put(wq_ref, 0, SCALE)
    put(wk_ref, HEAD_DIM + AUG, 1.0)
    put(wv_ref, 2 * (HEAD_DIM + AUG), 1.0)
    s = jnp.broadcast_to(seg_ref[...].astype(f32), (AUG, tokens))
    row = lax.broadcasted_iota(jnp.int32, (AUG, tokens), 0)
    q_rows = jnp.where(row == 0, s * BIG, jnp.where(row == 1, (1.0 - s) * BIG, 0.0)).astype(bf16)
    k_rows = jnp.where(
        row == 0, s - 1.0, jnp.where(row == 1, -s, jnp.where(row < 5, 1.0, 0.0))
    ).astype(bf16)
    full = (heads, AUG, tokens)
    out_ref[:, HEAD_DIM : HEAD_DIM + AUG, :] = jnp.broadcast_to(q_rows[None], full)
    out_ref[:, 2 * HEAD_DIM + AUG : 2 * (HEAD_DIM + AUG), :] = jnp.broadcast_to(k_rows[None], full)


QA = HEAD_DIM + AUG
TQ = 256


def bias_tiles(bucket_ref, tab_ref, tile_ref):
    length = bucket_ref.shape[1]
    buckets = bucket_ref[...]
    nb = tab_ref.shape[0]
    hot = jnp.broadcast_to(buckets, (nb, length)) == lax.broadcasted_iota(
        jnp.int32, (nb, length), 0
    )
    b = jnp.sum(jnp.where(hot, tab_ref[...], 0.0), axis=0, keepdims=True)
    w = jnp.concatenate([jnp.full((1, TQ), NEG, f32), b], axis=1)
    x = jnp.broadcast_to(w, (8, length + TQ))
    row = lax.broadcasted_iota(jnp.int32, x.shape, 0)
    for bit in (1, 2, 4):
        x = jnp.where((row & bit) > 0, pltpu.roll(x, bit, axis=1), x)
    for bit in (8, 16, 32, 64):
        x = jnp.concatenate([x, pltpu.roll(x, bit, axis=1)], axis=0)
    for d in range(length // TQ):
        at = (d + 1) * TQ
        tile_ref[d, 0:128, :] = x[:, at : at + TQ]
        tile_ref[d, 128:256, :] = x[:, at - 128 : at - 128 + TQ]


def transposed(block):
    return block.astype(f32).T.astype(bf16)


def pair(ref, index, at, size):
    return jnp.concatenate(
        [ref[2 * index, at : at + size, :], ref[2 * index + 1, at : at + size, :]], axis=1
    )


def boundary(recv_ref):
    ones = recv_ref[:, QA + HEAD_DIM : QA + HEAD_DIM + AUG, :].astype(f32)
    row = lax.broadcasted_iota(jnp.int32, ones.shape, 1)
    total = jnp.sum(jnp.where(row == 1, ones, 0.0))
    return recv_ref.shape[0] * recv_ref.shape[2] + total.astype(jnp.int32)


def first_tile(qb, edge):
    return jnp.where(qb * TQ >= edge, edge // TQ, 0)


def attend_kernel(recv_ref, bucket_ref, tab_ref, ot_ref, otf_ref, lse_ref, kn_ref, tile_ref):
    blocks = recv_ref.shape[0]
    bias_tiles(bucket_ref, tab_ref, tile_ref)
    for c in range(blocks):
        kn_ref[c // 2, (c % 2) * 128 : (c % 2) * 128 + 128, :] = transposed(
            recv_ref[c, QA : 2 * QA, :]
        )
    edge = boundary(recv_ref)

    def one_query_tile(qb, carry):
        qt = pair(recv_ref, qb, 0, QA)

        def one_key_tile(i, state):
            top, total, acc = state
            kb = qb - i
            s = nn(kn_ref[kb], qt) + tile_ref[i]
            new_top = jnp.maximum(top, jnp.max(s, axis=0, keepdims=True))
            p = jnp.exp(s - new_top)
            factor = jnp.exp(top - new_top)
            total = total * factor + jnp.sum(p, axis=0, keepdims=True)
            acc = acc * factor + nn(pair(recv_ref, kb, 2 * QA, HEAD_DIM), p.astype(bf16))
            return new_top, total, acc

        start = (jnp.full((1, TQ), NEG, f32), jnp.zeros((1, TQ), f32), jnp.zeros((HEAD_DIM, TQ), f32))
        top, total, acc = lax.fori_loop(0, qb - first_tile(qb, edge) + 1, one_key_tile, start)
        o = acc / total
        otf_ref[qb] = o
        lse_ref[qb] = top + jnp.log(total)
        low = o.astype(bf16)
        ot_ref[2 * qb] = low[:, :128]
        ot_ref[2 * qb + 1] = low[:, 128:]
        return carry

    lax.fori_loop(0, blocks // 2, one_query_tile, 0)


def attend_back_kernel(
    recv_ref, gt_ref, otf_ref, lse_ref, bucket_ref, tab_ref,
    out_ref, flat_ref, bias_ref,
    kn_ref, vn_ref, tile_ref, dtile_ref, dk_ref, dv_ref,
):
    blocks = recv_ref.shape[0]
    tiles = blocks // 2
    bias_tiles(bucket_ref, tab_ref, tile_ref)
    for c in range(blocks):
        at = (c % 2) * 128
        kn_ref[c // 2, at : at + 128, :] = transposed(recv_ref[c, QA : 2 * QA, :])
        vn_ref[c // 2, at : at + 128, :] = transposed(recv_ref[c, 2 * QA : 2 * QA + HEAD_DIM, :])
    edge = boundary(recv_ref)
    dtile_ref[...] = jnp.zeros_like(dtile_ref)
    dk_ref[...] = jnp.zeros_like(dk_ref)
    dv_ref[...] = jnp.zeros_like(dv_ref)

    def one_query_tile(qb, carry):
        qt = pair(recv_ref, qb, 0, QA)
        gt = pair(gt_ref, qb, 0, HEAD_DIM)
        lse = lse_ref[qb]
        delta = jnp.sum(gt.astype(f32) * otf_ref[qb], axis=0, keepdims=True)

        def one_key_tile(i, acc):
            kb = qb - i
            p = jnp.exp(nn(kn_ref[kb], qt) + tile_ref[i] - lse)
            dp = nn(vn_ref[kb], gt)
            ds = (p * (dp - delta)).astype(bf16)
            dtile_ref[i] += ds.astype(f32)
            dv_ref[kb] += nt(gt, p.astype(bf16))
            dk_ref[kb] += nt(qt[:HEAD_DIM], ds)
            return acc + nn(pair(recv_ref, kb, QA, HEAD_DIM), ds)

        acc = lax.fori_loop(
            0, qb - first_tile(qb, edge) + 1, one_key_tile, jnp.zeros((HEAD_DIM, TQ), f32)
        )
        low = (acc * SCALE).astype(bf16)
        out_ref[2 * qb, 0:HEAD_DIM, :] = low[:, :128]
        out_ref[2 * qb + 1, 0:HEAD_DIM, :] = low[:, 128:]
        return carry

    lax.fori_loop(0, tiles, one_query_tile, 0)
    for kb in range(tiles):
        for ref, at in ((dk_ref, HEAD_DIM), (dv_ref, 2 * HEAD_DIM)):
            low = ref[kb].astype(bf16)
            out_ref[2 * kb, at : at + HEAD_DIM, :] = low[:, :128]
            out_ref[2 * kb + 1, at : at + HEAD_DIM, :] = low[:, 128:]
    for c in range(blocks):
        flat_ref[:, c * 128 : (c + 1) * 128] = out_ref[c]
    upper = jnp.concatenate([dtile_ref[d, 0:128, :] for d in range(tiles)], axis=1)
    lower = jnp.concatenate([dtile_ref[d, 128:256, :] for d in range(tiles)], axis=1)
    pad = jnp.zeros((128, 128), f32)
    x = jnp.concatenate([pad, pad, upper], axis=1) + jnp.concatenate([pad, lower, pad], axis=1)
    wide = x.shape[1]
    for half in (64, 32, 16, 8, 4, 2, 1):
        x = x[0:half] + pltpu.roll(x[half : 2 * half], wide - half, axis=1)
    g = x[:, TQ:]
    nb, length = tab_ref.shape[0], bucket_ref.shape[1]
    hot = jnp.broadcast_to(bucket_ref[...], (nb, length)) == lax.broadcasted_iota(
        jnp.int32, (nb, length), 0
    )
    sums = jnp.sum(jnp.where(hot, jnp.broadcast_to(g, (nb, length)), 0.0), axis=1, keepdims=True)
    column = jnp.concatenate([jnp.broadcast_to(sums, (nb, 128)), jnp.zeros((128 - nb, 128), f32)], axis=0)
    bias_ref[...] = column.T[0:8, :]


def route_kernel(
    ot_ref, tok_ref, wo_ref, gain_ref, router_ref, rt_ref, rcol_ref, grad_ref,
    send_ref, res_ref, gate_ref, hid_ref,
):
    tokens, width = tok_ref.shape
    experts = router_ref.shape[1]
    slots_all = send_ref.shape[0]
    capacity = slots_all // experts
    att = ot_ref[0:HEADS].reshape(width, tokens)
    residual = tok_ref[...].astype(f32) + tn(att, wo_ref[...])
    res_ref[...] = residual
    hidden = (residual * inv_rms(residual) * gain_ref[...]).astype(bf16)
    hid_ref[...] = hidden
    logits = nn(hidden, router_ref[...])
    expert_lane = lax.broadcasted_iota(jnp.int32, (tokens, experts), 1)
    picked = [
        jnp.sum(jnp.where(expert_lane == rcol_ref[:, c : c + 1], logits, 0.0), axis=1, keepdims=True)
        for c in (0, 1)
    ]
    top = jnp.maximum(picked[0], picked[1])
    e0, e1 = jnp.exp(picked[0] - top), jnp.exp(picked[1] - top)
    gates = [e0 / (e0 + e1), e1 / (e0 + e1)]
    gate_ref[...] = jnp.concatenate(
        [jnp.broadcast_to(g, (tokens, 128)) for g in gates], axis=1
    )
    expert_row = lax.broadcasted_iota(jnp.int32, (experts, tokens), 0)
    before = (
        lax.broadcasted_iota(jnp.int32, (tokens, tokens), 0)
        < lax.broadcasted_iota(jnp.int32, (tokens, tokens), 1)
    ).astype(bf16)
    slot_row = lax.broadcasted_iota(jnp.int32, (slots_all, tokens), 0)
    hots = [(expert_row == rt_ref[c : c + 1, :]).astype(f32) for c in (0, 1)]
    counts = jnp.sum(hots[0], axis=1, keepdims=True)
    taken = [nn(hots[0].astype(bf16), before), nn(hots[1].astype(bf16), before) + counts]
    to_slot = []
    for c in (0, 1):
        slot = jnp.sum(hots[c] * taken[c], axis=0, keepdims=True).astype(jnp.int32)
        place = rt_ref[c : c + 1, :] * capacity + slot
        to_slot.append((slot_row == place).astype(bf16))
    send_ref[:, 0:width] = nn(to_slot[0] + to_slot[1], hidden).astype(bf16)
    upstream = grad_ref[...].astype(f32)
    weighted = jnp.concatenate([(g * upstream).astype(bf16) for g in gates], axis=0)
    send_ref[:, width:] = nn(jnp.concatenate(to_slot, axis=1), weighted).astype(bf16)


def combine_kernel(
    ret_ref, res_ref, grad_ref, gate_ref, hid_ref, rcol_ref, gain_ref, router_t_ref, wo_ref, ot_ref,
    layer_ref, rgrad_ref, gt_ref, wo_grad_ref, small_ref,
):
    tokens, width = res_ref.shape
    experts = router_t_ref.shape[0]
    slots_all = ret_ref.shape[0]
    capacity = slots_all // experts
    lane = lax.broadcasted_iota(jnp.int32, (tokens, 128), 1)
    earlier = (
        lax.broadcasted_iota(jnp.int32, (tokens, tokens), 1)
        < lax.broadcasted_iota(jnp.int32, (tokens, tokens), 0)
    ).astype(bf16)
    hots = [(lane == rcol_ref[:, c : c + 1]).astype(f32) for c in (0, 1)]
    counts = jnp.sum(hots[0], axis=0, keepdims=True)
    taken = [nn(earlier, hots[0].astype(bf16)), nn(earlier, hots[1].astype(bf16)) + counts]
    slot_lane = lax.broadcasted_iota(jnp.int32, (tokens, slots_all), 1)
    from_slot = []
    for c in (0, 1):
        slot = jnp.sum(hots[c] * taken[c], axis=1, keepdims=True).astype(jnp.int32)
        place = rcol_ref[:, c : c + 1] * capacity + slot
        from_slot.append((slot_lane == place).astype(bf16))
    outs = [nn(m, ret_ref[:, 0:width]) for m in from_slot]
    row_sum = nn(from_slot[0] + from_slot[1], ret_ref[:, width:])
    gates = [gate_ref[:, 0:1], gate_ref[:, 128:129]]
    residual = res_ref[...]
    layer_ref[...] = (residual + (gates[0] * outs[0] + gates[1] * outs[1])).astype(bf16)
    upstream = grad_ref[...].astype(f32)
    gate_grads = [jnp.sum(upstream * o, axis=1, keepdims=True) for o in outs]
    mixed = gates[0] * gate_grads[0] + gates[1] * gate_grads[1]
    logit_grad = (
        gates[0] * (gate_grads[0] - mixed) * hots[0] + gates[1] * (gate_grads[1] - mixed) * hots[1]
    )
    h2g = row_sum
    for e in range(experts):
        h2g = h2g + logit_grad[:, e : e + 1] * router_t_ref[e : e + 1, :]
    inverse = inv_rms(residual)
    normed = residual * inverse
    logit_t = logit_grad.T
    high = logit_t.astype(bf16)
    rest = (logit_t - high.astype(f32)).astype(bf16)
    router_grad = nn(high, hid_ref[...]) + nn(rest, hid_ref[...])
    small_ref[0:8, :] = jnp.broadcast_to(jnp.sum(h2g * normed, axis=0, keepdims=True), (8, width))
    small_ref[8:16, :] = router_grad[0:experts]
    scaled = h2g * gain_ref[...]
    average = jnp.mean(scaled * normed, axis=-1, keepdims=True)
    residual_grad = upstream + inverse * (scaled - normed * average)
    rgrad_ref[...] = residual_grad
    branch = residual_grad.astype(bf16)
    gt = nt(wo_ref[...], branch).astype(bf16)
    gt_ref[0:HEADS] = gt.reshape(HEADS, HEAD_DIM, tokens)
    gt_ref[HEADS:] = jnp.zeros((gt_ref.shape[0] - HEADS, HEAD_DIM, tokens), bf16)
    att = ot_ref[0:HEADS].reshape(width, tokens)
    wo_grad_ref[...] = nn(att, branch).astype(bf16)


def expert_kernel(rows_ref, up_ref, down_ref, ret_ref, pre_ref, act_ref, out_acc, row_acc):
    step = pl.program_id(0)
    width = up_ref.shape[0]
    rows = rows_ref[:, 0:width]
    grads = rows_ref[:, width:]
    up, down = up_ref[...], down_ref[...]
    x = nn(rows, up)
    c = 0.7978845608028654
    t = jnp.tanh(c * (x + 0.044715 * (x * x * x)))
    hidden = (0.5 * x * (1.0 + t)).astype(bf16)
    slope = 0.5 * (1.0 + t) + 0.5 * x * (1.0 - t * t) * (c * (1.0 + 3 * 0.044715 * (x * x)))
    pre = (nn(grads, down) * slope).astype(bf16)
    act_ref[...] = hidden
    pre_ref[...] = pre
    out_part, row_part = nt(hidden, down), nt(pre, up)

    @pl.when(step == 0)
    def _():
        out_acc[...] = out_part
        row_acc[...] = row_part

    @pl.when(step > 0)
    def _():
        out_acc[...] += out_part
        row_acc[...] += row_part

    @pl.when(step == pl.num_programs(0) - 1)
    def _():
        ret_ref[:, 0:width] = out_acc[...].astype(bf16)
        ret_ref[:, width:] = row_acc[...].astype(bf16)


def expert_grad_kernel(rows_ref, pre_ref, act_ref, out_ref, left_ref):
    step = pl.program_id(0)
    steps = pl.num_programs(0)
    width = out_ref.shape[0]

    @pl.when(step == 0)
    def _():
        left_ref[...] = rows_ref[:, 0:width].astype(f32).T.astype(bf16)

    @pl.when(step == steps // 2)
    def _():
        left_ref[...] = rows_ref[:, width:].astype(f32).T.astype(bf16)

    @pl.when(step < steps // 2)
    def _():
        out_ref[...] = nn(left_ref[...], pre_ref[...]).astype(bf16)

    @pl.when(step >= steps // 2)
    def _():
        out_ref[...] = nn(left_ref[...], act_ref[...]).astype(bf16)


def pack_kernel(flat_ref, hid_ref, wt_ref, gain_ref, wo_ref, small_ref, bias_ref, out_ref):
    width = hid_ref.shape[1]
    grad = nn(flat_ref[...], hid_ref[...])
    part = jnp.sum(grad * wt_ref[...].astype(f32), axis=0, keepdims=True) / gain_ref[...]
    out_ref[0:192, :] = grad.astype(bf16)
    wo = wo_ref[0].astype(f32)
    for c in range(1, wo_ref.shape[0]):
        wo = wo + wo_ref[c].astype(f32)
    out_ref[192:240, :] = wo.astype(bf16)
    bias = jnp.concatenate([bias_ref[...], jnp.zeros((8, width - 128), f32)], axis=1)
    row = lax.broadcasted_iota(jnp.int32, (8, width), 0)
    first = jnp.where(
        row == 0, jnp.broadcast_to(part, (8, width)), jnp.where(row == 1, small_ref[0:8, :], bias)
    )
    out_ref[240:256, :] = jnp.concatenate([first, small_ref[8:16, :]], axis=0).astype(bf16)


def tokens_kernel(recv_ref, tok_ref, gain_ref, rgrad_ref, wq_ref, wk_ref, wv_ref, out_ref):
    tokens, width = tok_ref.shape
    acc = None
    for weight_ref, at in ((wq_ref, 0), (wk_ref, HEAD_DIM), (wv_ref, 2 * HEAD_DIM)):
        grad = recv_ref[0:HEADS, at : at + HEAD_DIM, :].reshape(width, tokens)
        part = nn(weight_ref[...], grad)
        acc = part if acc is None else acc + part
    hidden_grad = acc.T
    x = tok_ref[...].astype(f32)
    inverse = inv_rms(x)
    normed = x * inverse
    scaled = hidden_grad * gain_ref[...]
    average = jnp.mean(scaled * normed, axis=-1, keepdims=True)
    out_ref[...] = rgrad_ref[...] + inverse * (scaled - normed * average)


def unpack_kernel(where_ref, *refs):
    pieces, (q_ref, k_ref, v_ref, wo_ref, tail_ref, bias_ref, all_ref) = refs[:20], refs[20:]
    step = pl.program_id(0)
    x, y, z, core = where_ref[0], where_ref[1], where_ref[2], where_ref[3]

    @pl.when(step == 0)
    def _():
        for k in range(4):
            own, ahead, far_one, far_two, behind = pieces[5 * k : 5 * k + 5]
            full = all_ref.shape[3:]
            for d, ref in ((0, own), (1, ahead), (3, behind)):
                all_ref[k // 2, k % 2, d] = ref[...].reshape(full)
            all_ref[k // 2, k % 2, 2, 0:2] = far_one[...].reshape(2, *full[1:])
            all_ref[k // 2, k % 2, 2, 2:4] = far_two[...].reshape(2, *full[1:])

    def rows(c, group):
        exp, half = group // 2, group % 2
        dx, dy = (x - c % 4 + 4) % 4, (y - c // 4 + 4) % 4
        dz, other = (z - exp // 2 + 4) % 4, (core + exp % 2) % 2
        first, second = (dy, dx) if half == 0 else (dx, dy)
        return all_ref[other, half, first, second, dz]

    def span(c, start, stop):
        return jnp.concatenate([rows(c, g) for g in range(start // 16, stop // 16)], axis=0)

    for ref, at in ((q_ref, 0), (k_ref, HEAD_DIM), (v_ref, 2 * HEAD_DIM)):
        both = [span(2 * step, at, at + HEAD_DIM), span(2 * step + 1, at, at + HEAD_DIM)]
        ref[...] = jnp.concatenate(both, axis=0).astype(f32).T
    for k in (0, 1):
        c = jnp.minimum(2 * step + k, 11)
        bias_ref[0, 8 * k : 8 * k + 8, :] = rows(c, 15)[0:8, 0:128].astype(f32)
    for k in (0, 1, 2):
        c = jnp.minimum(3 * step + k, 15)
        wo_ref[48 * k : 48 * k + 48, :] = span(c, 192, 240).astype(f32)

    @pl.when(step == 0)
    def _():
        total = rows(0, 15).astype(f32)
        for c in range(1, 16):
            total = total + rows(c, 15).astype(f32)
        tail_ref[...] = total


def ring(axis, stride, size, block, distance):
    def to(i):
        place = (i // stride) % 4
        return i + ((place + distance) % 4 - place) * stride

    return lax.ppermute(block, axis, [(i, to(i)) for i in range(size)])


def gather_ring(axis, stride, size, block):
    half = block.shape[0] // 2
    ahead = ring(axis, stride, size, block, 1)
    behind = ring(axis, stride, size, block, -1)
    far_one = ring(axis, stride, size, ahead[:half], 1)
    far_two = ring(axis, stride, size, behind[half:], -1)
    return [block, ahead, far_one, far_two, behind]


def gather_near(axis, stride, size, block):
    return [block] + [ring(axis, stride, size, block, d) for d in (1, 2, 3)]


def split_kernel(*refs):
    pieces, outs = refs[:4], refs[4:]
    for half, out in enumerate(outs):
        for d, ref in enumerate(pieces):
            block = ref[...]
            out[16 * d : 16 * d + 16, :] = block[16 * half : 16 * half + 16]


def join_kernel(*refs):
    for k in range(2):
        for d, ref in enumerate(refs[4 * k : 4 * k + 4]):
            size = ref.shape[0]
            refs[8 + k][d * size : (d + 1) * size, :] = ref[...]


def gather_near_all(share, n_ctx, n_exp):
    width = share.shape[1]
    along_z = gather_near("exp", 2, n_exp, share)
    quarter = sds((64, width), bf16)
    first, second = call(split_kernel, (quarter, quarter), vmem=8)(*along_z)
    plane = gather_near("ctx", 1, n_ctx, first) + gather_near("ctx", 4, n_ctx, second)
    side = sds((256, width), bf16)
    return call(join_kernel, (side, side), vmem=8)(*plane)


def gather_far(first, second, n_ctx, n_exp):
    own = gather_ring("ctx", 4, n_ctx, first) + gather_ring("ctx", 1, n_ctx, second)
    pairs = [(i, i ^ 1) for i in range(n_exp)]
    return own + [lax.ppermute(piece, "exp", pairs) for piece in own]


def on_device(
    tokens, segment_ids, buckets, routes, attention_gain, query_weight, key_weight, value_weight,
    output_weight, bias_table, expert_gain, router_weight, expert_up, expert_down, out_grad,
):
    n_ctx, n_exp = lax.axis_size("ctx"), lax.axis_size("exp")
    rows, width = tokens.shape[1:]
    length = buckets.shape[0]
    experts = router_weight.shape[1]
    capacity = 5 * rows // (2 * experts)
    slots = experts * capacity
    hidden_units = expert_up.shape[2]
    head = lax.axis_index("ctx")
    gain_one = attention_gain.reshape(1, width)
    gain_two = expert_gain.reshape(1, width)
    bucket_row = buckets.reshape(1, length)
    table = jnp.pad(bias_table, ((0, 0), (0, n_ctx - HEADS)))
    tab = lax.dynamic_slice_in_dim(table, head, 1, axis=1)

    up_down = jnp.concatenate([expert_up[:, 0], expert_down[:, 0]], axis=1)
    weights = lax.all_gather(up_down, "ctx", axis=0, tiled=True)

    x = tokens[0]
    qkv, hidden = call(
        project_kernel,
        (sds((n_ctx, 2 * QA + HEAD_DIM, rows), bf16), sds((rows, width), bf16)),
        flops=6 * rows * width * width,
        moved=4 * MB,
    )(x, gain_one, segment_ids, query_weight, key_weight, value_weight)
    qkv = lax.all_to_all(qkv, "ctx", split_axis=0, concat_axis=0, tiled=True)
    at = jnp.minimum(head, HEADS - 1) * HEAD_DIM
    own_weights = jnp.concatenate(
        [
            lax.dynamic_slice_in_dim(w, at, HEAD_DIM, axis=1).T
            for w in (query_weight, key_weight, value_weight)
        ],
        axis=0,
    )
    qkv, own_weights = lax.optimization_barrier((qkv, own_weights))
    hidden_all = lax.all_gather(hidden, "ctx", axis=0, tiled=True)

    tiles = length // TQ
    ot, otf, lse = call(
        attend_kernel,
        (
            sds((n_ctx, HEAD_DIM, rows), bf16),
            sds((tiles, HEAD_DIM, TQ), f32),
            sds((tiles, 1, TQ), f32),
        ),
        scratch_shapes=[pltpu.VMEM((tiles, TQ, QA), bf16), pltpu.VMEM((tiles, TQ, TQ), f32)],
        flops=8 * 10**9,
        moved=10 * MB,
    )(qkv, bucket_row, tab)
    ot = lax.all_to_all(ot, "ctx", split_axis=0, concat_axis=0, tiled=True)

    routed = routes[0]
    grads_in = out_grad[0]
    send, residual, gates, hidden_two = call(
        route_kernel,
        (
            sds((slots, 2 * width), bf16),
            sds((rows, width), f32),
            sds((rows, 256), f32),
            sds((rows, width), bf16),
        ),
        flops=10**9,
        moved=4 * MB,
    )(ot, x, output_weight, gain_two, router_weight, routed.T, routed, grads_in)
    received = lax.all_to_all(send, "exp", split_axis=0, concat_axis=0, tiled=True)

    chunk = 512
    steps = hidden_units // chunk
    whole = lambda shape: pl.BlockSpec(shape, lambda i: (0, 0))
    result, pre, act = call(
        expert_kernel,
        (
            sds((slots, 2 * width), bf16),
            sds((slots, hidden_units), bf16),
            sds((slots, hidden_units), bf16),
        ),
        grid=(steps,),
        in_specs=[
            whole((slots, 2 * width)),
            pl.BlockSpec((width, chunk), lambda i: (0, i)),
            pl.BlockSpec((width, chunk), lambda i: (0, steps + i)),
        ],
        out_specs=[
            whole((slots, 2 * width)),
            pl.BlockSpec((slots, chunk), lambda i: (0, i)),
            pl.BlockSpec((slots, chunk), lambda i: (0, i)),
        ],
        scratch_shapes=[pltpu.VMEM((slots, width), f32), pltpu.VMEM((slots, width), f32)],
        flops=8 * slots * width * hidden_units,
        moved=16 * MB,
    )(received, weights, weights)
    returned = lax.all_to_all(result, "exp", split_axis=0, concat_axis=0, tiled=True)
    weight_grads = call(
        expert_grad_kernel,
        sds((width, 2 * hidden_units), bf16),
        grid=(2 * steps,),
        in_specs=[
            whole((slots, 2 * width)),
            pl.BlockSpec((slots, chunk), lambda i: (0, jnp.minimum(i, steps - 1))),
            pl.BlockSpec((slots, chunk), lambda i: (0, jnp.maximum(i - steps, 0))),
        ],
        out_specs=pl.BlockSpec((width, chunk), lambda i: (0, i)),
        scratch_shapes=[pltpu.VMEM((width, slots), bf16)],
        flops=4 * slots * width * hidden_units,
        moved=16 * MB,
    )(received, pre, act)
    returned, weight_grads = lax.optimization_barrier((returned, weight_grads))

    layer_out, residual_grad, gt, wo_grad, small = call(
        combine_kernel,
        (
            sds((rows, width), bf16),
            sds((rows, width), f32),
            sds((n_ctx, HEAD_DIM, rows), bf16),
            sds((width, width), bf16),
            sds((16, width), f32),
        ),
        flops=10**9,
        moved=6 * MB,
    )(
        returned, residual, grads_in, gates, hidden_two, routed, gain_two,
        router_weight.astype(f32).T, output_weight, ot,
    )
    gt = lax.all_to_all(gt, "ctx", split_axis=0, concat_axis=0, tiled=True)
    weight_grads, hidden_all, gt = lax.optimization_barrier((weight_grads, hidden_all, gt))
    summed = lax.psum_scatter(weight_grads, "ctx", scatter_dimension=0, tiled=True)
    wo_parts = lax.all_to_all(
        wo_grad.reshape(n_ctx, width // n_ctx, width), "ctx", split_axis=0, concat_axis=0, tiled=True
    )

    dqkv, flat, bias_grad = call(
        attend_back_kernel,
        (
            sds((n_ctx, 3 * HEAD_DIM, rows), bf16),
            sds((3 * HEAD_DIM, length), bf16),
            sds((8, 128), f32),
        ),
        scratch_shapes=[
            pltpu.VMEM((tiles, TQ, QA), bf16),
            pltpu.VMEM((tiles, TQ, HEAD_DIM), bf16),
            pltpu.VMEM((tiles, TQ, TQ), f32),
            pltpu.VMEM((tiles, TQ, TQ), f32),
            pltpu.VMEM((tiles, HEAD_DIM, TQ), f32),
            pltpu.VMEM((tiles, HEAD_DIM, TQ), f32),
        ],
        flops=20 * 10**9,
        moved=20 * MB,
    )(qkv, gt, otf, lse, bucket_row, tab)

    packed = call(
        pack_kernel,
        sds((ROWS, width), bf16),
        flops=6 * length * width * HEAD_DIM,
        moved=6 * MB,
    )(flat, hidden_all, own_weights, gain_one, wo_parts, small, bias_grad)
    parts = lax.all_to_all(
        packed.reshape(n_exp, ROWS // n_exp, width), "exp", split_axis=0, concat_axis=0, tiled=True
    )
    parts, dqkv = lax.optimization_barrier((parts, dqkv))
    back = lax.all_to_all(dqkv, "ctx", split_axis=0, concat_axis=0, tiled=True)
    share = jnp.sum(parts.astype(f32), axis=0).astype(bf16)
    tokens_grad = call(
        tokens_kernel,
        sds((rows, width), f32),
        flops=6 * rows * width * width,
        moved=6 * MB,
    )(back, x, gain_one, residual_grad, query_weight, key_weight, value_weight)
    first, second = gather_near_all(share, n_ctx, n_exp)
    first, second, tokens_grad = lax.optimization_barrier((first, second, tokens_grad))
    everything = gather_far(first, second, n_ctx, n_exp)

    full = sds((width, width), f32)
    column = pl.BlockSpec((width, 128), lambda i, w: (0, i))
    exp = lax.axis_index("exp")
    where = jnp.stack([head % 4, head // 4, exp // 2, exp % 2]).astype(jnp.int32)
    query_grad, key_grad, value_grad, output_grad, tails, bias_rows = call(
        unpack_kernel,
        (
            full,
            full,
            full,
            full,
            sds((16, width), f32),
            sds((HEADS // 2, 16, 128), f32),
        ),
        grid_spec=pltpu.PrefetchScalarGridSpec(
            num_scalar_prefetch=1,
            grid=(HEADS // 2,),
            in_specs=[pl.BlockSpec(piece.shape, lambda i, w: (0, 0)) for piece in everything],
            out_specs=[
                column,
                column,
                column,
                pl.BlockSpec((144, width), lambda i, w: (i, 0)),
                pl.BlockSpec((16, width), lambda i, w: (0, 0)),
                pl.BlockSpec((1, 16, 128), lambda i, w: (i, 0, 0)),
            ],
            scratch_shapes=[pltpu.VMEM((2, 2, 4, 4, 4, 16, width), bf16)],
        ),
        vmem=40,
        moved=16 * MB,
    )(where, *everything)
    table_grad = bias_rows.reshape(HEADS, 8, 128)[:, 2, : bias_table.shape[0]].T
    return (
        layer_out[None],
        tokens_grad[None],
        tails[0],
        query_grad,
        key_grad,
        value_grad,
        output_grad,
        table_grad,
        tails[1],
        tails[8:].T,
        summed[:, :hidden_units].astype(f32)[:, None],
        summed[:, hidden_units:].astype(f32)[:, None],
    )


def solution(mesh):
    placed = (
        P("exp", "ctx", None),
        P("exp", "ctx"),
        P(),
        P("exp", "ctx", None),
        P(),
        P(),
        P(),
        P(),
        P(),
        P(),
        P(),
        P(),
        P("ctx", "exp", None),
        P("ctx", "exp", None),
        P("exp", "ctx", None),
    )
    return jax.shard_map(
        on_device,
        mesh=mesh,
        in_specs=placed,
        out_specs=(
            P("exp", "ctx", None),
            P("exp", "ctx", None),
            P(),
            P(),
            P(),
            P(),
            P(),
            P(),
            P(),
            P(),
            P("ctx", "exp", None),
            P("ctx", "exp", None),
        ),
        check_vma=False,
    )
```

```python
import jax
import jax.numpy as jnp
from jax import lax
from jax.experimental import pallas as pl
from jax.experimental.pallas import tpu as pltpu
from jax.sharding import PartitionSpec as P

HEADS = 12
HEAD_DIM = 64
EPS = 1e-06
NEG = -1e30
BIG = 2.0**99
SCALE = HEAD_DIM ** (-0.5)
AUG = 16
ROWS = 256
f32 = jnp.float32
bf16 = jnp.bfloat16
MB = 1024 * 1024


def nn(a, b):
    return lax.dot_general(a, b, (((1,), (0,)), ((), ())), preferred_element_type=f32)


def nt(a, b):
    return lax.dot_general(a, b, (((1,), (1,)), ((), ())), preferred_element_type=f32)


def tn(a, b):
    return lax.dot_general(a, b, (((0,), (0,)), ((), ())), preferred_element_type=f32)


def call(kernel, vmem, out_shape, flops=0, moved=0, **kw):
    return pl.pallas_call(
        kernel,
        out_shape=out_shape,
        compiler_params=pltpu.CompilerParams(vmem_limit_bytes=vmem * MB),
        cost_estimate=pl.CostEstimate(flops=flops, bytes_accessed=moved, transcendentals=0),
        **kw,
    )


def sds(shape, dtype):
    return jax.ShapeDtypeStruct(shape, dtype)


def inv_rms(value):
    return lax.rsqrt(jnp.mean(value * value, axis=-1, keepdims=True) + EPS)


def project_kernel(tok_ref, gain_ref, seg_ref, wq_ref, wk_ref, wv_ref, out_ref, hid_ref):
    x = tok_ref[...].astype(f32)
    hidden = (x * inv_rms(x) * gain_ref[...]).astype(bf16)
    hid_ref[...] = hidden
    tokens = x.shape[0]
    heads = out_ref.shape[0]

    def put(weight_ref, at, factor):
        t = (nn(hidden, weight_ref[...]).astype(bf16).astype(f32) * factor).T.astype(bf16)
        out_ref[0:HEADS, at : at + HEAD_DIM, :] = t.reshape(HEADS, HEAD_DIM, tokens)
        out_ref[HEADS:, at : at + HEAD_DIM, :] = jnp.zeros((heads - HEADS, HEAD_DIM, tokens), bf16)

    put(wq_ref, 0, SCALE)
    put(wk_ref, HEAD_DIM + AUG, 1.0)
    put(wv_ref, 2 * (HEAD_DIM + AUG), 1.0)
    s = jnp.broadcast_to(seg_ref[...].astype(f32), (AUG, tokens))
    row = lax.broadcasted_iota(jnp.int32, (AUG, tokens), 0)
    q_rows = jnp.where(row == 0, s * BIG, jnp.where(row == 1, (1.0 - s) * BIG, 0.0)).astype(bf16)
    k_rows = jnp.where(
        row == 0, s - 1.0, jnp.where(row == 1, -s, jnp.where(row < 5, 1.0, 0.0))
    ).astype(bf16)
    full = (heads, AUG, tokens)
    out_ref[:, HEAD_DIM : HEAD_DIM + AUG, :] = jnp.broadcast_to(q_rows[None], full)
    out_ref[:, 2 * HEAD_DIM + AUG : 2 * (HEAD_DIM + AUG), :] = jnp.broadcast_to(k_rows[None], full)


QA = HEAD_DIM + AUG
TQ = 256


def bias_tiles(bucket_ref, tab_ref, tile_ref):
    length = bucket_ref.shape[1]
    buckets = bucket_ref[...]
    nb = tab_ref.shape[0]
    hot = jnp.broadcast_to(buckets, (nb, length)) == lax.broadcasted_iota(
        jnp.int32, (nb, length), 0
    )
    b = jnp.sum(jnp.where(hot, tab_ref[...], 0.0), axis=0, keepdims=True)
    w = jnp.concatenate([jnp.full((1, TQ), NEG, f32), b], axis=1)
    x = jnp.broadcast_to(w, (8, length + TQ))
    row = lax.broadcasted_iota(jnp.int32, x.shape, 0)
    for bit in (1, 2, 4):
        x = jnp.where((row & bit) > 0, pltpu.roll(x, bit, axis=1), x)
    for bit in (8, 16, 32, 64):
        x = jnp.concatenate([x, pltpu.roll(x, bit, axis=1)], axis=0)
    tiles = length // TQ
    for d in range(tiles):
        at = (d + 1) * TQ
        tile_ref[tiles - 1 - d, 0:128, :] = x[:, at : at + TQ]
        tile_ref[tiles - 1 - d, 128:256, :] = x[:, at - 128 : at - 128 + TQ]
    tile_ref[tiles] = jnp.full((TQ, TQ), NEG, f32)


def transposed(block):
    return block.astype(f32).T.astype(bf16)


def pair(ref, index, at, size, count=2):
    return jnp.concatenate(
        [ref[count * index + k, at : at + size, :] for k in range(count)], axis=1
    )


def boundary(recv_ref):
    ones = recv_ref[:, QA + HEAD_DIM : QA + HEAD_DIM + AUG, :].astype(f32)
    row = lax.broadcasted_iota(jnp.int32, ones.shape, 1)
    total = jnp.sum(jnp.where(row == 1, ones, 0.0))
    return recv_ref.shape[0] * recv_ref.shape[2] + total.astype(jnp.int32)


def first_chunk(qb, edge):
    return jnp.where(qb * TQ >= edge, edge // (2 * TQ), 0)


def attend_kernel(recv_ref, bucket_ref, tab_ref, ot_ref, otf_ref, lse_ref, kn_ref, tile_ref):
    blocks = recv_ref.shape[0]
    bias_tiles(bucket_ref, tab_ref, tile_ref)
    for c in range(blocks):
        kn_ref[c // 4, (c % 4) * 128 : (c % 4) * 128 + 128, :] = transposed(
            recv_ref[c, QA : 2 * QA, :]
        )
    edge = boundary(recv_ref)
    last = blocks // 2 - 1

    def one_query_tile(qb, carry):
        qt = pair(recv_ref, qb, 0, QA)

        def one_key_tile(i, state):
            top, total, acc = state
            kc = qb // 2 - i
            bias = tile_ref[pl.ds(last - qb + 2 * kc, 2)].reshape(2 * TQ, TQ)
            s = nn(kn_ref[kc], qt) + bias
            new_top = jnp.maximum(top, jnp.max(s, axis=0, keepdims=True))
            p = jnp.exp(s - new_top)
            factor = jnp.exp(top - new_top)
            total = total * factor + jnp.sum(p, axis=0, keepdims=True)
            acc = acc * factor + nn(pair(recv_ref, kc, 2 * QA, HEAD_DIM, 4), p.astype(bf16))
            return new_top, total, acc

        start = (jnp.full((1, TQ), NEG, f32), jnp.zeros((1, TQ), f32), jnp.zeros((HEAD_DIM, TQ), f32))
        turns = qb // 2 - first_chunk(qb, edge) + 1
        top, total, acc = lax.fori_loop(0, turns, one_key_tile, start)
        o = acc / total
        otf_ref[qb] = o
        lse_ref[qb] = top + jnp.log(total)
        low = o.astype(bf16)
        ot_ref[2 * qb] = low[:, :128]
        ot_ref[2 * qb + 1] = low[:, 128:]
        return carry

    lax.fori_loop(0, blocks // 2, one_query_tile, 0)


def attend_back_kernel(
    recv_ref, gt_ref, otf_ref, lse_ref, bucket_ref, tab_ref,
    out_ref, flat_ref, bias_ref,
    kn_ref, vn_ref, tile_ref, dtile_ref, dk_ref, dv_ref,
):
    blocks = recv_ref.shape[0]
    tiles = blocks // 2
    bias_tiles(bucket_ref, tab_ref, tile_ref)
    for c in range(blocks):
        at = (c % 4) * 128
        kn_ref[c // 4, at : at + 128, :] = transposed(recv_ref[c, QA : 2 * QA, :])
        vn_ref[c // 4, at : at + 128, :] = transposed(recv_ref[c, 2 * QA : 2 * QA + HEAD_DIM, :])
    edge = boundary(recv_ref)
    dtile_ref[...] = jnp.zeros_like(dtile_ref)
    dk_ref[...] = jnp.zeros_like(dk_ref)
    dv_ref[...] = jnp.zeros_like(dv_ref)

    def one_query_tile(qb, carry):
        qt = pair(recv_ref, qb, 0, QA)
        gt = pair(gt_ref, qb, 0, HEAD_DIM)
        lse = lse_ref[qb]
        delta = jnp.sum(gt.astype(f32) * otf_ref[qb], axis=0, keepdims=True)

        def one_key_tile(i, acc):
            kc = qb // 2 - i
            place = pl.ds(tiles - 1 - qb + 2 * kc, 2)
            p = jnp.exp(nn(kn_ref[kc], qt) + tile_ref[place].reshape(2 * TQ, TQ) - lse)
            dp = nn(vn_ref[kc], gt)
            ds = (p * (dp - delta)).astype(bf16)
            dtile_ref[place] += ds.astype(f32).reshape(2, TQ, TQ)
            dv_ref[kc] += nt(gt, p.astype(bf16))
            dk_ref[kc] += nt(qt[:HEAD_DIM], ds)
            return acc + nn(pair(recv_ref, kc, QA, HEAD_DIM, 4), ds)

        acc = lax.fori_loop(
            0, qb // 2 - first_chunk(qb, edge) + 1, one_key_tile, jnp.zeros((HEAD_DIM, TQ), f32)
        )
        low = (acc * SCALE).astype(bf16)
        out_ref[2 * qb, 0:HEAD_DIM, :] = low[:, :128]
        out_ref[2 * qb + 1, 0:HEAD_DIM, :] = low[:, 128:]
        return carry

    lax.fori_loop(0, tiles, one_query_tile, 0)
    for c in range(blocks):
        for ref, at in ((dk_ref, HEAD_DIM), (dv_ref, 2 * HEAD_DIM)):
            lanes = slice((c % 4) * 128, (c % 4) * 128 + 128)
            out_ref[c, at : at + HEAD_DIM, :] = ref[c // 4, :, lanes].astype(bf16)
    for c in range(blocks):
        flat_ref[:, c * 128 : (c + 1) * 128] = out_ref[c]
    upper = jnp.concatenate([dtile_ref[tiles - 1 - d, 0:128, :] for d in range(tiles)], axis=1)
    lower = jnp.concatenate([dtile_ref[tiles - 1 - d, 128:256, :] for d in range(tiles)], axis=1)
    pad = jnp.zeros((128, 128), f32)
    x = jnp.concatenate([pad, pad, upper], axis=1) + jnp.concatenate([pad, lower, pad], axis=1)
    wide = x.shape[1]
    for half in (64, 32, 16, 8, 4, 2, 1):
        x = x[0:half] + pltpu.roll(x[half : 2 * half], wide - half, axis=1)
    g = x[:, TQ:]
    nb, length = tab_ref.shape[0], bucket_ref.shape[1]
    hot = jnp.broadcast_to(bucket_ref[...], (nb, length)) == lax.broadcasted_iota(
        jnp.int32, (nb, length), 0
    )
    sums = jnp.sum(jnp.where(hot, jnp.broadcast_to(g, (nb, length)), 0.0), axis=1, keepdims=True)
    column = jnp.concatenate([jnp.broadcast_to(sums, (nb, 128)), jnp.zeros((128 - nb, 128), f32)], axis=0)
    bias_ref[...] = column.T[0:8, :]


def route_kernel(
    ot_ref, tok_ref, wo_ref, gain_ref, router_ref, rt_ref, rcol_ref, grad_ref,
    send_ref, res_ref, gate_ref, hid_ref,
):
    tokens, width = tok_ref.shape
    experts = router_ref.shape[1]
    slots_all = send_ref.shape[0]
    capacity = slots_all // experts
    att = ot_ref[0:HEADS].reshape(width, tokens)
    residual = tok_ref[...].astype(f32) + tn(att, wo_ref[...])
    res_ref[...] = residual
    hidden = (residual * inv_rms(residual) * gain_ref[...]).astype(bf16)
    hid_ref[...] = hidden
    logits = nn(hidden, router_ref[...])
    expert_lane = lax.broadcasted_iota(jnp.int32, (tokens, experts), 1)
    picked = [
        jnp.sum(jnp.where(expert_lane == rcol_ref[:, c : c + 1], logits, 0.0), axis=1, keepdims=True)
        for c in (0, 1)
    ]
    top = jnp.maximum(picked[0], picked[1])
    e0, e1 = jnp.exp(picked[0] - top), jnp.exp(picked[1] - top)
    gates = [e0 / (e0 + e1), e1 / (e0 + e1)]
    gate_ref[...] = jnp.concatenate(
        [jnp.broadcast_to(g, (tokens, 128)) for g in gates], axis=1
    )
    expert_row = lax.broadcasted_iota(jnp.int32, (experts, tokens), 0)
    before = (
        lax.broadcasted_iota(jnp.int32, (tokens, tokens), 0)
        < lax.broadcasted_iota(jnp.int32, (tokens, tokens), 1)
    ).astype(bf16)
    slot_row = lax.broadcasted_iota(jnp.int32, (slots_all, tokens), 0)
    hots = [(expert_row == rt_ref[c : c + 1, :]).astype(f32) for c in (0, 1)]
    counts = jnp.sum(hots[0], axis=1, keepdims=True)
    taken = [nn(hots[0].astype(bf16), before), nn(hots[1].astype(bf16), before) + counts]
    to_slot = []
    for c in (0, 1):
        slot = jnp.sum(hots[c] * taken[c], axis=0, keepdims=True).astype(jnp.int32)
        place = rt_ref[c : c + 1, :] * capacity + slot
        to_slot.append((slot_row == place).astype(bf16))
    send_ref[:, 0:width] = nn(to_slot[0] + to_slot[1], hidden).astype(bf16)
    upstream = grad_ref[...].astype(f32)
    weighted = jnp.concatenate([(g * upstream).astype(bf16) for g in gates], axis=0)
    send_ref[:, width:] = nn(jnp.concatenate(to_slot, axis=1), weighted).astype(bf16)


def combine_kernel(
    ret_ref, res_ref, grad_ref, gate_ref, hid_ref, rcol_ref, gain_ref, router_t_ref, wo_ref, ot_ref,
    layer_ref, rgrad_ref, gt_ref, wo_grad_ref, small_ref,
):
    tokens, width = res_ref.shape
    experts = router_t_ref.shape[0]
    slots_all = ret_ref.shape[0]
    capacity = slots_all // experts
    lane = lax.broadcasted_iota(jnp.int32, (tokens, 128), 1)
    earlier = (
        lax.broadcasted_iota(jnp.int32, (tokens, tokens), 1)
        < lax.broadcasted_iota(jnp.int32, (tokens, tokens), 0)
    ).astype(bf16)
    hots = [(lane == rcol_ref[:, c : c + 1]).astype(f32) for c in (0, 1)]
    counts = jnp.sum(hots[0], axis=0, keepdims=True)
    taken = [nn(earlier, hots[0].astype(bf16)), nn(earlier, hots[1].astype(bf16)) + counts]
    slot_lane = lax.broadcasted_iota(jnp.int32, (tokens, slots_all), 1)
    from_slot = []
    for c in (0, 1):
        slot = jnp.sum(hots[c] * taken[c], axis=1, keepdims=True).astype(jnp.int32)
        place = rcol_ref[:, c : c + 1] * capacity + slot
        from_slot.append((slot_lane == place).astype(bf16))
    outs = [nn(m, ret_ref[:, 0:width]) for m in from_slot]
    row_sum = nn(from_slot[0] + from_slot[1], ret_ref[:, width:])
    gates = [gate_ref[:, 0:1], gate_ref[:, 128:129]]
    residual = res_ref[...]
    layer_ref[...] = (residual + (gates[0] * outs[0] + gates[1] * outs[1])).astype(bf16)
    upstream = grad_ref[...].astype(f32)
    gate_grads = [jnp.sum(upstream * o, axis=1, keepdims=True) for o in outs]
    mixed = gates[0] * gate_grads[0] + gates[1] * gate_grads[1]
    logit_grad = (
        gates[0] * (gate_grads[0] - mixed) * hots[0] + gates[1] * (gate_grads[1] - mixed) * hots[1]
    )
    h2g = row_sum
    for e in range(experts):
        h2g = h2g + logit_grad[:, e : e + 1] * router_t_ref[e : e + 1, :]
    inverse = inv_rms(residual)
    normed = residual * inverse
    logit_t = logit_grad.T
    high = logit_t.astype(bf16)
    rest = (logit_t - high.astype(f32)).astype(bf16)
    router_grad = nn(high, hid_ref[...]) + nn(rest, hid_ref[...])
    small_ref[0:8, :] = jnp.broadcast_to(jnp.sum(h2g * normed, axis=0, keepdims=True), (8, width))
    small_ref[8:16, :] = router_grad[0:experts]
    scaled = h2g * gain_ref[...]
    average = jnp.mean(scaled * normed, axis=-1, keepdims=True)
    residual_grad = upstream + inverse * (scaled - normed * average)
    rgrad_ref[...] = residual_grad
    branch = residual_grad.astype(bf16)
    gt = nt(wo_ref[...], branch).astype(bf16)
    gt_ref[0:HEADS] = gt.reshape(HEADS, HEAD_DIM, tokens)
    gt_ref[HEADS:] = jnp.zeros((gt_ref.shape[0] - HEADS, HEAD_DIM, tokens), bf16)
    att = ot_ref[0:HEADS].reshape(width, tokens)
    wo_grad_ref[...] = nn(att, branch).astype(bf16)


def expert_kernel(rows_ref, up_ref, down_ref, ret_ref, pre_ref, act_ref, out_acc, row_acc):
    step = pl.program_id(0)
    width = up_ref.shape[0]
    rows = rows_ref[:, 0:width]
    grads = rows_ref[:, width:]
    up, down = up_ref[...], down_ref[...]
    x = nn(rows, up)
    c = 0.7978845608028654
    t = jnp.tanh(c * (x + 0.044715 * (x * x * x)))
    hidden = (0.5 * x * (1.0 + t)).astype(bf16)
    slope = 0.5 * (1.0 + t) + 0.5 * x * (1.0 - t * t) * (c * (1.0 + 3 * 0.044715 * (x * x)))
    pre = (nn(grads, down) * slope).astype(bf16)
    act_ref[...] = hidden
    pre_ref[...] = pre
    out_part, row_part = nt(hidden, down), nt(pre, up)

    @pl.when(step == 0)
    def _():
        out_acc[...] = out_part
        row_acc[...] = row_part

    @pl.when(step > 0)
    def _():
        out_acc[...] += out_part
        row_acc[...] += row_part

    @pl.when(step == pl.num_programs(0) - 1)
    def _():
        ret_ref[:, 0:width] = out_acc[...].astype(bf16)
        ret_ref[:, width:] = row_acc[...].astype(bf16)


def expert_grad_kernel(rows_ref, pre_ref, act_ref, out_ref, left_ref):
    step = pl.program_id(0)
    steps = pl.num_programs(0)
    width = out_ref.shape[0]

    @pl.when(step == 0)
    def _():
        left_ref[...] = rows_ref[:, 0:width].astype(f32).T.astype(bf16)

    @pl.when(step == steps // 2)
    def _():
        left_ref[...] = rows_ref[:, width:].astype(f32).T.astype(bf16)

    @pl.when(step < steps // 2)
    def _():
        out_ref[...] = nn(left_ref[...], pre_ref[...]).astype(bf16)

    @pl.when(step >= steps // 2)
    def _():
        out_ref[...] = nn(left_ref[...], act_ref[...]).astype(bf16)


def pack_kernel(
    flat_ref, hid_ref, wt_ref, gain_ref, wo_ref, small_ref, bias_ref, out_ref, grad_ref, sum_ref
):
    step = pl.program_id(0)
    width = hid_ref.shape[1]
    part = nn(flat_ref[...], hid_ref[...])
    wo = wo_ref[0].astype(f32)
    for c in range(1, wo_ref.shape[0]):
        wo = wo + wo_ref[c].astype(f32)

    @pl.when(step == 0)
    def _():
        grad_ref[...] = part
        sum_ref[...] = wo

    @pl.when(step > 0)
    def _():
        grad_ref[...] += part
        sum_ref[...] += wo

    @pl.when(step == pl.num_programs(0) - 1)
    def _():
        grad = grad_ref[...]
        gain = jnp.sum(grad * wt_ref[...].astype(f32), axis=0, keepdims=True) / gain_ref[...]
        out_ref[0:192, :] = grad.astype(bf16)
        out_ref[192:240, :] = sum_ref[...].astype(bf16)
        bias = jnp.concatenate([bias_ref[...], jnp.zeros((8, width - 128), f32)], axis=1)
        row = lax.broadcasted_iota(jnp.int32, (8, width), 0)
        first = jnp.where(
            row == 0,
            jnp.broadcast_to(gain, (8, width)),
            jnp.where(row == 1, small_ref[0:8, :], bias),
        )
        out_ref[240:256, :] = jnp.concatenate([first, small_ref[8:16, :]], axis=0).astype(bf16)


def tokens_kernel(recv_ref, tok_ref, gain_ref, rgrad_ref, wq_ref, wk_ref, wv_ref, out_ref):
    tokens, width = tok_ref.shape
    acc = None
    for weight_ref, at in ((wq_ref, 0), (wk_ref, HEAD_DIM), (wv_ref, 2 * HEAD_DIM)):
        grad = recv_ref[0:HEADS, at : at + HEAD_DIM, :].reshape(width, tokens)
        part = nn(weight_ref[...], grad)
        acc = part if acc is None else acc + part
    hidden_grad = acc.T
    x = tok_ref[...].astype(f32)
    inverse = inv_rms(x)
    normed = x * inverse
    scaled = hidden_grad * gain_ref[...]
    average = jnp.mean(scaled * normed, axis=-1, keepdims=True)
    out_ref[...] = rgrad_ref[...] + inverse * (scaled - normed * average)


def widen_kernel(in_ref, up_ref, down_ref):
    units = up_ref.shape[2]
    up_ref[:, 0, :] = in_ref[:, 0:units].astype(f32)
    down_ref[:, 0, :] = in_ref[:, units:].astype(f32)


def ring_rows(piece):
    rows, width = piece.shape
    shape = (4, 4, 16, width) if rows == 256 else (2, 4, 16, width)
    return piece.reshape(shape)


def unpack_kernel(where_ref, *refs):
    pieces, (q_ref, k_ref, v_ref, wo_ref, tail_ref, bias_ref, all_ref, sems) = refs[:20], refs[20:]
    step = pl.program_id(0)
    x, y, z, core = where_ref[0], where_ref[1], where_ref[2], where_ref[3]

    @pl.when(step == 0)
    def _():
        copies = []
        for k in range(4):
            slot = all_ref.at[k // 2, k % 2]
            places = [slot.at[0], slot.at[1], slot.at[2, 0:2], slot.at[2, 2:4], slot.at[3]]
            for j, place in enumerate(places):
                n = 5 * k + j
                copies.append(pltpu.make_async_copy(pieces[n], place, sems.at[n]))
        for copy in copies:
            copy.start()
        for copy in copies:
            copy.wait()

    def rows(c, group):
        exp, half = group // 2, group % 2
        dx, dy = (x - c % 4 + 4) % 4, (y - c // 4 + 4) % 4
        dz, other = (z - exp // 2 + 4) % 4, (core + exp % 2) % 2
        first, second = (dy, dx) if half == 0 else (dx, dy)
        return all_ref[other, half, first, second, dz]

    def span(c, start, stop):
        return jnp.concatenate([rows(c, g) for g in range(start // 16, stop // 16)], axis=0)

    for ref, at in ((q_ref, 0), (k_ref, HEAD_DIM), (v_ref, 2 * HEAD_DIM)):
        both = [span(2 * step, at, at + HEAD_DIM), span(2 * step + 1, at, at + HEAD_DIM)]
        ref[...] = jnp.concatenate(both, axis=0).astype(f32).T
    for k in (0, 1):
        c = jnp.minimum(2 * step + k, 11)
        bias_ref[0, 8 * k : 8 * k + 8, :] = rows(c, 15)[0:8, 0:128].astype(f32)
    for k in (0, 1, 2):
        c = jnp.minimum(3 * step + k, 15)
        wo_ref[48 * k : 48 * k + 48, :] = span(c, 192, 240).astype(f32)

    @pl.when(step == 0)
    def _():
        total = rows(0, 15).astype(f32)
        for c in range(1, 16):
            total = total + rows(c, 15).astype(f32)
        tail_ref[...] = total


def ring(axis, stride, size, block, distance):
    def to(i):
        place = (i // stride) % 4
        return i + ((place + distance) % 4 - place) * stride

    return lax.ppermute(block, axis, [(i, to(i)) for i in range(size)])


def gather_ring(axis, stride, size, block):
    half = block.shape[0] // 2
    ahead = ring(axis, stride, size, block, 1)
    behind = ring(axis, stride, size, block, -1)
    far_one = ring(axis, stride, size, ahead[:half], 1)
    far_two = ring(axis, stride, size, behind[half:], -1)
    return [block, ahead, far_one, far_two, behind]


def gather_near(axis, stride, size, block):
    return [block] + [ring(axis, stride, size, block, d) for d in (1, 2, 3)]


def split_kernel(*refs):
    pieces, outs = refs[:4], refs[4:]
    for half, out in enumerate(outs):
        for d, ref in enumerate(pieces):
            block = ref[...]
            out[16 * d : 16 * d + 16, :] = block[16 * half : 16 * half + 16]


def join_kernel(*refs):
    for k in range(2):
        for d, ref in enumerate(refs[4 * k : 4 * k + 4]):
            size = ref.shape[0]
            refs[8 + k][d * size : (d + 1) * size, :] = ref[...]


def gather_near_all(share, n_ctx, n_exp):
    width = share.shape[1]
    along_z = gather_near("exp", 2, n_exp, share)
    quarter = sds((64, width), bf16)
    first, second = call(split_kernel, 8, (quarter, quarter))(*along_z)
    plane = gather_near("ctx", 1, n_ctx, first) + gather_near("ctx", 4, n_ctx, second)
    side = sds((256, width), bf16)
    return call(join_kernel, 8, (side, side))(*plane)


def gather_far(first, second, n_ctx, n_exp, done):
    own = gather_ring("ctx", 4, n_ctx, first) + gather_ring("ctx", 1, n_ctx, second)
    own[0], own[5], tokens_grad = lax.optimization_barrier((own[0], own[5], done[0]))
    tied = lax.optimization_barrier((own[2], own[3], own[7], own[8], *done[1:]))
    own[2], own[3], own[7], own[8] = tied[:4]
    pairs = [(i, i ^ 1) for i in range(n_exp)]
    other = [lax.ppermute(piece, "exp", pairs) for piece in own]
    return own + other, (tokens_grad, *tied[4:])


def on_device(
    tokens, segment_ids, buckets, routes, attention_gain, query_weight, key_weight, value_weight,
    output_weight, bias_table, expert_gain, router_weight, expert_up, expert_down, out_grad,
):
    n_ctx, n_exp = lax.axis_size("ctx"), lax.axis_size("exp")
    rows, width = tokens.shape[1:]
    length = buckets.shape[0]
    experts = router_weight.shape[1]
    capacity = 5 * rows // (2 * experts)
    slots = experts * capacity
    hidden_units = expert_up.shape[2]
    head = lax.axis_index("ctx")
    gain_one = attention_gain.reshape(1, width)
    gain_two = expert_gain.reshape(1, width)
    bucket_row = buckets.reshape(1, length)
    table = jnp.pad(bias_table, ((0, 0), (0, n_ctx - HEADS)))
    tab = lax.dynamic_slice_in_dim(table, head, 1, axis=1)

    up_down = jnp.concatenate([expert_up[:, 0], expert_down[:, 0]], axis=1)
    weights = lax.all_gather(up_down, "ctx", axis=0, tiled=True)

    x = tokens[0]
    qkv, hidden = call(
        project_kernel,
        60,
        (sds((n_ctx, 2 * QA + HEAD_DIM, rows), bf16), sds((rows, width), bf16)),
        flops=6 * rows * width * width,
        moved=4 * MB,
    )(x, gain_one, segment_ids, query_weight, key_weight, value_weight)
    qkv = lax.all_to_all(qkv, "ctx", split_axis=0, concat_axis=0, tiled=True)
    at = jnp.minimum(head, HEADS - 1) * HEAD_DIM
    own_weights = jnp.concatenate(
        [
            lax.dynamic_slice_in_dim(w, at, HEAD_DIM, axis=1).T
            for w in (query_weight, key_weight, value_weight)
        ],
        axis=0,
    )
    qkv, own_weights = lax.optimization_barrier((qkv, own_weights))
    hidden_all = lax.all_gather(hidden, "ctx", axis=0, tiled=True)

    tiles = length // TQ
    ot, otf, lse = call(
        attend_kernel,
        60,
        (
            sds((n_ctx, HEAD_DIM, rows), bf16),
            sds((tiles, HEAD_DIM, TQ), f32),
            sds((tiles, 1, TQ), f32),
        ),
        scratch_shapes=[
            pltpu.VMEM((tiles // 2, 2 * TQ, QA), bf16),
            pltpu.VMEM((tiles + 1, TQ, TQ), f32),
        ],
        flops=8 * 10**9,
        moved=10 * MB,
    )(qkv, bucket_row, tab)
    ot = lax.all_to_all(ot, "ctx", split_axis=0, concat_axis=0, tiled=True)

    routed = routes[0]
    grads_in = out_grad[0]
    send, residual, gates, hidden_two = call(
        route_kernel,
        60,
        (
            sds((slots, 2 * width), bf16),
            sds((rows, width), f32),
            sds((rows, 256), f32),
            sds((rows, width), bf16),
        ),
        flops=10**9,
        moved=4 * MB,
    )(ot, x, output_weight, gain_two, router_weight, routed.T, routed, grads_in)
    received = lax.all_to_all(send, "exp", split_axis=0, concat_axis=0, tiled=True)

    chunk = 512
    steps = hidden_units // chunk
    whole = lambda shape: pl.BlockSpec(shape, lambda i: (0, 0))
    result, pre, act = call(
        expert_kernel,
        60,
        (
            sds((slots, 2 * width), bf16),
            sds((slots, hidden_units), bf16),
            sds((slots, hidden_units), bf16),
        ),
        grid=(steps,),
        in_specs=[
            whole((slots, 2 * width)),
            pl.BlockSpec((width, chunk), lambda i: (0, i)),
            pl.BlockSpec((width, chunk), lambda i: (0, steps + i)),
        ],
        out_specs=[
            whole((slots, 2 * width)),
            pl.BlockSpec((slots, chunk), lambda i: (0, i)),
            pl.BlockSpec((slots, chunk), lambda i: (0, i)),
        ],
        scratch_shapes=[pltpu.VMEM((slots, width), f32), pltpu.VMEM((slots, width), f32)],
        flops=8 * slots * width * hidden_units,
        moved=16 * MB,
    )(received, weights, weights)
    returned = lax.all_to_all(result, "exp", split_axis=0, concat_axis=0, tiled=True)
    weight_grads = call(
        expert_grad_kernel,
        60,
        sds((width, 2 * hidden_units), bf16),
        grid=(2 * steps,),
        in_specs=[
            whole((slots, 2 * width)),
            pl.BlockSpec((slots, chunk), lambda i: (0, jnp.minimum(i, steps - 1))),
            pl.BlockSpec((slots, chunk), lambda i: (0, jnp.maximum(i - steps, 0))),
        ],
        out_specs=pl.BlockSpec((width, chunk), lambda i: (0, i)),
        scratch_shapes=[pltpu.VMEM((width, slots), bf16)],
        flops=4 * slots * width * hidden_units,
        moved=16 * MB,
    )(received, pre, act)
    returned, weight_grads = lax.optimization_barrier((returned, weight_grads))

    layer_out, residual_grad, gt, wo_grad, small = call(
        combine_kernel,
        60,
        (
            sds((rows, width), bf16),
            sds((rows, width), f32),
            sds((n_ctx, HEAD_DIM, rows), bf16),
            sds((width, width), bf16),
            sds((16, width), f32),
        ),
        flops=10**9,
        moved=6 * MB,
    )(
        returned, residual, grads_in, gates, hidden_two, routed, gain_two,
        router_weight.astype(f32).T, output_weight, ot,
    )
    gt = lax.all_to_all(gt, "ctx", split_axis=0, concat_axis=0, tiled=True)
    weight_grads, hidden_all, gt = lax.optimization_barrier((weight_grads, hidden_all, gt))
    summed = lax.psum_scatter(weight_grads, "ctx", scatter_dimension=0, tiled=True)
    wo_parts = lax.all_to_all(
        wo_grad.reshape(n_ctx, width // n_ctx, width), "ctx", split_axis=0, concat_axis=0, tiled=True
    )

    dqkv, flat, bias_grad = call(
        attend_back_kernel,
        60,
        (
            sds((n_ctx, 3 * HEAD_DIM, rows), bf16),
            sds((3 * HEAD_DIM, length), bf16),
            sds((8, 128), f32),
        ),
        scratch_shapes=[
            pltpu.VMEM((tiles // 2, 2 * TQ, QA), bf16),
            pltpu.VMEM((tiles // 2, 2 * TQ, HEAD_DIM), bf16),
            pltpu.VMEM((tiles + 1, TQ, TQ), f32),
            pltpu.VMEM((tiles + 1, TQ, TQ), f32),
            pltpu.VMEM((tiles // 2, HEAD_DIM, 2 * TQ), f32),
            pltpu.VMEM((tiles // 2, HEAD_DIM, 2 * TQ), f32),
        ],
        flops=20 * 10**9,
        moved=20 * MB,
    )(qkv, gt, otf, lse, bucket_row, tab)

    packed = call(
        pack_kernel,
        60,
        sds((ROWS, width), bf16),
        grid=(4,),
        in_specs=[
            pl.BlockSpec((3 * HEAD_DIM, length // 4), lambda i: (0, i)),
            pl.BlockSpec((length // 4, width), lambda i: (i, 0)),
            whole((3 * HEAD_DIM, width)),
            whole((1, width)),
            pl.BlockSpec((n_ctx // 4, width // n_ctx, width), lambda i: (i, 0, 0)),
            whole((16, width)),
            whole((8, 128)),
        ],
        out_specs=whole((ROWS, width)),
        scratch_shapes=[
            pltpu.VMEM((3 * HEAD_DIM, width), f32),
            pltpu.VMEM((width // n_ctx, width), f32),
        ],
        flops=6 * length * width * HEAD_DIM,
        moved=6 * MB,
    )(flat, hidden_all, own_weights, gain_one, wo_parts, small, bias_grad)
    parts = lax.all_to_all(
        packed.reshape(n_exp, ROWS // n_exp, width), "exp", split_axis=0, concat_axis=0, tiled=True
    )
    parts, dqkv = lax.optimization_barrier((parts, dqkv))
    back = lax.all_to_all(dqkv, "ctx", split_axis=0, concat_axis=0, tiled=True)
    share = jnp.sum(parts.astype(f32), axis=0).astype(bf16)
    first, second = gather_near_all(share, n_ctx, n_exp)
    first, second, back = lax.optimization_barrier((first, second, back))
    tokens_grad = call(
        tokens_kernel,
        60,
        sds((rows, width), f32),
        flops=6 * rows * width * width,
        moved=6 * MB,
    )(back, x, gain_one, residual_grad, query_weight, key_weight, value_weight)
    own_rows = sds((summed.shape[0], 1, hidden_units), f32)
    ups, downs = call(
        widen_kernel,
        60,
        (own_rows, own_rows),
        grid=(summed.shape[0] // 16,),
        in_specs=[pl.BlockSpec((16, 2 * hidden_units), lambda i: (i, 0))],
        out_specs=[pl.BlockSpec((16, 1, hidden_units), lambda i: (i, 0, 0))] * 2,
        moved=2 * MB,
    )(summed)
    everything, (tokens_grad, ups, downs) = gather_far(
        first, second, n_ctx, n_exp, (tokens_grad, ups, downs)
    )

    full = sds((width, width), f32)
    column = pl.BlockSpec((width, 128), lambda i, w: (0, i))
    exp = lax.axis_index("exp")
    where = jnp.stack([head % 4, head // 4, exp // 2, exp % 2]).astype(jnp.int32)
    query_grad, key_grad, value_grad, output_grad, tails, bias_rows = call(
        unpack_kernel,
        60,
        (
            full,
            full,
            full,
            full,
            sds((16, width), f32),
            sds((HEADS // 2, 16, 128), f32),
        ),
        grid_spec=pltpu.PrefetchScalarGridSpec(
            num_scalar_prefetch=1,
            grid=(HEADS // 2,),
            in_specs=[pl.BlockSpec(memory_space=pl.ANY) for _ in everything],
            out_specs=[
                column,
                column,
                column,
                pl.BlockSpec((144, width), lambda i, w: (i, 0)),
                pl.BlockSpec((16, width), lambda i, w: (0, 0)),
                pl.BlockSpec((1, 16, 128), lambda i, w: (i, 0, 0)),
            ],
            scratch_shapes=[
                pltpu.VMEM((2, 2, 4, 4, 4, 16, width), bf16),
                pltpu.SemaphoreType.DMA((20,)),
            ],
        ),
        moved=16 * MB,
    )(where, *[ring_rows(piece) for piece in everything])
    table_grad = bias_rows.reshape(HEADS, 8, 128)[:, 2, : bias_table.shape[0]].T
    return (
        layer_out[None],
        tokens_grad[None],
        tails[0],
        query_grad,
        key_grad,
        value_grad,
        output_grad,
        table_grad,
        tails[1],
        tails[8:].T,
        ups,
        downs,
    )


def solution(mesh):
    placed = (
        P("exp", "ctx", None),
        P("exp", "ctx"),
        P(),
        P("exp", "ctx", None),
        P(),
        P(),
        P(),
        P(),
        P(),
        P(),
        P(),
        P(),
        P("ctx", "exp", None),
        P("ctx", "exp", None),
        P("exp", "ctx", None),
    )
    return jax.shard_map(
        on_device,
        mesh=mesh,
        in_specs=placed,
        out_specs=(
            P("exp", "ctx", None),
            P("exp", "ctx", None),
            P(),
            P(),
            P(),
            P(),
            P(),
            P(),
            P(),
            P(),
            P("ctx", "exp", None),
            P("ctx", "exp", None),
        ),
        check_vma=False,
    )
```

```python
import jax
import jax.numpy as jnp
from jax import lax
from jax.experimental import pallas as pl
from jax.experimental.pallas import tpu as pltpu
from jax.sharding import PartitionSpec as P

HEADS = 12
HEAD_DIM = 64
EPS = 1e-06
NEG = -1e30
BIG = 2.0**99
SCALE = HEAD_DIM ** (-0.5)
AUG = 16
ROWS = 256
f32 = jnp.float32
bf16 = jnp.bfloat16
MB = 1024 * 1024


def nn(a, b):
    return lax.dot_general(a, b, (((1,), (0,)), ((), ())), preferred_element_type=f32)


def nt(a, b):
    return lax.dot_general(a, b, (((1,), (1,)), ((), ())), preferred_element_type=f32)


def tn(a, b):
    return lax.dot_general(a, b, (((0,), (0,)), ((), ())), preferred_element_type=f32)


def call(kernel, vmem, out_shape, flops=0, moved=0, **kw):
    return pl.pallas_call(
        kernel,
        out_shape=out_shape,
        compiler_params=pltpu.CompilerParams(vmem_limit_bytes=vmem * MB),
        cost_estimate=pl.CostEstimate(flops=flops, bytes_accessed=moved, transcendentals=0),
        **kw,
    )


def sds(shape, dtype):
    return jax.ShapeDtypeStruct(shape, dtype)


def inv_rms(value):
    return lax.rsqrt(jnp.mean(value * value, axis=-1, keepdims=True) + EPS)


def project_kernel(tok_ref, gain_ref, seg_ref, wq_ref, wk_ref, wv_ref, out_ref, hid_ref):
    x = tok_ref[...].astype(f32)
    hidden = (x * inv_rms(x) * gain_ref[...]).astype(bf16)
    hid_ref[...] = hidden
    tokens = x.shape[0]
    heads = out_ref.shape[0]

    def put(weight_ref, at, factor):
        t = (nn(hidden, weight_ref[...]).astype(bf16).astype(f32) * factor).T.astype(bf16)
        out_ref[0:HEADS, at : at + HEAD_DIM, :] = t.reshape(HEADS, HEAD_DIM, tokens)
        out_ref[HEADS:, at : at + HEAD_DIM, :] = jnp.zeros((heads - HEADS, HEAD_DIM, tokens), bf16)

    put(wq_ref, 0, SCALE)
    put(wk_ref, HEAD_DIM + AUG, 1.0)
    put(wv_ref, 2 * (HEAD_DIM + AUG), 1.0)
    s = jnp.broadcast_to(seg_ref[...].astype(f32), (AUG, tokens))
    row = lax.broadcasted_iota(jnp.int32, (AUG, tokens), 0)
    q_rows = jnp.where(row == 0, s * BIG, jnp.where(row == 1, (1.0 - s) * BIG, 0.0)).astype(bf16)
    k_rows = jnp.where(
        row == 0, s - 1.0, jnp.where(row == 1, -s, jnp.where(row < 5, 1.0, 0.0))
    ).astype(bf16)
    full = (heads, AUG, tokens)
    out_ref[:, HEAD_DIM : HEAD_DIM + AUG, :] = jnp.broadcast_to(q_rows[None], full)
    out_ref[:, 2 * HEAD_DIM + AUG : 2 * (HEAD_DIM + AUG), :] = jnp.broadcast_to(k_rows[None], full)


QA = HEAD_DIM + AUG
TQ = 256


def bias_tiles(bucket_ref, tab_ref, tile_ref):
    length = bucket_ref.shape[1]
    buckets = bucket_ref[...]
    nb = tab_ref.shape[0]
    hot = jnp.broadcast_to(buckets, (nb, length)) == lax.broadcasted_iota(
        jnp.int32, (nb, length), 0
    )
    b = jnp.sum(jnp.where(hot, tab_ref[...], 0.0), axis=0, keepdims=True)
    w = jnp.concatenate([jnp.full((1, TQ), NEG, f32), b], axis=1)
    x = jnp.broadcast_to(w, (8, length + TQ))
    row = lax.broadcasted_iota(jnp.int32, x.shape, 0)
    for bit in (1, 2, 4):
        x = jnp.where((row & bit) > 0, pltpu.roll(x, bit, axis=1), x)
    for bit in (8, 16, 32, 64):
        x = jnp.concatenate([x, pltpu.roll(x, bit, axis=1)], axis=0)
    tiles = length // TQ
    for d in range(tiles):
        at = (d + 1) * TQ
        tile_ref[tiles - 1 - d, 0:128, :] = x[:, at : at + TQ]
        tile_ref[tiles - 1 - d, 128:256, :] = x[:, at - 128 : at - 128 + TQ]
    tile_ref[tiles] = jnp.full((TQ, TQ), NEG, f32)


def transposed(block):
    return block.astype(f32).T.astype(bf16)


def pair(ref, index, at, size, count=2):
    return jnp.concatenate(
        [ref[count * index + k, at : at + size, :] for k in range(count)], axis=1
    )


def boundary(recv_ref):
    ones = recv_ref[:, QA + HEAD_DIM : QA + HEAD_DIM + AUG, :].astype(f32)
    row = lax.broadcasted_iota(jnp.int32, ones.shape, 1)
    total = jnp.sum(jnp.where(row == 1, ones, 0.0))
    return recv_ref.shape[0] * recv_ref.shape[2] + total.astype(jnp.int32)


def first_chunk(qb, edge):
    return jnp.where(qb * TQ >= edge, edge // (2 * TQ), 0)


def attend_kernel(recv_ref, bucket_ref, tab_ref, ot_ref, otf_ref, lse_ref, kn_ref, tile_ref):
    blocks = recv_ref.shape[0]
    bias_tiles(bucket_ref, tab_ref, tile_ref)
    for c in range(blocks):
        kn_ref[c // 4, (c % 4) * 128 : (c % 4) * 128 + 128, :] = transposed(
            recv_ref[c, QA : 2 * QA, :]
        )
    edge = boundary(recv_ref)
    last = blocks // 2 - 1

    def one_query_tile(qb, carry):
        qt = pair(recv_ref, qb, 0, QA)

        def one_key_tile(i, state):
            top, total, acc = state
            kc = qb // 2 - i
            bias = tile_ref[pl.ds(last - qb + 2 * kc, 2)].reshape(2 * TQ, TQ)
            s = nn(kn_ref[kc], qt) + bias
            new_top = jnp.maximum(top, jnp.max(s, axis=0, keepdims=True))
            p = jnp.exp(s - new_top)
            factor = jnp.exp(top - new_top)
            total = total * factor + jnp.sum(p, axis=0, keepdims=True)
            acc = acc * factor + nn(pair(recv_ref, kc, 2 * QA, HEAD_DIM, 4), p.astype(bf16))
            return new_top, total, acc

        start = (jnp.full((1, TQ), NEG, f32), jnp.zeros((1, TQ), f32), jnp.zeros((HEAD_DIM, TQ), f32))
        turns = qb // 2 - first_chunk(qb, edge) + 1
        top, total, acc = lax.fori_loop(0, turns, one_key_tile, start)
        o = acc / total
        otf_ref[qb] = o
        lse_ref[qb] = top + jnp.log(total)
        low = o.astype(bf16)
        ot_ref[2 * qb] = low[:, :128]
        ot_ref[2 * qb + 1] = low[:, 128:]
        return carry

    lax.fori_loop(0, blocks // 2, one_query_tile, 0)


def attend_back_kernel(
    recv_ref, gt_ref, otf_ref, lse_ref, bucket_ref, tab_ref,
    out_ref, flat_ref, bias_ref,
    kn_ref, vn_ref, tile_ref, dtile_ref, dk_ref, dv_ref,
):
    blocks = recv_ref.shape[0]
    tiles = blocks // 2
    bias_tiles(bucket_ref, tab_ref, tile_ref)
    for c in range(blocks):
        at = (c % 4) * 128
        kn_ref[c // 4, at : at + 128, :] = transposed(recv_ref[c, QA : 2 * QA, :])
        vn_ref[c // 4, at : at + 128, :] = transposed(recv_ref[c, 2 * QA : 2 * QA + HEAD_DIM, :])
    edge = boundary(recv_ref)
    dtile_ref[...] = jnp.zeros_like(dtile_ref)
    dk_ref[...] = jnp.zeros_like(dk_ref)
    dv_ref[...] = jnp.zeros_like(dv_ref)

    def one_query_tile(qb, carry):
        qt = pair(recv_ref, qb, 0, QA)
        gt = pair(gt_ref, qb, 0, HEAD_DIM)
        lse = lse_ref[qb]
        delta = jnp.sum(gt.astype(f32) * otf_ref[qb], axis=0, keepdims=True)

        def one_key_tile(i, acc):
            kc = qb // 2 - i
            place = pl.ds(tiles - 1 - qb + 2 * kc, 2)
            p = jnp.exp(nn(kn_ref[kc], qt) + tile_ref[place].reshape(2 * TQ, TQ) - lse)
            dp = nn(vn_ref[kc], gt)
            ds = (p * (dp - delta)).astype(bf16)
            dtile_ref[place] += ds.astype(f32).reshape(2, TQ, TQ)
            dv_ref[kc] += nt(gt, p.astype(bf16))
            dk_ref[kc] += nt(qt[:HEAD_DIM], ds)
            return acc + nn(pair(recv_ref, kc, QA, HEAD_DIM, 4), ds)

        acc = lax.fori_loop(
            0, qb // 2 - first_chunk(qb, edge) + 1, one_key_tile, jnp.zeros((HEAD_DIM, TQ), f32)
        )
        low = (acc * SCALE).astype(bf16)
        out_ref[2 * qb, 0:HEAD_DIM, :] = low[:, :128]
        out_ref[2 * qb + 1, 0:HEAD_DIM, :] = low[:, 128:]
        return carry

    lax.fori_loop(0, tiles, one_query_tile, 0)
    for c in range(blocks):
        for ref, at in ((dk_ref, HEAD_DIM), (dv_ref, 2 * HEAD_DIM)):
            lanes = slice((c % 4) * 128, (c % 4) * 128 + 128)
            out_ref[c, at : at + HEAD_DIM, :] = ref[c // 4, :, lanes].astype(bf16)
    for c in range(blocks):
        flat_ref[:, c * 128 : (c + 1) * 128] = out_ref[c]
    upper = jnp.concatenate([dtile_ref[tiles - 1 - d, 0:128, :] for d in range(tiles)], axis=1)
    lower = jnp.concatenate([dtile_ref[tiles - 1 - d, 128:256, :] for d in range(tiles)], axis=1)
    pad = jnp.zeros((128, 128), f32)
    x = jnp.concatenate([pad, pad, upper], axis=1) + jnp.concatenate([pad, lower, pad], axis=1)
    wide = x.shape[1]
    for half in (64, 32, 16, 8, 4, 2, 1):
        x = x[0:half] + pltpu.roll(x[half : 2 * half], wide - half, axis=1)
    g = x[:, TQ:]
    nb, length = tab_ref.shape[0], bucket_ref.shape[1]
    hot = jnp.broadcast_to(bucket_ref[...], (nb, length)) == lax.broadcasted_iota(
        jnp.int32, (nb, length), 0
    )
    sums = jnp.sum(jnp.where(hot, jnp.broadcast_to(g, (nb, length)), 0.0), axis=1, keepdims=True)
    column = jnp.concatenate([jnp.broadcast_to(sums, (nb, 128)), jnp.zeros((128 - nb, 128), f32)], axis=0)
    bias_ref[...] = column.T[0:8, :]


def route_kernel(
    ot_ref, tok_ref, wo_ref, gain_ref, router_ref, rt_ref, rcol_ref, grad_ref,
    send_ref, res_ref, gate_ref, hid_ref,
):
    tokens, width = tok_ref.shape
    experts = router_ref.shape[1]
    slots_all = send_ref.shape[0]
    capacity = slots_all // experts
    att = ot_ref[0:HEADS].reshape(width, tokens)
    residual = tok_ref[...].astype(f32) + tn(att, wo_ref[...])
    res_ref[...] = residual
    hidden = (residual * inv_rms(residual) * gain_ref[...]).astype(bf16)
    hid_ref[...] = hidden
    logits = nn(hidden, router_ref[...])
    expert_lane = lax.broadcasted_iota(jnp.int32, (tokens, experts), 1)
    picked = [
        jnp.sum(jnp.where(expert_lane == rcol_ref[:, c : c + 1], logits, 0.0), axis=1, keepdims=True)
        for c in (0, 1)
    ]
    top = jnp.maximum(picked[0], picked[1])
    e0, e1 = jnp.exp(picked[0] - top), jnp.exp(picked[1] - top)
    gates = [e0 / (e0 + e1), e1 / (e0 + e1)]
    gate_ref[...] = jnp.concatenate(
        [jnp.broadcast_to(g, (tokens, 128)) for g in gates], axis=1
    )
    expert_row = lax.broadcasted_iota(jnp.int32, (experts, tokens), 0)
    before = (
        lax.broadcasted_iota(jnp.int32, (tokens, tokens), 0)
        < lax.broadcasted_iota(jnp.int32, (tokens, tokens), 1)
    ).astype(bf16)
    slot_row = lax.broadcasted_iota(jnp.int32, (slots_all, tokens), 0)
    hots = [(expert_row == rt_ref[c : c + 1, :]).astype(f32) for c in (0, 1)]
    counts = jnp.sum(hots[0], axis=1, keepdims=True)
    taken = [nn(hots[0].astype(bf16), before), nn(hots[1].astype(bf16), before) + counts]
    to_slot = []
    for c in (0, 1):
        slot = jnp.sum(hots[c] * taken[c], axis=0, keepdims=True).astype(jnp.int32)
        place = rt_ref[c : c + 1, :] * capacity + slot
        to_slot.append((slot_row == place).astype(bf16))
    send_ref[:, 0:width] = nn(to_slot[0] + to_slot[1], hidden).astype(bf16)
    upstream = grad_ref[...].astype(f32)
    weighted = jnp.concatenate([(g * upstream).astype(bf16) for g in gates], axis=0)
    send_ref[:, width:] = nn(jnp.concatenate(to_slot, axis=1), weighted).astype(bf16)


def combine_kernel(
    ret_ref, res_ref, grad_ref, gate_ref, hid_ref, rcol_ref, gain_ref, router_t_ref, wo_ref, ot_ref,
    layer_ref, rgrad_ref, gt_ref, wo_grad_ref, small_ref,
):
    tokens, width = res_ref.shape
    experts = router_t_ref.shape[0]
    slots_all = ret_ref.shape[0]
    capacity = slots_all // experts
    lane = lax.broadcasted_iota(jnp.int32, (tokens, 128), 1)
    earlier = (
        lax.broadcasted_iota(jnp.int32, (tokens, tokens), 1)
        < lax.broadcasted_iota(jnp.int32, (tokens, tokens), 0)
    ).astype(bf16)
    hots = [(lane == rcol_ref[:, c : c + 1]).astype(f32) for c in (0, 1)]
    counts = jnp.sum(hots[0], axis=0, keepdims=True)
    taken = [nn(earlier, hots[0].astype(bf16)), nn(earlier, hots[1].astype(bf16)) + counts]
    slot_lane = lax.broadcasted_iota(jnp.int32, (tokens, slots_all), 1)
    from_slot = []
    for c in (0, 1):
        slot = jnp.sum(hots[c] * taken[c], axis=1, keepdims=True).astype(jnp.int32)
        place = rcol_ref[:, c : c + 1] * capacity + slot
        from_slot.append((slot_lane == place).astype(bf16))
    outs = [nn(m, ret_ref[:, 0:width]) for m in from_slot]
    row_sum = nn(from_slot[0] + from_slot[1], ret_ref[:, width:])
    gates = [gate_ref[:, 0:1], gate_ref[:, 128:129]]
    residual = res_ref[...]
    layer_ref[...] = (residual + (gates[0] * outs[0] + gates[1] * outs[1])).astype(bf16)
    upstream = grad_ref[...].astype(f32)
    gate_grads = [jnp.sum(upstream * o, axis=1, keepdims=True) for o in outs]
    mixed = gates[0] * gate_grads[0] + gates[1] * gate_grads[1]
    logit_grad = (
        gates[0] * (gate_grads[0] - mixed) * hots[0] + gates[1] * (gate_grads[1] - mixed) * hots[1]
    )
    h2g = row_sum
    for e in range(experts):
        h2g = h2g + logit_grad[:, e : e + 1] * router_t_ref[e : e + 1, :]
    inverse = inv_rms(residual)
    normed = residual * inverse
    logit_t = logit_grad.T
    high = logit_t.astype(bf16)
    rest = (logit_t - high.astype(f32)).astype(bf16)
    router_grad = nn(high, hid_ref[...]) + nn(rest, hid_ref[...])
    small_ref[0:8, :] = jnp.broadcast_to(jnp.sum(h2g * normed, axis=0, keepdims=True), (8, width))
    small_ref[8:16, :] = router_grad[0:experts]
    scaled = h2g * gain_ref[...]
    average = jnp.mean(scaled * normed, axis=-1, keepdims=True)
    residual_grad = upstream + inverse * (scaled - normed * average)
    rgrad_ref[...] = residual_grad
    branch = residual_grad.astype(bf16)
    gt = nt(wo_ref[...], branch).astype(bf16)
    gt_ref[0:HEADS] = gt.reshape(HEADS, HEAD_DIM, tokens)
    gt_ref[HEADS:] = jnp.zeros((gt_ref.shape[0] - HEADS, HEAD_DIM, tokens), bf16)
    att = ot_ref[0:HEADS].reshape(width, tokens)
    wo_grad_ref[...] = nn(att, branch).astype(bf16)


def expert_kernel(rows_ref, up_ref, down_ref, ret_ref, pre_ref, act_ref, out_acc, row_acc):
    step = pl.program_id(0)
    width = up_ref.shape[0]
    rows = rows_ref[:, 0:width]
    grads = rows_ref[:, width:]
    up, down = up_ref[...], down_ref[...]
    x = nn(rows, up)
    c = 0.7978845608028654
    t = jnp.tanh(c * (x + 0.044715 * (x * x * x)))
    hidden = (0.5 * x * (1.0 + t)).astype(bf16)
    slope = 0.5 * (1.0 + t) + 0.5 * x * (1.0 - t * t) * (c * (1.0 + 3 * 0.044715 * (x * x)))
    pre = (nn(grads, down) * slope).astype(bf16)
    act_ref[...] = hidden
    pre_ref[...] = pre
    out_part, row_part = nt(hidden, down), nt(pre, up)

    @pl.when(step == 0)
    def _():
        out_acc[...] = out_part
        row_acc[...] = row_part

    @pl.when(step > 0)
    def _():
        out_acc[...] += out_part
        row_acc[...] += row_part

    @pl.when(step == pl.num_programs(0) - 1)
    def _():
        ret_ref[:, 0:width] = out_acc[...].astype(bf16)
        ret_ref[:, width:] = row_acc[...].astype(bf16)


def expert_grad_kernel(rows_ref, pre_ref, act_ref, out_ref, left_ref):
    step = pl.program_id(0)
    steps = pl.num_programs(0)
    width = out_ref.shape[0]

    @pl.when(step == 0)
    def _():
        left_ref[...] = rows_ref[:, 0:width].astype(f32).T.astype(bf16)

    @pl.when(step == steps // 2)
    def _():
        left_ref[...] = rows_ref[:, width:].astype(f32).T.astype(bf16)

    @pl.when(step < steps // 2)
    def _():
        out_ref[...] = nn(left_ref[...], pre_ref[...]).astype(bf16)

    @pl.when(step >= steps // 2)
    def _():
        out_ref[...] = nn(left_ref[...], act_ref[...]).astype(bf16)


def pack_kernel(flat_ref, hid_ref, wt_ref, gain_ref, wo_ref, small_ref, bias_ref, out_ref):
    width = hid_ref.shape[1]
    grad = nn(flat_ref[...], hid_ref[...])
    part = jnp.sum(grad * wt_ref[...].astype(f32), axis=0, keepdims=True) / gain_ref[...]
    out_ref[0:192, :] = grad.astype(bf16)
    wo = wo_ref[0].astype(f32)
    for c in range(1, wo_ref.shape[0]):
        wo = wo + wo_ref[c].astype(f32)
    out_ref[192:240, :] = wo.astype(bf16)
    bias = jnp.concatenate([bias_ref[...], jnp.zeros((8, width - 128), f32)], axis=1)
    row = lax.broadcasted_iota(jnp.int32, (8, width), 0)
    first = jnp.where(
        row == 0, jnp.broadcast_to(part, (8, width)), jnp.where(row == 1, small_ref[0:8, :], bias)
    )
    out_ref[240:256, :] = jnp.concatenate([first, small_ref[8:16, :]], axis=0).astype(bf16)


def tokens_kernel(recv_ref, tok_ref, gain_ref, rgrad_ref, wq_ref, wk_ref, wv_ref, out_ref):
    tokens, width = tok_ref.shape
    acc = None
    for weight_ref, at in ((wq_ref, 0), (wk_ref, HEAD_DIM), (wv_ref, 2 * HEAD_DIM)):
        grad = recv_ref[0:HEADS, at : at + HEAD_DIM, :].reshape(width, tokens)
        part = nn(weight_ref[...], grad)
        acc = part if acc is None else acc + part
    hidden_grad = acc.T
    x = tok_ref[...].astype(f32)
    inverse = inv_rms(x)
    normed = x * inverse
    scaled = hidden_grad * gain_ref[...]
    average = jnp.mean(scaled * normed, axis=-1, keepdims=True)
    out_ref[...] = rgrad_ref[...] + inverse * (scaled - normed * average)


def ring_rows(piece):
    rows, width = piece.shape
    shape = (4, 4, 16, width) if rows == 256 else (2, 4, 16, width)
    return piece.reshape(shape)


def unpack_kernel(where_ref, sum_ref, *refs):
    pieces, (q_ref, k_ref, v_ref, wo_ref, gain_ref, router_ref, table_ref) = refs[:20], refs[20:27]
    up_ref, down_ref, all_ref, sems = refs[27:]
    units = up_ref.shape[2]
    up_ref[:, 0, :] = sum_ref[:, 0:units].astype(f32)
    down_ref[:, 0, :] = sum_ref[:, units:].astype(f32)
    step = pl.program_id(0)
    x, y, z, core = where_ref[0], where_ref[1], where_ref[2], where_ref[3]

    @pl.when(step == 0)
    def _():
        copies = []
        for k in range(4):
            slot = all_ref.at[k // 2, k % 2]
            places = [slot.at[0], slot.at[1], slot.at[2, 0:2], slot.at[2, 2:4], slot.at[3]]
            for j, place in enumerate(places):
                n = 5 * k + j
                copies.append(pltpu.make_async_copy(pieces[n], place, sems.at[n]))
        for copy in copies:
            copy.start()
        for copy in copies:
            copy.wait()

    def rows(c, group):
        exp, half = group // 2, group % 2
        dx, dy = (x - c % 4 + 4) % 4, (y - c // 4 + 4) % 4
        dz, other = (z - exp // 2 + 4) % 4, (core + exp % 2) % 2
        first, second = (dy, dx) if half == 0 else (dx, dy)
        return all_ref[other, half, first, second, dz]

    def span(c, start, stop):
        return jnp.concatenate([rows(c, g) for g in range(start // 16, stop // 16)], axis=0)

    for ref, at in ((q_ref, 0), (k_ref, HEAD_DIM), (v_ref, 2 * HEAD_DIM)):
        both = [span(2 * step, at, at + HEAD_DIM), span(2 * step + 1, at, at + HEAD_DIM)]
        ref[...] = jnp.concatenate(both, axis=0).astype(f32).T
    @pl.when(step < 4)
    def _():
        for k in range(4):
            wo_ref[48 * k : 48 * k + 48, :] = span(4 * step + k, 192, 240).astype(f32)

    @pl.when(step == 0)
    def _():
        tails = [rows(c, 15).astype(f32) for c in range(16)]
        total = tails[0]
        for part in tails[1:]:
            total = total + part
        gain_ref[...] = total[0:8]
        router_ref[...] = jnp.concatenate([total, total], axis=0).T[:, 8:16]
        table = jnp.concatenate(
            [part[2:3, 0:128] for part in tails[:HEADS]] + [jnp.zeros((128 - HEADS, 128), f32)], axis=0
        )
        table_ref[...] = table.T[0 : table_ref.shape[0], 0:HEADS]


def ring(axis, stride, size, block, distance):
    def to(i):
        place = (i // stride) % 4
        return i + ((place + distance) % 4 - place) * stride

    return lax.ppermute(block, axis, [(i, to(i)) for i in range(size)])


def gather_ring(axis, stride, size, block):
    half = block.shape[0] // 2
    ahead = ring(axis, stride, size, block, 1)
    behind = ring(axis, stride, size, block, -1)
    far_one = ring(axis, stride, size, ahead[:half], 1)
    far_two = ring(axis, stride, size, behind[half:], -1)
    return [block, ahead, far_one, far_two, behind]


def gather_near(axis, stride, size, block):
    return [block] + [ring(axis, stride, size, block, d) for d in (1, 2, 3)]


def split_kernel(*refs):
    pieces, outs = refs[:4], refs[4:]
    for half, out in enumerate(outs):
        for d, ref in enumerate(pieces):
            block = ref[...]
            out[16 * d : 16 * d + 16, :] = block[16 * half : 16 * half + 16]


def join_kernel(*refs):
    for k in range(2):
        for d, ref in enumerate(refs[4 * k : 4 * k + 4]):
            size = ref.shape[0]
            refs[8 + k][d * size : (d + 1) * size, :] = ref[...]


def gather_near_all(share, n_ctx, n_exp):
    width = share.shape[1]
    along_z = gather_near("exp", 2, n_exp, share)
    quarter = sds((64, width), bf16)
    first, second = call(split_kernel, 8, (quarter, quarter))(*along_z)
    plane = gather_near("ctx", 1, n_ctx, first) + gather_near("ctx", 4, n_ctx, second)
    side = sds((256, width), bf16)
    return call(join_kernel, 8, (side, side))(*plane)


def gather_far(first, second, n_ctx, n_exp, done):
    own = gather_ring("ctx", 4, n_ctx, first) + gather_ring("ctx", 1, n_ctx, second)
    own[0], own[5], done = lax.optimization_barrier((own[0], own[5], done))
    pairs = [(i, i ^ 1) for i in range(n_exp)]
    return own + [lax.ppermute(piece, "exp", pairs) for piece in own], done


def on_device(
    tokens, segment_ids, buckets, routes, attention_gain, query_weight, key_weight, value_weight,
    output_weight, bias_table, expert_gain, router_weight, expert_up, expert_down, out_grad,
):
    n_ctx, n_exp = lax.axis_size("ctx"), lax.axis_size("exp")
    rows, width = tokens.shape[1:]
    length = buckets.shape[0]
    experts = router_weight.shape[1]
    capacity = 5 * rows // (2 * experts)
    slots = experts * capacity
    hidden_units = expert_up.shape[2]
    head = lax.axis_index("ctx")
    gain_one = attention_gain.reshape(1, width)
    gain_two = expert_gain.reshape(1, width)
    bucket_row = buckets.reshape(1, length)
    table = jnp.pad(bias_table, ((0, 0), (0, n_ctx - HEADS)))
    tab = lax.dynamic_slice_in_dim(table, head, 1, axis=1)

    up_down = jnp.concatenate([expert_up[:, 0], expert_down[:, 0]], axis=1)
    weights = lax.all_gather(up_down, "ctx", axis=0, tiled=True)

    x = tokens[0]
    qkv, hidden = call(
        project_kernel,
        60,
        (sds((n_ctx, 2 * QA + HEAD_DIM, rows), bf16), sds((rows, width), bf16)),
        flops=6 * rows * width * width,
        moved=4 * MB,
    )(x, gain_one, segment_ids, query_weight, key_weight, value_weight)
    qkv = lax.all_to_all(qkv, "ctx", split_axis=0, concat_axis=0, tiled=True)
    at = jnp.minimum(head, HEADS - 1) * HEAD_DIM
    own_weights = jnp.concatenate(
        [
            lax.dynamic_slice_in_dim(w, at, HEAD_DIM, axis=1).T
            for w in (query_weight, key_weight, value_weight)
        ],
        axis=0,
    )
    qkv, own_weights = lax.optimization_barrier((qkv, own_weights))
    hidden_all = lax.all_gather(hidden, "ctx", axis=0, tiled=True)

    tiles = length // TQ
    ot, otf, lse = call(
        attend_kernel,
        60,
        (
            sds((n_ctx, HEAD_DIM, rows), bf16),
            sds((tiles, HEAD_DIM, TQ), f32),
            sds((tiles, 1, TQ), f32),
        ),
        scratch_shapes=[
            pltpu.VMEM((tiles // 2, 2 * TQ, QA), bf16),
            pltpu.VMEM((tiles + 1, TQ, TQ), f32),
        ],
        flops=8 * 10**9,
        moved=10 * MB,
    )(qkv, bucket_row, tab)
    ot = lax.all_to_all(ot, "ctx", split_axis=0, concat_axis=0, tiled=True)

    routed = routes[0]
    grads_in = out_grad[0]
    send, residual, gates, hidden_two = call(
        route_kernel,
        60,
        (
            sds((slots, 2 * width), bf16),
            sds((rows, width), f32),
            sds((rows, 256), f32),
            sds((rows, width), bf16),
        ),
        flops=10**9,
        moved=4 * MB,
    )(ot, x, output_weight, gain_two, router_weight, routed.T, routed, grads_in)
    received = lax.all_to_all(send, "exp", split_axis=0, concat_axis=0, tiled=True)

    chunk = 512
    steps = hidden_units // chunk
    whole = lambda shape: pl.BlockSpec(shape, lambda i: (0, 0))
    result, pre, act = call(
        expert_kernel,
        60,
        (
            sds((slots, 2 * width), bf16),
            sds((slots, hidden_units), bf16),
            sds((slots, hidden_units), bf16),
        ),
        grid=(steps,),
        in_specs=[
            whole((slots, 2 * width)),
            pl.BlockSpec((width, chunk), lambda i: (0, i)),
            pl.BlockSpec((width, chunk), lambda i: (0, steps + i)),
        ],
        out_specs=[
            whole((slots, 2 * width)),
            pl.BlockSpec((slots, chunk), lambda i: (0, i)),
            pl.BlockSpec((slots, chunk), lambda i: (0, i)),
        ],
        scratch_shapes=[pltpu.VMEM((slots, width), f32), pltpu.VMEM((slots, width), f32)],
        flops=8 * slots * width * hidden_units,
        moved=16 * MB,
    )(received, weights, weights)
    returned = lax.all_to_all(result, "exp", split_axis=0, concat_axis=0, tiled=True)
    weight_grads = call(
        expert_grad_kernel,
        60,
        sds((width, 2 * hidden_units), bf16),
        grid=(2 * steps,),
        in_specs=[
            whole((slots, 2 * width)),
            pl.BlockSpec((slots, chunk), lambda i: (0, jnp.minimum(i, steps - 1))),
            pl.BlockSpec((slots, chunk), lambda i: (0, jnp.maximum(i - steps, 0))),
        ],
        out_specs=pl.BlockSpec((width, chunk), lambda i: (0, i)),
        scratch_shapes=[pltpu.VMEM((width, slots), bf16)],
        flops=4 * slots * width * hidden_units,
        moved=16 * MB,
    )(received, pre, act)
    returned, weight_grads = lax.optimization_barrier((returned, weight_grads))

    layer_out, residual_grad, gt, wo_grad, small = call(
        combine_kernel,
        60,
        (
            sds((rows, width), bf16),
            sds((rows, width), f32),
            sds((n_ctx, HEAD_DIM, rows), bf16),
            sds((width, width), bf16),
            sds((16, width), f32),
        ),
        flops=10**9,
        moved=6 * MB,
    )(
        returned, residual, grads_in, gates, hidden_two, routed, gain_two,
        router_weight.astype(f32).T, output_weight, ot,
    )
    gt = lax.all_to_all(gt, "ctx", split_axis=0, concat_axis=0, tiled=True)
    weight_grads, hidden_all, gt = lax.optimization_barrier((weight_grads, hidden_all, gt))
    summed = lax.psum_scatter(weight_grads, "ctx", scatter_dimension=0, tiled=True)
    wo_parts = lax.all_to_all(
        wo_grad.reshape(n_ctx, width // n_ctx, width), "ctx", split_axis=0, concat_axis=0, tiled=True
    )

    dqkv, flat, bias_grad = call(
        attend_back_kernel,
        60,
        (
            sds((n_ctx, 3 * HEAD_DIM, rows), bf16),
            sds((3 * HEAD_DIM, length), bf16),
            sds((8, 128), f32),
        ),
        scratch_shapes=[
            pltpu.VMEM((tiles // 2, 2 * TQ, QA), bf16),
            pltpu.VMEM((tiles // 2, 2 * TQ, HEAD_DIM), bf16),
            pltpu.VMEM((tiles + 1, TQ, TQ), f32),
            pltpu.VMEM((tiles + 1, TQ, TQ), f32),
            pltpu.VMEM((tiles // 2, HEAD_DIM, 2 * TQ), f32),
            pltpu.VMEM((tiles // 2, HEAD_DIM, 2 * TQ), f32),
        ],
        flops=20 * 10**9,
        moved=20 * MB,
    )(qkv, gt, otf, lse, bucket_row, tab)

    packed = call(
        pack_kernel,
        60,
        sds((ROWS, width), bf16),
        flops=6 * length * width * HEAD_DIM,
        moved=6 * MB,
    )(flat, hidden_all, own_weights, gain_one, wo_parts, small, bias_grad)
    parts = lax.all_to_all(
        packed.reshape(n_exp, ROWS // n_exp, width), "exp", split_axis=0, concat_axis=0, tiled=True
    )
    parts, dqkv = lax.optimization_barrier((parts, dqkv))
    back = lax.all_to_all(dqkv, "ctx", split_axis=0, concat_axis=0, tiled=True)
    share = jnp.sum(parts.astype(f32), axis=0).astype(bf16)
    first, second = gather_near_all(share, n_ctx, n_exp)
    first, second, back = lax.optimization_barrier((first, second, back))
    tokens_grad = call(
        tokens_kernel,
        60,
        sds((rows, width), f32),
        flops=6 * rows * width * width,
        moved=6 * MB,
    )(back, x, gain_one, residual_grad, query_weight, key_weight, value_weight)
    everything, tokens_grad = gather_far(first, second, n_ctx, n_exp, tokens_grad)

    full = sds((width, width), f32)
    column = pl.BlockSpec((width, 128), lambda i, w: (0, i))
    exp = lax.axis_index("exp")
    where = jnp.stack([head % 4, head // 4, exp // 2, exp % 2]).astype(jnp.int32)
    own_rows = sds((summed.shape[0], 1, hidden_units), f32)
    own_block = pl.BlockSpec((16, 1, hidden_units), lambda i, w: (jnp.minimum(i, 2), 0, 0))
    once = lambda shape: pl.BlockSpec(shape, lambda i, w: (0, 0))
    query_grad, key_grad, value_grad, output_grad, gains, router_grad, table_grad, ups, downs = call(
        unpack_kernel,
        32,
        (
            full,
            full,
            full,
            full,
            sds((8, width), f32),
            sds(router_weight.shape, f32),
            sds(bias_table.shape, f32),
            own_rows,
            own_rows,
        ),
        grid_spec=pltpu.PrefetchScalarGridSpec(
            num_scalar_prefetch=1,
            grid=(HEADS // 2,),
            in_specs=[pl.BlockSpec((16, 2 * hidden_units), lambda i, w: (jnp.minimum(i, 2), 0))]
            + [pl.BlockSpec(memory_space=pl.ANY) for _ in everything],
            out_specs=[
                column,
                column,
                column,
                pl.BlockSpec((192, width), lambda i, w: (jnp.minimum(i, 3), 0)),
                once((8, width)),
                once(router_weight.shape),
                once(bias_table.shape),
                own_block,
                own_block,
            ],
            scratch_shapes=[
                pltpu.VMEM((2, 2, 4, 4, 4, 16, width), bf16),
                pltpu.SemaphoreType.DMA((20,)),
            ],
        ),
        moved=16 * MB,
    )(where, summed, *[ring_rows(piece) for piece in everything])
    return (
        layer_out[None],
        tokens_grad[None],
        gains[0],
        query_grad,
        key_grad,
        value_grad,
        output_grad,
        table_grad,
        gains[1],
        router_grad,
        ups,
        downs,
    )


def solution(mesh):
    placed = (
        P("exp", "ctx", None),
        P("exp", "ctx"),
        P(),
        P("exp", "ctx", None),
        P(),
        P(),
        P(),
        P(),
        P(),
        P(),
        P(),
        P(),
        P("ctx", "exp", None),
        P("ctx", "exp", None),
        P("exp", "ctx", None),
    )
    return jax.shard_map(
        on_device,
        mesh=mesh,
        in_specs=placed,
        out_specs=(
            P("exp", "ctx", None),
            P("exp", "ctx", None),
            P(),
            P(),
            P(),
            P(),
            P(),
            P(),
            P(),
            P(),
            P("ctx", "exp", None),
            P("ctx", "exp", None),
        ),
        check_vma=False,
    )
```

```python
import jax
import jax.numpy as jnp
from jax import lax
from jax.experimental import pallas as pl
from jax.experimental.pallas import tpu as pltpu
from jax.sharding import PartitionSpec as P

HEADS = 12
HEAD_DIM = 64
EPS = 1e-06
NEG = -1e30
BIG = 2.0**99
SCALE = HEAD_DIM ** (-0.5)
AUG = 16
ROWS = 256
f32 = jnp.float32
bf16 = jnp.bfloat16
MB = 1024 * 1024


def nn(a, b):
    return lax.dot_general(a, b, (((1,), (0,)), ((), ())), preferred_element_type=f32)


def nt(a, b):
    return lax.dot_general(a, b, (((1,), (1,)), ((), ())), preferred_element_type=f32)


def tn(a, b):
    return lax.dot_general(a, b, (((0,), (0,)), ((), ())), preferred_element_type=f32)


def call(kernel, vmem, out_shape, flops=0, moved=0, **kw):
    return pl.pallas_call(
        kernel,
        out_shape=out_shape,
        compiler_params=pltpu.CompilerParams(vmem_limit_bytes=vmem * MB),
        cost_estimate=pl.CostEstimate(flops=flops, bytes_accessed=moved, transcendentals=0),
        **kw,
    )


def sds(shape, dtype):
    return jax.ShapeDtypeStruct(shape, dtype)


def inv_rms(value):
    return lax.rsqrt(jnp.mean(value * value, axis=-1, keepdims=True) + EPS)


def project_kernel(tok_ref, gain_ref, seg_ref, wq_ref, wk_ref, wv_ref, out_ref, hid_ref):
    x = tok_ref[...].astype(f32)
    hidden = (x * inv_rms(x) * gain_ref[...]).astype(bf16)
    hid_ref[...] = hidden
    tokens = x.shape[0]
    heads = out_ref.shape[0]

    def put(weight_ref, at, factor):
        t = (nn(hidden, weight_ref[...]).astype(bf16).astype(f32) * factor).T.astype(bf16)
        out_ref[0:HEADS, at : at + HEAD_DIM, :] = t.reshape(HEADS, HEAD_DIM, tokens)
        out_ref[HEADS:, at : at + HEAD_DIM, :] = jnp.zeros((heads - HEADS, HEAD_DIM, tokens), bf16)

    put(wq_ref, 0, SCALE)
    put(wk_ref, HEAD_DIM + AUG, 1.0)
    put(wv_ref, 2 * (HEAD_DIM + AUG), 1.0)
    s = jnp.broadcast_to(seg_ref[...].astype(f32), (AUG, tokens))
    row = lax.broadcasted_iota(jnp.int32, (AUG, tokens), 0)
    q_rows = jnp.where(row == 0, s * BIG, jnp.where(row == 1, (1.0 - s) * BIG, 0.0)).astype(bf16)
    k_rows = jnp.where(
        row == 0, s - 1.0, jnp.where(row == 1, -s, jnp.where(row < 5, 1.0, 0.0))
    ).astype(bf16)
    full = (heads, AUG, tokens)
    out_ref[:, HEAD_DIM : HEAD_DIM + AUG, :] = jnp.broadcast_to(q_rows[None], full)
    out_ref[:, 2 * HEAD_DIM + AUG : 2 * (HEAD_DIM + AUG), :] = jnp.broadcast_to(k_rows[None], full)


QA = HEAD_DIM + AUG
TQ = 256


def bias_tiles(bucket_ref, tab_ref, tile_ref):
    length = bucket_ref.shape[1]
    buckets = bucket_ref[...]
    nb = tab_ref.shape[0]
    hot = jnp.broadcast_to(buckets, (nb, length)) == lax.broadcasted_iota(
        jnp.int32, (nb, length), 0
    )
    b = jnp.sum(jnp.where(hot, tab_ref[...], 0.0), axis=0, keepdims=True)
    w = jnp.concatenate([jnp.full((1, TQ), NEG, f32), b], axis=1)
    x = jnp.broadcast_to(w, (8, length + TQ))
    row = lax.broadcasted_iota(jnp.int32, x.shape, 0)
    for bit in (1, 2, 4):
        x = jnp.where((row & bit) > 0, pltpu.roll(x, bit, axis=1), x)
    for bit in (8, 16, 32, 64):
        x = jnp.concatenate([x, pltpu.roll(x, bit, axis=1)], axis=0)
    tiles = length // TQ
    for d in range(tiles):
        at = (d + 1) * TQ
        tile_ref[tiles - 1 - d, 0:128, :] = x[:, at : at + TQ]
        tile_ref[tiles - 1 - d, 128:256, :] = x[:, at - 128 : at - 128 + TQ]
    tile_ref[tiles] = jnp.full((TQ, TQ), NEG, f32)


def transposed(block):
    return block.astype(f32).T.astype(bf16)


def pair(ref, index, at, size, count=2):
    return jnp.concatenate(
        [ref[count * index + k, at : at + size, :] for k in range(count)], axis=1
    )


def boundary(recv_ref):
    ones = recv_ref[:, QA + HEAD_DIM : QA + HEAD_DIM + AUG, :].astype(f32)
    row = lax.broadcasted_iota(jnp.int32, ones.shape, 1)
    total = jnp.sum(jnp.where(row == 1, ones, 0.0))
    return recv_ref.shape[0] * recv_ref.shape[2] + total.astype(jnp.int32)


def first_chunk(qb, edge):
    return jnp.where(qb * TQ >= edge, edge // (2 * TQ), 0)


def attend_kernel(recv_ref, bucket_ref, tab_ref, ot_ref, otf_ref, lse_ref, kn_ref, tile_ref):
    blocks = recv_ref.shape[0]
    bias_tiles(bucket_ref, tab_ref, tile_ref)
    for c in range(blocks):
        kn_ref[c // 4, (c % 4) * 128 : (c % 4) * 128 + 128, :] = transposed(
            recv_ref[c, QA : 2 * QA, :]
        )
    edge = boundary(recv_ref)
    last = blocks // 2 - 1

    def one_query_tile(qb, carry):
        qt = pair(recv_ref, qb, 0, QA)

        def one_key_tile(i, state):
            top, total, acc = state
            kc = qb // 2 - i
            bias = tile_ref[pl.ds(last - qb + 2 * kc, 2)].reshape(2 * TQ, TQ)
            s = nn(kn_ref[kc], qt) + bias
            new_top = jnp.maximum(top, jnp.max(s, axis=0, keepdims=True))
            p = jnp.exp(s - new_top)
            factor = jnp.exp(top - new_top)
            total = total * factor + jnp.sum(p, axis=0, keepdims=True)
            acc = acc * factor + nn(pair(recv_ref, kc, 2 * QA, HEAD_DIM, 4), p.astype(bf16))
            return new_top, total, acc

        start = (jnp.full((1, TQ), NEG, f32), jnp.zeros((1, TQ), f32), jnp.zeros((HEAD_DIM, TQ), f32))
        turns = qb // 2 - first_chunk(qb, edge) + 1
        top, total, acc = lax.fori_loop(0, turns, one_key_tile, start)
        o = acc / total
        otf_ref[qb] = o
        lse_ref[qb] = top + jnp.log(total)
        low = o.astype(bf16)
        ot_ref[2 * qb] = low[:, :128]
        ot_ref[2 * qb + 1] = low[:, 128:]
        return carry

    lax.fori_loop(0, blocks // 2, one_query_tile, 0)


def attend_back_kernel(
    recv_ref, gt_ref, otf_ref, lse_ref, bucket_ref, tab_ref,
    out_ref, flat_ref, bias_ref,
    kn_ref, vn_ref, tile_ref, dtile_ref, dk_ref, dv_ref,
):
    blocks = recv_ref.shape[0]
    tiles = blocks // 2
    bias_tiles(bucket_ref, tab_ref, tile_ref)
    for c in range(blocks):
        at = (c % 4) * 128
        kn_ref[c // 4, at : at + 128, :] = transposed(recv_ref[c, QA : 2 * QA, :])
        vn_ref[c // 4, at : at + 128, :] = transposed(recv_ref[c, 2 * QA : 2 * QA + HEAD_DIM, :])
    edge = boundary(recv_ref)
    dtile_ref[...] = jnp.zeros_like(dtile_ref)
    dk_ref[...] = jnp.zeros_like(dk_ref)
    dv_ref[...] = jnp.zeros_like(dv_ref)

    def one_query_tile(qb, carry):
        qt = pair(recv_ref, qb, 0, QA)
        gt = pair(gt_ref, qb, 0, HEAD_DIM)
        lse = lse_ref[qb]
        delta = jnp.sum(gt.astype(f32) * otf_ref[qb], axis=0, keepdims=True)

        def one_key_tile(i, acc):
            kc = qb // 2 - i
            place = pl.ds(tiles - 1 - qb + 2 * kc, 2)
            p = jnp.exp(nn(kn_ref[kc], qt) + tile_ref[place].reshape(2 * TQ, TQ) - lse)
            dp = nn(vn_ref[kc], gt)
            ds = (p * (dp - delta)).astype(bf16)
            dtile_ref[place] += ds.astype(f32).reshape(2, TQ, TQ)
            dv_ref[kc] += nt(gt, p.astype(bf16))
            dk_ref[kc] += nt(qt[:HEAD_DIM], ds)
            return acc + nn(pair(recv_ref, kc, QA, HEAD_DIM, 4), ds)

        acc = lax.fori_loop(
            0, qb // 2 - first_chunk(qb, edge) + 1, one_key_tile, jnp.zeros((HEAD_DIM, TQ), f32)
        )
        low = (acc * SCALE).astype(bf16)
        out_ref[2 * qb, 0:HEAD_DIM, :] = low[:, :128]
        out_ref[2 * qb + 1, 0:HEAD_DIM, :] = low[:, 128:]
        return carry

    lax.fori_loop(0, tiles, one_query_tile, 0)
    for c in range(blocks):
        for ref, at in ((dk_ref, HEAD_DIM), (dv_ref, 2 * HEAD_DIM)):
            lanes = slice((c % 4) * 128, (c % 4) * 128 + 128)
            out_ref[c, at : at + HEAD_DIM, :] = ref[c // 4, :, lanes].astype(bf16)
    for c in range(blocks):
        flat_ref[:, c * 128 : (c + 1) * 128] = out_ref[c]
    upper = jnp.concatenate([dtile_ref[tiles - 1 - d, 0:128, :] for d in range(tiles)], axis=1)
    lower = jnp.concatenate([dtile_ref[tiles - 1 - d, 128:256, :] for d in range(tiles)], axis=1)
    pad = jnp.zeros((128, 128), f32)
    x = jnp.concatenate([pad, pad, upper], axis=1) + jnp.concatenate([pad, lower, pad], axis=1)
    wide = x.shape[1]
    for half in (64, 32, 16, 8, 4, 2, 1):
        x = x[0:half] + pltpu.roll(x[half : 2 * half], wide - half, axis=1)
    g = x[:, TQ:]
    nb, length = tab_ref.shape[0], bucket_ref.shape[1]
    hot = jnp.broadcast_to(bucket_ref[...], (nb, length)) == lax.broadcasted_iota(
        jnp.int32, (nb, length), 0
    )
    sums = jnp.sum(jnp.where(hot, jnp.broadcast_to(g, (nb, length)), 0.0), axis=1, keepdims=True)
    column = jnp.concatenate([jnp.broadcast_to(sums, (nb, 128)), jnp.zeros((128 - nb, 128), f32)], axis=0)
    bias_ref[...] = column.T[0:8, :]


def route_kernel(
    ot_ref, tok_ref, wo_ref, gain_ref, router_ref, rt_ref, rcol_ref, grad_ref,
    send_ref, res_ref, gate_ref, hid_ref,
):
    tokens, width = tok_ref.shape
    experts = router_ref.shape[1]
    slots_all = send_ref.shape[0]
    capacity = slots_all // experts
    att = ot_ref[0:HEADS].reshape(width, tokens)
    residual = tok_ref[...].astype(f32) + tn(att, wo_ref[...])
    res_ref[...] = residual
    hidden = (residual * inv_rms(residual) * gain_ref[...]).astype(bf16)
    hid_ref[...] = hidden
    logits = nn(hidden, router_ref[...])
    expert_lane = lax.broadcasted_iota(jnp.int32, (tokens, experts), 1)
    picked = [
        jnp.sum(jnp.where(expert_lane == rcol_ref[:, c : c + 1], logits, 0.0), axis=1, keepdims=True)
        for c in (0, 1)
    ]
    top = jnp.maximum(picked[0], picked[1])
    e0, e1 = jnp.exp(picked[0] - top), jnp.exp(picked[1] - top)
    gates = [e0 / (e0 + e1), e1 / (e0 + e1)]
    gate_ref[...] = jnp.concatenate(
        [jnp.broadcast_to(g, (tokens, 128)) for g in gates], axis=1
    )
    expert_row = lax.broadcasted_iota(jnp.int32, (experts, tokens), 0)
    before = (
        lax.broadcasted_iota(jnp.int32, (tokens, tokens), 0)
        < lax.broadcasted_iota(jnp.int32, (tokens, tokens), 1)
    ).astype(bf16)
    slot_row = lax.broadcasted_iota(jnp.int32, (slots_all, tokens), 0)
    hots = [(expert_row == rt_ref[c : c + 1, :]).astype(f32) for c in (0, 1)]
    counts = jnp.sum(hots[0], axis=1, keepdims=True)
    taken = [nn(hots[0].astype(bf16), before), nn(hots[1].astype(bf16), before) + counts]
    to_slot = []
    for c in (0, 1):
        slot = jnp.sum(hots[c] * taken[c], axis=0, keepdims=True).astype(jnp.int32)
        place = rt_ref[c : c + 1, :] * capacity + slot
        to_slot.append((slot_row == place).astype(bf16))
    send_ref[:, 0:width] = nn(to_slot[0] + to_slot[1], hidden).astype(bf16)
    upstream = grad_ref[...].astype(f32)
    weighted = jnp.concatenate([(g * upstream).astype(bf16) for g in gates], axis=0)
    send_ref[:, width:] = nn(jnp.concatenate(to_slot, axis=1), weighted).astype(bf16)


def combine_kernel(
    ret_ref, res_ref, grad_ref, gate_ref, hid_ref, rcol_ref, gain_ref, router_t_ref, wo_ref, ot_ref,
    layer_ref, rgrad_ref, gt_ref, wo_grad_ref, small_ref, weight_ref, sem,
):
    weight_copy = pltpu.make_async_copy(wo_ref, weight_ref, sem)
    weight_copy.start()
    tokens, width = res_ref.shape
    experts = router_t_ref.shape[0]
    slots_all = ret_ref.shape[0]
    capacity = slots_all // experts
    lane = lax.broadcasted_iota(jnp.int32, (tokens, 128), 1)
    earlier = (
        lax.broadcasted_iota(jnp.int32, (tokens, tokens), 1)
        < lax.broadcasted_iota(jnp.int32, (tokens, tokens), 0)
    ).astype(bf16)
    hots = [(lane == rcol_ref[:, c : c + 1]).astype(f32) for c in (0, 1)]
    counts = jnp.sum(hots[0], axis=0, keepdims=True)
    taken = [nn(earlier, hots[0].astype(bf16)), nn(earlier, hots[1].astype(bf16)) + counts]
    slot_lane = lax.broadcasted_iota(jnp.int32, (tokens, slots_all), 1)
    from_slot = []
    for c in (0, 1):
        slot = jnp.sum(hots[c] * taken[c], axis=1, keepdims=True).astype(jnp.int32)
        place = rcol_ref[:, c : c + 1] * capacity + slot
        from_slot.append((slot_lane == place).astype(bf16))
    outs = [nn(m, ret_ref[:, 0:width]) for m in from_slot]
    row_sum = nn(from_slot[0] + from_slot[1], ret_ref[:, width:])
    gates = [gate_ref[:, 0:1], gate_ref[:, 128:129]]
    residual = res_ref[...]
    layer_ref[...] = (residual + (gates[0] * outs[0] + gates[1] * outs[1])).astype(bf16)
    upstream = grad_ref[...].astype(f32)
    gate_grads = [jnp.sum(upstream * o, axis=1, keepdims=True) for o in outs]
    mixed = gates[0] * gate_grads[0] + gates[1] * gate_grads[1]
    logit_grad = (
        gates[0] * (gate_grads[0] - mixed) * hots[0] + gates[1] * (gate_grads[1] - mixed) * hots[1]
    )
    h2g = row_sum
    for e in range(experts):
        h2g = h2g + logit_grad[:, e : e + 1] * router_t_ref[e : e + 1, :]
    inverse = inv_rms(residual)
    normed = residual * inverse
    logit_t = logit_grad.T
    high = logit_t.astype(bf16)
    rest = (logit_t - high.astype(f32)).astype(bf16)
    router_grad = nn(high, hid_ref[...]) + nn(rest, hid_ref[...])
    small_ref[0:8, :] = jnp.broadcast_to(jnp.sum(h2g * normed, axis=0, keepdims=True), (8, width))
    small_ref[8:16, :] = router_grad[0:experts]
    scaled = h2g * gain_ref[...]
    average = jnp.mean(scaled * normed, axis=-1, keepdims=True)
    residual_grad = upstream + inverse * (scaled - normed * average)
    rgrad_ref[...] = residual_grad
    branch = residual_grad.astype(bf16)
    weight_copy.wait()
    gt = nt(weight_ref[...], branch).astype(bf16)
    gt_ref[0:HEADS] = gt.reshape(HEADS, HEAD_DIM, tokens)
    gt_ref[HEADS:] = jnp.zeros((gt_ref.shape[0] - HEADS, HEAD_DIM, tokens), bf16)
    att = ot_ref[0:HEADS].reshape(width, tokens)
    wo_grad_ref[...] = nn(att, branch).astype(bf16)


def expert_kernel(rows_ref, up_ref, down_ref, ret_ref, pre_ref, act_ref, out_acc, row_acc):
    step = pl.program_id(0)
    width = up_ref.shape[0]
    rows = rows_ref[:, 0:width]
    grads = rows_ref[:, width:]
    up, down = up_ref[...], down_ref[...]
    x = nn(rows, up)
    c = 0.7978845608028654
    t = jnp.tanh(c * (x + 0.044715 * (x * x * x)))
    hidden = (0.5 * x * (1.0 + t)).astype(bf16)
    slope = 0.5 * (1.0 + t) + 0.5 * x * (1.0 - t * t) * (c * (1.0 + 3 * 0.044715 * (x * x)))
    pre = (nn(grads, down) * slope).astype(bf16)
    act_ref[...] = hidden
    pre_ref[...] = pre
    out_part, row_part = nt(hidden, down), nt(pre, up)

    @pl.when(step == 0)
    def _():
        out_acc[...] = out_part
        row_acc[...] = row_part

    @pl.when(step > 0)
    def _():
        out_acc[...] += out_part
        row_acc[...] += row_part

    @pl.when(step == pl.num_programs(0) - 1)
    def _():
        ret_ref[:, 0:width] = out_acc[...].astype(bf16)
        ret_ref[:, width:] = row_acc[...].astype(bf16)


def expert_grad_kernel(rows_ref, pre_ref, act_ref, out_ref, left_ref):
    step = pl.program_id(0)
    steps = pl.num_programs(0)
    width = out_ref.shape[0]

    @pl.when(step == 0)
    def _():
        left_ref[...] = rows_ref[:, 0:width].astype(f32).T.astype(bf16)

    @pl.when(step == steps // 2)
    def _():
        left_ref[...] = rows_ref[:, width:].astype(f32).T.astype(bf16)

    @pl.when(step < steps // 2)
    def _():
        out_ref[...] = nn(left_ref[...], pre_ref[...]).astype(bf16)

    @pl.when(step >= steps // 2)
    def _():
        out_ref[...] = nn(left_ref[...], act_ref[...]).astype(bf16)


def pack_kernel(flat_ref, hid_ref, wt_ref, gain_ref, wo_ref, small_ref, bias_ref, out_ref):
    width = hid_ref.shape[1]
    grad = nn(flat_ref[...], hid_ref[...])
    part = jnp.sum(grad * wt_ref[...].astype(f32), axis=0, keepdims=True) / gain_ref[...]
    out_ref[0:192, :] = grad.astype(bf16)
    wo = wo_ref[0].astype(f32)
    for c in range(1, wo_ref.shape[0]):
        wo = wo + wo_ref[c].astype(f32)
    out_ref[192:240, :] = wo.astype(bf16)
    bias = jnp.concatenate([bias_ref[...], jnp.zeros((8, width - 128), f32)], axis=1)
    row = lax.broadcasted_iota(jnp.int32, (8, width), 0)
    first = jnp.where(
        row == 0, jnp.broadcast_to(part, (8, width)), jnp.where(row == 1, small_ref[0:8, :], bias)
    )
    out_ref[240:256, :] = jnp.concatenate([first, small_ref[8:16, :]], axis=0).astype(bf16)


def tokens_kernel(recv_ref, tok_ref, gain_ref, rgrad_ref, wq_ref, wk_ref, wv_ref, out_ref):
    tokens, width = tok_ref.shape
    acc = None
    for weight_ref, at in ((wq_ref, 0), (wk_ref, HEAD_DIM), (wv_ref, 2 * HEAD_DIM)):
        grad = recv_ref[0:HEADS, at : at + HEAD_DIM, :].reshape(width, tokens)
        part = nn(weight_ref[...], grad)
        acc = part if acc is None else acc + part
    hidden_grad = acc.T
    x = tok_ref[...].astype(f32)
    inverse = inv_rms(x)
    normed = x * inverse
    scaled = hidden_grad * gain_ref[...]
    average = jnp.mean(scaled * normed, axis=-1, keepdims=True)
    out_ref[...] = rgrad_ref[...] + inverse * (scaled - normed * average)


def ring_rows(piece):
    rows, width = piece.shape
    shape = (4, 4, 16, width) if rows == 256 else (2, 4, 4, 16, width)
    return piece.reshape(shape)


def unpack_kernel(where_ref, sum_ref, *refs):
    pieces, (q_ref, k_ref, v_ref, wo_ref, gain_ref, router_ref, table_ref) = refs[:14], refs[14:21]
    up_ref, down_ref, all_ref, sems = refs[21:]
    step = pl.program_id(0)
    x, y, z, core = where_ref[0], where_ref[1], where_ref[2], where_ref[3]
    copies = []
    for k in range(2):
        part = pieces[7 * k : 7 * k + 7]
        moves = [(part[3 * half + j], all_ref.at[k, half, d]) for half in (0, 1) for j, d in enumerate((0, 1, 3))]
        moves += [(part[6].at[half], all_ref.at[k, half, 2]) for half in (0, 1)]
        for j, (source, place) in enumerate(moves):
            copies.append(pltpu.make_async_copy(source, place, sems.at[8 * k + j]))

    @pl.when(step == 0)
    def _():
        for copy in copies:
            copy.start()

    @pl.when(step < 3)
    def _():
        units = up_ref.shape[2]
        up_ref[:, 0, :] = sum_ref[:, 0:units].astype(f32)
        down_ref[:, 0, :] = sum_ref[:, units:].astype(f32)

    @pl.when(step == 0)
    def _():
        for copy in copies:
            copy.wait()

    def rows(c, group):
        exp, half = group // 2, group % 2
        dx, dy = (x - c % 4 + 4) % 4, (y - c // 4 + 4) % 4
        dz, other = (z - exp // 2 + 4) % 4, (core + exp % 2) % 2
        first, second = (dy, dx) if half == 0 else (dx, dy)
        return all_ref[other, half, first, second, dz]

    def span(c, start, stop):
        return jnp.concatenate([rows(c, g) for g in range(start // 16, stop // 16)], axis=0)

    for ref, at in ((q_ref, 0), (k_ref, HEAD_DIM), (v_ref, 2 * HEAD_DIM)):
        both = [span(2 * step, at, at + HEAD_DIM), span(2 * step + 1, at, at + HEAD_DIM)]
        ref[...] = jnp.concatenate(both, axis=0).astype(f32).T
    @pl.when(step < 4)
    def _():
        for k in range(4):
            wo_ref[48 * k : 48 * k + 48, :] = span(4 * step + k, 192, 240).astype(f32)

    @pl.when(step == 0)
    def _():
        tails = [rows(c, 15).astype(f32) for c in range(16)]
        total = tails[0]
        for part in tails[1:]:
            total = total + part
        gain_ref[...] = total[0:8]
        router_ref[...] = jnp.concatenate([total, total], axis=0).T[:, 8:16]
        table = jnp.concatenate(
            [part[2:3, 0:128] for part in tails[:HEADS]] + [jnp.zeros((128 - HEADS, 128), f32)], axis=0
        )
        table_ref[...] = table.T[0 : table_ref.shape[0], 0:HEADS]


def ring(axis, stride, size, block, distance):
    def to(i):
        place = (i // stride) % 4
        return i + ((place + distance) % 4 - place) * stride

    return lax.ppermute(block, axis, [(i, to(i)) for i in range(size)])


def gather_ring(axis, stride, size, block):
    half = block.shape[0] // 2
    ahead = ring(axis, stride, size, block, 1)
    behind = ring(axis, stride, size, block, -1)
    far_one = ring(axis, stride, size, ahead[:half], 1)
    far_two = ring(axis, stride, size, behind[half:], -1)
    return [block, ahead, far_one, far_two, behind]


def gather_near(axis, stride, size, block):
    return [block] + [ring(axis, stride, size, block, d) for d in (1, 2, 3)]


def split_kernel(*refs):
    pieces, outs = refs[:4], refs[4:]
    for half, out in enumerate(outs):
        for d, ref in enumerate(pieces):
            block = ref[...]
            out[16 * d : 16 * d + 16, :] = block[16 * half : 16 * half + 16]


def join_kernel(*refs):
    for k in range(2):
        for d, ref in enumerate(refs[4 * k : 4 * k + 4]):
            size = ref.shape[0]
            refs[8 + k][d * size : (d + 1) * size, :] = ref[...]


def gather_near_all(share, n_ctx, n_exp):
    width = share.shape[1]
    along_z = gather_near("exp", 2, n_exp, share)
    quarter = sds((64, width), bf16)
    first, second = call(split_kernel, 8, (quarter, quarter))(*along_z)
    plane = gather_near("ctx", 1, n_ctx, first) + gather_near("ctx", 4, n_ctx, second)
    side = sds((256, width), bf16)
    return call(join_kernel, 8, (side, side))(*plane)


def far_kernel(*refs):
    size = refs[0].shape[0]
    for k, ref in enumerate(refs[:4]):
        refs[4][k * size : (k + 1) * size, :] = ref[...]


def gather_far(first, second, n_ctx, n_exp, done):
    a = gather_ring("ctx", 4, n_ctx, first)
    b = gather_ring("ctx", 1, n_ctx, second)
    far = call(far_kernel, 8, sds((2 * first.shape[0], first.shape[1]), bf16))(a[2], a[3], b[2], b[3])
    own = [a[0], a[1], a[4], b[0], b[1], b[4], far]
    own[0], own[3], done = lax.optimization_barrier((own[0], own[3], done))
    pairs = [(i, i ^ 1) for i in range(n_exp)]
    return own + [lax.ppermute(piece, "exp", pairs) for piece in own], done


def on_device(
    tokens, segment_ids, buckets, routes, attention_gain, query_weight, key_weight, value_weight,
    output_weight, bias_table, expert_gain, router_weight, expert_up, expert_down, out_grad,
):
    n_ctx, n_exp = lax.axis_size("ctx"), lax.axis_size("exp")
    rows, width = tokens.shape[1:]
    length = buckets.shape[0]
    experts = router_weight.shape[1]
    capacity = 5 * rows // (2 * experts)
    slots = experts * capacity
    hidden_units = expert_up.shape[2]
    head = lax.axis_index("ctx")
    gain_one = attention_gain.reshape(1, width)
    gain_two = expert_gain.reshape(1, width)
    bucket_row = buckets.reshape(1, length)
    table = jnp.pad(bias_table, ((0, 0), (0, n_ctx - HEADS)))
    tab = lax.dynamic_slice_in_dim(table, head, 1, axis=1)

    up_down = jnp.concatenate([expert_up[:, 0], expert_down[:, 0]], axis=1)
    weights = lax.all_gather(up_down, "ctx", axis=0, tiled=True)

    x = tokens[0]
    qkv, hidden = call(
        project_kernel,
        60,
        (sds((n_ctx, 2 * QA + HEAD_DIM, rows), bf16), sds((rows, width), bf16)),
        flops=6 * rows * width * width,
        moved=4 * MB,
    )(x, gain_one, segment_ids, query_weight, key_weight, value_weight)
    qkv = lax.all_to_all(qkv, "ctx", split_axis=0, concat_axis=0, tiled=True)
    at = jnp.minimum(head, HEADS - 1) * HEAD_DIM
    own_weights = jnp.concatenate(
        [
            lax.dynamic_slice_in_dim(w, at, HEAD_DIM, axis=1).T
            for w in (query_weight, key_weight, value_weight)
        ],
        axis=0,
    )
    qkv, own_weights = lax.optimization_barrier((qkv, own_weights))
    hidden_all = lax.all_gather(hidden, "ctx", axis=0, tiled=True)

    tiles = length // TQ
    ot, otf, lse = call(
        attend_kernel,
        60,
        (
            sds((n_ctx, HEAD_DIM, rows), bf16),
            sds((tiles, HEAD_DIM, TQ), f32),
            sds((tiles, 1, TQ), f32),
        ),
        scratch_shapes=[
            pltpu.VMEM((tiles // 2, 2 * TQ, QA), bf16),
            pltpu.VMEM((tiles + 1, TQ, TQ), f32),
        ],
        flops=8 * 10**9,
        moved=10 * MB,
    )(qkv, bucket_row, tab)
    ot = lax.all_to_all(ot, "ctx", split_axis=0, concat_axis=0, tiled=True)

    routed = routes[0]
    grads_in = out_grad[0]
    send, residual, gates, hidden_two = call(
        route_kernel,
        60,
        (
            sds((slots, 2 * width), bf16),
            sds((rows, width), f32),
            sds((rows, 256), f32),
            sds((rows, width), bf16),
        ),
        flops=10**9,
        moved=4 * MB,
    )(ot, x, output_weight, gain_two, router_weight, routed.T, routed, grads_in)
    received = lax.all_to_all(send, "exp", split_axis=0, concat_axis=0, tiled=True)

    chunk = 512
    steps = hidden_units // chunk
    whole = lambda shape: pl.BlockSpec(shape, lambda i: (0, 0))
    result, pre, act = call(
        expert_kernel,
        60,
        (
            sds((slots, 2 * width), bf16),
            sds((slots, hidden_units), bf16),
            sds((slots, hidden_units), bf16),
        ),
        grid=(steps,),
        in_specs=[
            whole((slots, 2 * width)),
            pl.BlockSpec((width, chunk), lambda i: (0, i)),
            pl.BlockSpec((width, chunk), lambda i: (0, steps + i)),
        ],
        out_specs=[
            whole((slots, 2 * width)),
            pl.BlockSpec((slots, chunk), lambda i: (0, i)),
            pl.BlockSpec((slots, chunk), lambda i: (0, i)),
        ],
        scratch_shapes=[pltpu.VMEM((slots, width), f32), pltpu.VMEM((slots, width), f32)],
        flops=8 * slots * width * hidden_units,
        moved=16 * MB,
    )(received, weights, weights)
    returned = lax.all_to_all(result, "exp", split_axis=0, concat_axis=0, tiled=True)
    weight_grads = call(
        expert_grad_kernel,
        60,
        sds((width, 2 * hidden_units), bf16),
        grid=(2 * steps,),
        in_specs=[
            whole((slots, 2 * width)),
            pl.BlockSpec((slots, chunk), lambda i: (0, jnp.minimum(i, steps - 1))),
            pl.BlockSpec((slots, chunk), lambda i: (0, jnp.maximum(i - steps, 0))),
        ],
        out_specs=pl.BlockSpec((width, chunk), lambda i: (0, i)),
        scratch_shapes=[pltpu.VMEM((width, slots), bf16)],
        flops=4 * slots * width * hidden_units,
        moved=16 * MB,
    )(received, pre, act)
    returned, weight_grads = lax.optimization_barrier((returned, weight_grads))

    layer_out, residual_grad, gt, wo_grad, small = call(
        combine_kernel,
        60,
        (
            sds((rows, width), bf16),
            sds((rows, width), f32),
            sds((n_ctx, HEAD_DIM, rows), bf16),
            sds((width, width), bf16),
            sds((16, width), f32),
        ),
        in_specs=[pl.BlockSpec(memory_space=pltpu.VMEM)] * 8
        + [pl.BlockSpec(memory_space=pl.ANY), pl.BlockSpec(memory_space=pltpu.VMEM)],
        scratch_shapes=[pltpu.VMEM((width, width), bf16), pltpu.SemaphoreType.DMA(())],
        flops=10**9,
        moved=6 * MB,
    )(
        returned, residual, grads_in, gates, hidden_two, routed, gain_two,
        router_weight.astype(f32).T, output_weight, ot,
    )
    gt = lax.all_to_all(gt, "ctx", split_axis=0, concat_axis=0, tiled=True)
    weight_grads, hidden_all, gt = lax.optimization_barrier((weight_grads, hidden_all, gt))
    summed = lax.psum_scatter(weight_grads, "ctx", scatter_dimension=0, tiled=True)
    wo_parts = lax.all_to_all(
        wo_grad.reshape(n_ctx, width // n_ctx, width), "ctx", split_axis=0, concat_axis=0, tiled=True
    )

    dqkv, flat, bias_grad = call(
        attend_back_kernel,
        60,
        (
            sds((n_ctx, 3 * HEAD_DIM, rows), bf16),
            sds((3 * HEAD_DIM, length), bf16),
            sds((8, 128), f32),
        ),
        scratch_shapes=[
            pltpu.VMEM((tiles // 2, 2 * TQ, QA), bf16),
            pltpu.VMEM((tiles // 2, 2 * TQ, HEAD_DIM), bf16),
            pltpu.VMEM((tiles + 1, TQ, TQ), f32),
            pltpu.VMEM((tiles + 1, TQ, TQ), f32),
            pltpu.VMEM((tiles // 2, HEAD_DIM, 2 * TQ), f32),
            pltpu.VMEM((tiles // 2, HEAD_DIM, 2 * TQ), f32),
        ],
        flops=20 * 10**9,
        moved=20 * MB,
    )(qkv, gt, otf, lse, bucket_row, tab)

    packed = call(
        pack_kernel,
        60,
        sds((ROWS, width), bf16),
        flops=6 * length * width * HEAD_DIM,
        moved=6 * MB,
    )(flat, hidden_all, own_weights, gain_one, wo_parts, small, bias_grad)
    parts = lax.all_to_all(
        packed.reshape(n_exp, ROWS // n_exp, width), "exp", split_axis=0, concat_axis=0, tiled=True
    )
    parts, dqkv = lax.optimization_barrier((parts, dqkv))
    back = lax.all_to_all(dqkv, "ctx", split_axis=0, concat_axis=0, tiled=True)
    share = jnp.sum(parts.astype(f32), axis=0).astype(bf16)
    first, second = gather_near_all(share, n_ctx, n_exp)
    first, second, back = lax.optimization_barrier((first, second, back))
    tokens_grad = call(
        tokens_kernel,
        60,
        sds((rows, width), f32),
        flops=6 * rows * width * width,
        moved=6 * MB,
    )(back, x, gain_one, residual_grad, query_weight, key_weight, value_weight)
    everything, tokens_grad = gather_far(first, second, n_ctx, n_exp, tokens_grad)

    full = sds((width, width), f32)
    column = pl.BlockSpec((width, 128), lambda i, w: (0, i))
    exp = lax.axis_index("exp")
    where = jnp.stack([head % 4, head // 4, exp // 2, exp % 2]).astype(jnp.int32)
    own_rows = sds((summed.shape[0], 1, hidden_units), f32)
    own_block = pl.BlockSpec((16, 1, hidden_units), lambda i, w: (jnp.minimum(i, 2), 0, 0))
    once = lambda shape: pl.BlockSpec(shape, lambda i, w: (0, 0))
    query_grad, key_grad, value_grad, output_grad, gains, router_grad, table_grad, ups, downs = call(
        unpack_kernel,
        60,
        (
            full,
            full,
            full,
            full,
            sds((8, width), f32),
            sds(router_weight.shape, f32),
            sds(bias_table.shape, f32),
            own_rows,
            own_rows,
        ),
        grid_spec=pltpu.PrefetchScalarGridSpec(
            num_scalar_prefetch=1,
            grid=(HEADS // 2,),
            in_specs=[pl.BlockSpec((16, 2 * hidden_units), lambda i, w: (jnp.minimum(i, 2), 0))]
            + [pl.BlockSpec(memory_space=pl.ANY) for _ in everything],
            out_specs=[
                column,
                column,
                column,
                pl.BlockSpec((192, width), lambda i, w: (jnp.minimum(i, 3), 0)),
                once((8, width)),
                once(router_weight.shape),
                once(bias_table.shape),
                own_block,
                own_block,
            ],
            scratch_shapes=[
                pltpu.VMEM((2, 2, 4, 4, 4, 16, width), bf16),
                pltpu.SemaphoreType.DMA((16,)),
            ],
        ),
        moved=16 * MB,
    )(where, summed, *[ring_rows(piece) for piece in everything])
    return (
        layer_out[None],
        tokens_grad[None],
        gains[0],
        query_grad,
        key_grad,
        value_grad,
        output_grad,
        table_grad,
        gains[1],
        router_grad,
        ups,
        downs,
    )


def solution(mesh):
    placed = (
        P("exp", "ctx", None),
        P("exp", "ctx"),
        P(),
        P("exp", "ctx", None),
        P(),
        P(),
        P(),
        P(),
        P(),
        P(),
        P(),
        P(),
        P("ctx", "exp", None),
        P("ctx", "exp", None),
        P("exp", "ctx", None),
    )
    return jax.shard_map(
        on_device,
        mesh=mesh,
        in_specs=placed,
        out_specs=(
            P("exp", "ctx", None),
            P("exp", "ctx", None),
            P(),
            P(),
            P(),
            P(),
            P(),
            P(),
            P(),
            P(),
            P("ctx", "exp", None),
            P("ctx", "exp", None),
        ),
        check_vma=False,
    )
```

```python
import jax
import jax.numpy as jnp
from jax import lax
from jax.experimental import pallas as pl
from jax.experimental.pallas import tpu as pltpu
from jax.sharding import PartitionSpec as P

HEADS = 12
HEAD_DIM = 64
EPS = 1e-06
NEG = -1e30
BIG = 2.0**99
SCALE = HEAD_DIM ** (-0.5)
AUG = 16
ROWS = 256
f32 = jnp.float32
bf16 = jnp.bfloat16
MB = 1024 * 1024


def nn(a, b):
    return lax.dot_general(a, b, (((1,), (0,)), ((), ())), preferred_element_type=f32)


def nt(a, b):
    return lax.dot_general(a, b, (((1,), (1,)), ((), ())), preferred_element_type=f32)


def tn(a, b):
    return lax.dot_general(a, b, (((0,), (0,)), ((), ())), preferred_element_type=f32)


def call(kernel, vmem, out_shape, flops=0, moved=0, **kw):
    return pl.pallas_call(
        kernel,
        out_shape=out_shape,
        compiler_params=pltpu.CompilerParams(vmem_limit_bytes=vmem * MB),
        cost_estimate=pl.CostEstimate(flops=flops, bytes_accessed=moved, transcendentals=0),
        **kw,
    )


def sds(shape, dtype):
    return jax.ShapeDtypeStruct(shape, dtype)


def inv_rms(value):
    return lax.rsqrt(jnp.mean(value * value, axis=-1, keepdims=True) + EPS)


def project_kernel(tok_ref, gain_ref, seg_ref, wq_ref, wk_ref, wv_ref, out_ref, hid_ref):
    x = tok_ref[...].astype(f32)
    hidden = (x * inv_rms(x) * gain_ref[...]).astype(bf16)
    hid_ref[...] = hidden
    tokens = x.shape[0]
    heads = out_ref.shape[0]

    def put(weight_ref, at, factor):
        t = (nn(hidden, weight_ref[...]).astype(bf16).astype(f32) * factor).T.astype(bf16)
        out_ref[0:HEADS, at : at + HEAD_DIM, :] = t.reshape(HEADS, HEAD_DIM, tokens)
        out_ref[HEADS:, at : at + HEAD_DIM, :] = jnp.zeros((heads - HEADS, HEAD_DIM, tokens), bf16)

    put(wq_ref, 0, SCALE)
    put(wk_ref, HEAD_DIM + AUG, 1.0)
    put(wv_ref, 2 * (HEAD_DIM + AUG), 1.0)
    s = jnp.broadcast_to(seg_ref[...].astype(f32), (AUG, tokens))
    row = lax.broadcasted_iota(jnp.int32, (AUG, tokens), 0)
    q_rows = jnp.where(row == 0, s * BIG, jnp.where(row == 1, (1.0 - s) * BIG, 0.0)).astype(bf16)
    k_rows = jnp.where(
        row == 0, s - 1.0, jnp.where(row == 1, -s, jnp.where(row < 5, 1.0, 0.0))
    ).astype(bf16)
    full = (heads, AUG, tokens)
    out_ref[:, HEAD_DIM : HEAD_DIM + AUG, :] = jnp.broadcast_to(q_rows[None], full)
    out_ref[:, 2 * HEAD_DIM + AUG : 2 * (HEAD_DIM + AUG), :] = jnp.broadcast_to(k_rows[None], full)


QA = HEAD_DIM + AUG
TQ = 256


def bias_tiles(bucket_ref, tab_ref, tile_ref):
    length = bucket_ref.shape[1]
    buckets = bucket_ref[...]
    nb = tab_ref.shape[0]
    hot = jnp.broadcast_to(buckets, (nb, length)) == lax.broadcasted_iota(
        jnp.int32, (nb, length), 0
    )
    b = jnp.sum(jnp.where(hot, tab_ref[...], 0.0), axis=0, keepdims=True)
    w = jnp.concatenate([jnp.full((1, TQ), NEG, f32), b], axis=1)
    x = jnp.broadcast_to(w, (8, length + TQ))
    row = lax.broadcasted_iota(jnp.int32, x.shape, 0)
    for bit in (1, 2, 4):
        x = jnp.where((row & bit) > 0, pltpu.roll(x, bit, axis=1), x)
    for bit in (8, 16, 32, 64):
        x = jnp.concatenate([x, pltpu.roll(x, bit, axis=1)], axis=0)
    tiles = length // TQ
    for d in range(tiles):
        at = (d + 1) * TQ
        tile_ref[tiles - 1 - d, 0:128, :] = x[:, at : at + TQ]
        tile_ref[tiles - 1 - d, 128:256, :] = x[:, at - 128 : at - 128 + TQ]
    tile_ref[tiles] = jnp.full((TQ, TQ), NEG, f32)


def transposed(block):
    return block.astype(f32).T.astype(bf16)


def pair(ref, index, at, size, count=2):
    return jnp.concatenate(
        [ref[count * index + k, at : at + size, :] for k in range(count)], axis=1
    )


def boundary(recv_ref):
    ones = recv_ref[:, QA + HEAD_DIM : QA + HEAD_DIM + AUG, :].astype(f32)
    row = lax.broadcasted_iota(jnp.int32, ones.shape, 1)
    total = jnp.sum(jnp.where(row == 1, ones, 0.0))
    return recv_ref.shape[0] * recv_ref.shape[2] + total.astype(jnp.int32)


def first_chunk(qb, edge):
    return jnp.where(qb * TQ >= edge, edge // (2 * TQ), 0)


def attend_kernel(recv_ref, bucket_ref, tab_ref, ot_ref, otf_ref, lse_ref, kn_ref, tile_ref):
    blocks = recv_ref.shape[0]
    bias_tiles(bucket_ref, tab_ref, tile_ref)
    for c in range(blocks):
        kn_ref[c // 4, (c % 4) * 128 : (c % 4) * 128 + 128, :] = transposed(
            recv_ref[c, QA : 2 * QA, :]
        )
    edge = boundary(recv_ref)
    last = blocks // 2 - 1

    def one_query_tile(qb, carry):
        qt = pair(recv_ref, qb, 0, QA)

        def one_key_tile(i, state):
            top, total, acc = state
            kc = qb // 2 - i
            bias = tile_ref[pl.ds(last - qb + 2 * kc, 2)].reshape(2 * TQ, TQ)
            s = nn(kn_ref[kc], qt) + bias
            new_top = jnp.maximum(top, jnp.max(s, axis=0, keepdims=True))
            p = jnp.exp(s - new_top)
            factor = jnp.exp(top - new_top)
            total = total * factor + jnp.sum(p, axis=0, keepdims=True)
            acc = acc * factor + nn(pair(recv_ref, kc, 2 * QA, HEAD_DIM, 4), p.astype(bf16))
            return new_top, total, acc

        start = (jnp.full((1, TQ), NEG, f32), jnp.zeros((1, TQ), f32), jnp.zeros((HEAD_DIM, TQ), f32))
        turns = qb // 2 - first_chunk(qb, edge) + 1
        top, total, acc = lax.fori_loop(0, turns, one_key_tile, start)
        o = acc / total
        otf_ref[qb] = o
        lse_ref[qb] = top + jnp.log(total)
        low = o.astype(bf16)
        ot_ref[2 * qb] = low[:, :128]
        ot_ref[2 * qb + 1] = low[:, 128:]
        return carry

    lax.fori_loop(0, blocks // 2, one_query_tile, 0)


def attend_back_kernel(
    recv_ref, gt_ref, otf_ref, lse_ref, bucket_ref, tab_ref,
    out_ref, flat_ref, bias_ref,
    kn_ref, vn_ref, tile_ref, dtile_ref, dk_ref, dv_ref,
):
    blocks = recv_ref.shape[0]
    tiles = blocks // 2
    bias_tiles(bucket_ref, tab_ref, tile_ref)
    for c in range(blocks):
        at = (c % 4) * 128
        kn_ref[c // 4, at : at + 128, :] = transposed(recv_ref[c, QA : 2 * QA, :])
        vn_ref[c // 4, at : at + 128, :] = transposed(recv_ref[c, 2 * QA : 2 * QA + HEAD_DIM, :])
    edge = boundary(recv_ref)
    dtile_ref[...] = jnp.zeros_like(dtile_ref)
    dk_ref[...] = jnp.zeros_like(dk_ref)
    dv_ref[...] = jnp.zeros_like(dv_ref)

    def one_query_tile(qb, carry):
        qt = pair(recv_ref, qb, 0, QA)
        gt = pair(gt_ref, qb, 0, HEAD_DIM)
        lse = lse_ref[qb]
        delta = jnp.sum(gt.astype(f32) * otf_ref[qb], axis=0, keepdims=True)

        def one_key_tile(i, acc):
            kc = qb // 2 - i
            place = pl.ds(tiles - 1 - qb + 2 * kc, 2)
            p = jnp.exp(nn(kn_ref[kc], qt) + tile_ref[place].reshape(2 * TQ, TQ) - lse)
            dp = nn(vn_ref[kc], gt)
            ds = (p * (dp - delta)).astype(bf16)
            dtile_ref[place] += ds.astype(f32).reshape(2, TQ, TQ)
            dv_ref[kc] += nt(gt, p.astype(bf16))
            dk_ref[kc] += nt(qt[:HEAD_DIM], ds)
            return acc + nn(pair(recv_ref, kc, QA, HEAD_DIM, 4), ds)

        acc = lax.fori_loop(
            0, qb // 2 - first_chunk(qb, edge) + 1, one_key_tile, jnp.zeros((HEAD_DIM, TQ), f32)
        )
        low = (acc * SCALE).astype(bf16)
        out_ref[2 * qb, 0:HEAD_DIM, :] = low[:, :128]
        out_ref[2 * qb + 1, 0:HEAD_DIM, :] = low[:, 128:]
        return carry

    lax.fori_loop(0, tiles, one_query_tile, 0)
    for c in range(blocks):
        for ref, at in ((dk_ref, HEAD_DIM), (dv_ref, 2 * HEAD_DIM)):
            lanes = slice((c % 4) * 128, (c % 4) * 128 + 128)
            out_ref[c, at : at + HEAD_DIM, :] = ref[c // 4, :, lanes].astype(bf16)
    for c in range(blocks):
        flat_ref[:, c * 128 : (c + 1) * 128] = out_ref[c]
    upper = jnp.concatenate([dtile_ref[tiles - 1 - d, 0:128, :] for d in range(tiles)], axis=1)
    lower = jnp.concatenate([dtile_ref[tiles - 1 - d, 128:256, :] for d in range(tiles)], axis=1)
    pad = jnp.zeros((128, 128), f32)
    x = jnp.concatenate([pad, pad, upper], axis=1) + jnp.concatenate([pad, lower, pad], axis=1)
    wide = x.shape[1]
    for half in (64, 32, 16, 8, 4, 2, 1):
        x = x[0:half] + pltpu.roll(x[half : 2 * half], wide - half, axis=1)
    g = x[:, TQ:]
    nb, length = tab_ref.shape[0], bucket_ref.shape[1]
    hot = jnp.broadcast_to(bucket_ref[...], (nb, length)) == lax.broadcasted_iota(
        jnp.int32, (nb, length), 0
    )
    sums = jnp.sum(jnp.where(hot, jnp.broadcast_to(g, (nb, length)), 0.0), axis=1, keepdims=True)
    column = jnp.concatenate([jnp.broadcast_to(sums, (nb, 128)), jnp.zeros((128 - nb, 128), f32)], axis=0)
    bias_ref[...] = column.T[0:8, :]


def route_kernel(
    ot_ref, tok_ref, wo_ref, gain_ref, router_ref, rt_ref, rcol_ref, grad_ref,
    send_ref, res_ref, gate_ref, hid_ref,
):
    tokens, width = tok_ref.shape
    experts = router_ref.shape[1]
    slots_all = send_ref.shape[0]
    capacity = slots_all // experts
    att = ot_ref[0:HEADS].reshape(width, tokens)
    residual = tok_ref[...].astype(f32) + tn(att, wo_ref[...])
    res_ref[...] = residual
    hidden = (residual * inv_rms(residual) * gain_ref[...]).astype(bf16)
    hid_ref[...] = hidden
    logits = nn(hidden, router_ref[...])
    expert_lane = lax.broadcasted_iota(jnp.int32, (tokens, experts), 1)
    picked = [
        jnp.sum(jnp.where(expert_lane == rcol_ref[:, c : c + 1], logits, 0.0), axis=1, keepdims=True)
        for c in (0, 1)
    ]
    top = jnp.maximum(picked[0], picked[1])
    e0, e1 = jnp.exp(picked[0] - top), jnp.exp(picked[1] - top)
    gates = [e0 / (e0 + e1), e1 / (e0 + e1)]
    gate_ref[...] = jnp.concatenate(
        [jnp.broadcast_to(g, (tokens, 128)) for g in gates], axis=1
    )
    expert_row = lax.broadcasted_iota(jnp.int32, (experts, tokens), 0)
    before = (
        lax.broadcasted_iota(jnp.int32, (tokens, tokens), 0)
        < lax.broadcasted_iota(jnp.int32, (tokens, tokens), 1)
    ).astype(bf16)
    slot_row = lax.broadcasted_iota(jnp.int32, (slots_all, tokens), 0)
    hots = [(expert_row == rt_ref[c : c + 1, :]).astype(f32) for c in (0, 1)]
    counts = jnp.sum(hots[0], axis=1, keepdims=True)
    taken = [nn(hots[0].astype(bf16), before), nn(hots[1].astype(bf16), before) + counts]
    to_slot = []
    for c in (0, 1):
        slot = jnp.sum(hots[c] * taken[c], axis=0, keepdims=True).astype(jnp.int32)
        place = rt_ref[c : c + 1, :] * capacity + slot
        to_slot.append((slot_row == place).astype(bf16))
    send_ref[:, 0:width] = nn(to_slot[0] + to_slot[1], hidden).astype(bf16)
    upstream = grad_ref[...].astype(f32)
    weighted = jnp.concatenate([(g * upstream).astype(bf16) for g in gates], axis=0)
    send_ref[:, width:] = nn(jnp.concatenate(to_slot, axis=1), weighted).astype(bf16)


def combine_kernel(
    ret_ref, res_ref, grad_ref, gate_ref, hid_ref, rcol_ref, gain_ref, router_t_ref, wo_ref, ot_ref,
    layer_ref, rgrad_ref, gt_ref, wo_grad_ref, small_ref, weight_ref, sem,
):
    weight_copy = pltpu.make_async_copy(wo_ref, weight_ref, sem)
    weight_copy.start()
    tokens, width = res_ref.shape
    experts = router_t_ref.shape[0]
    slots_all = ret_ref.shape[0]
    capacity = slots_all // experts
    lane = lax.broadcasted_iota(jnp.int32, (tokens, 128), 1)
    earlier = (
        lax.broadcasted_iota(jnp.int32, (tokens, tokens), 1)
        < lax.broadcasted_iota(jnp.int32, (tokens, tokens), 0)
    ).astype(bf16)
    hots = [(lane == rcol_ref[:, c : c + 1]).astype(f32) for c in (0, 1)]
    counts = jnp.sum(hots[0], axis=0, keepdims=True)
    taken = [nn(earlier, hots[0].astype(bf16)), nn(earlier, hots[1].astype(bf16)) + counts]
    slot_lane = lax.broadcasted_iota(jnp.int32, (tokens, slots_all), 1)
    from_slot = []
    for c in (0, 1):
        slot = jnp.sum(hots[c] * taken[c], axis=1, keepdims=True).astype(jnp.int32)
        place = rcol_ref[:, c : c + 1] * capacity + slot
        from_slot.append((slot_lane == place).astype(bf16))
    outs = [nn(m, ret_ref[:, 0:width]) for m in from_slot]
    row_sum = nn(from_slot[0] + from_slot[1], ret_ref[:, width:])
    gates = [gate_ref[:, 0:1], gate_ref[:, 128:129]]
    residual = res_ref[...]
    layer_ref[...] = (residual + (gates[0] * outs[0] + gates[1] * outs[1])).astype(bf16)
    upstream = grad_ref[...].astype(f32)
    gate_grads = [jnp.sum(upstream * o, axis=1, keepdims=True) for o in outs]
    mixed = gates[0] * gate_grads[0] + gates[1] * gate_grads[1]
    logit_grad = (
        gates[0] * (gate_grads[0] - mixed) * hots[0] + gates[1] * (gate_grads[1] - mixed) * hots[1]
    )
    h2g = row_sum
    for e in range(experts):
        h2g = h2g + logit_grad[:, e : e + 1] * router_t_ref[e : e + 1, :]
    inverse = inv_rms(residual)
    normed = residual * inverse
    logit_t = logit_grad.T
    high = logit_t.astype(bf16)
    rest = (logit_t - high.astype(f32)).astype(bf16)
    router_grad = nn(high, hid_ref[...]) + nn(rest, hid_ref[...])
    small_ref[0:8, :] = jnp.broadcast_to(jnp.sum(h2g * normed, axis=0, keepdims=True), (8, width))
    small_ref[8:16, :] = router_grad[0:experts]
    scaled = h2g * gain_ref[...]
    average = jnp.mean(scaled * normed, axis=-1, keepdims=True)
    residual_grad = upstream + inverse * (scaled - normed * average)
    rgrad_ref[...] = residual_grad
    branch = residual_grad.astype(bf16)
    weight_copy.wait()
    gt = nt(weight_ref[...], branch).astype(bf16)
    gt_ref[0:HEADS] = gt.reshape(HEADS, HEAD_DIM, tokens)
    gt_ref[HEADS:] = jnp.zeros((gt_ref.shape[0] - HEADS, HEAD_DIM, tokens), bf16)
    att = ot_ref[0:HEADS].reshape(width, tokens)
    wo_grad_ref[...] = nn(att, branch).astype(bf16)


def expert_kernel(rows_ref, up_ref, down_ref, ret_ref, pre_ref, act_ref, out_acc, row_acc):
    step = pl.program_id(0)
    width = up_ref.shape[0]
    rows = rows_ref[:, 0:width]
    grads = rows_ref[:, width:]
    up, down = up_ref[...], down_ref[...]
    x = nn(rows, up)
    c = 0.7978845608028654
    t = jnp.tanh(c * (x + 0.044715 * (x * x * x)))
    hidden = (0.5 * x * (1.0 + t)).astype(bf16)
    slope = 0.5 * (1.0 + t) + 0.5 * x * (1.0 - t * t) * (c * (1.0 + 3 * 0.044715 * (x * x)))
    pre = (nn(grads, down) * slope).astype(bf16)
    act_ref[...] = hidden
    pre_ref[...] = pre
    out_part, row_part = nt(hidden, down), nt(pre, up)

    @pl.when(step == 0)
    def _():
        out_acc[...] = out_part
        row_acc[...] = row_part

    @pl.when(step > 0)
    def _():
        out_acc[...] += out_part
        row_acc[...] += row_part

    @pl.when(step == pl.num_programs(0) - 1)
    def _():
        ret_ref[:, 0:width] = out_acc[...].astype(bf16)
        ret_ref[:, width:] = row_acc[...].astype(bf16)


def expert_grad_kernel(rows_ref, pre_ref, act_ref, out_ref, left_ref):
    step = pl.program_id(0)
    steps = pl.num_programs(0)
    width = out_ref.shape[0]

    @pl.when(step == 0)
    def _():
        left_ref[...] = rows_ref[:, 0:width].astype(f32).T.astype(bf16)

    @pl.when(step == steps // 2)
    def _():
        left_ref[...] = rows_ref[:, width:].astype(f32).T.astype(bf16)

    @pl.when(step < steps // 2)
    def _():
        out_ref[...] = nn(left_ref[...], pre_ref[...]).astype(bf16)

    @pl.when(step >= steps // 2)
    def _():
        out_ref[...] = nn(left_ref[...], act_ref[...]).astype(bf16)


def pack_kernel(flat_ref, hid_ref, wt_ref, gain_ref, wo_ref, small_ref, bias_ref, out_ref):
    width = hid_ref.shape[1]
    grad = nn(flat_ref[...], hid_ref[...])
    part = jnp.sum(grad * wt_ref[...].astype(f32), axis=0, keepdims=True) / gain_ref[...]
    out_ref[0:192, :] = grad.astype(bf16)
    wo = wo_ref[0].astype(f32)
    for c in range(1, wo_ref.shape[0]):
        wo = wo + wo_ref[c].astype(f32)
    out_ref[192:240, :] = wo.astype(bf16)
    bias = jnp.concatenate([bias_ref[...], jnp.zeros((8, width - 128), f32)], axis=1)
    row = lax.broadcasted_iota(jnp.int32, (8, width), 0)
    first = jnp.where(
        row == 0, jnp.broadcast_to(part, (8, width)), jnp.where(row == 1, small_ref[0:8, :], bias)
    )
    out_ref[240:256, :] = jnp.concatenate([first, small_ref[8:16, :]], axis=0).astype(bf16)


def tokens_kernel(recv_ref, tok_ref, gain_ref, rgrad_ref, wq_ref, wk_ref, wv_ref, out_ref):
    tokens, width = tok_ref.shape
    acc = None
    for weight_ref, at in ((wq_ref, 0), (wk_ref, HEAD_DIM), (wv_ref, 2 * HEAD_DIM)):
        grad = recv_ref[0:HEADS, at : at + HEAD_DIM, :].reshape(width, tokens)
        part = nn(weight_ref[...], grad)
        acc = part if acc is None else acc + part
    hidden_grad = acc.T
    x = tok_ref[...].astype(f32)
    inverse = inv_rms(x)
    normed = x * inverse
    scaled = hidden_grad * gain_ref[...]
    average = jnp.mean(scaled * normed, axis=-1, keepdims=True)
    out_ref[...] = rgrad_ref[...] + inverse * (scaled - normed * average)


def ring_rows(piece):
    rows, width = piece.shape
    shape = (4, 4, 16, width) if rows == 256 else (2, 4, 4, 16, width)
    return piece.reshape(shape)


def widen_kernel(in_ref, up_ref, down_ref):
    units = up_ref.shape[2]
    up_ref[:, 0, :] = in_ref[:, 0:units].astype(f32)
    down_ref[:, 0, :] = in_ref[:, units:].astype(f32)


def unpack_kernel(where_ref, *refs):
    pieces, (q_ref, k_ref, v_ref, wo_ref, gain_one_ref, gain_two_ref) = refs[:14], refs[14:20]
    router_ref, table_ref, all_ref, sems = refs[20:]
    step = pl.program_id(0)
    x, y, z, core = where_ref[0], where_ref[1], where_ref[2], where_ref[3]
    copies = []
    for k in range(2):
        part = pieces[7 * k : 7 * k + 7]
        moves = [(part[3 * half + j], all_ref.at[k, half, d]) for half in (0, 1) for j, d in enumerate((0, 1, 3))]
        moves += [(part[6].at[half], all_ref.at[k, half, 2]) for half in (0, 1)]
        for j, (source, place) in enumerate(moves):
            copies.append(pltpu.make_async_copy(source, place, sems.at[8 * k + j]))

    @pl.when(step == 0)
    def _():
        for copy in copies:
            copy.start()

    @pl.when(step == 0)
    def _():
        for copy in copies:
            copy.wait()

    def rows(c, group):
        exp, half = group // 2, group % 2
        dx, dy = (x - c % 4 + 4) % 4, (y - c // 4 + 4) % 4
        dz, other = (z - exp // 2 + 4) % 4, (core + exp % 2) % 2
        first, second = (dy, dx) if half == 0 else (dx, dy)
        return all_ref[other, half, first, second, dz]

    def span(c, start, stop):
        return jnp.concatenate([rows(c, g) for g in range(start // 16, stop // 16)], axis=0)

    for ref, at in ((q_ref, 0), (k_ref, HEAD_DIM), (v_ref, 2 * HEAD_DIM)):
        both = [span(2 * step, at, at + HEAD_DIM), span(2 * step + 1, at, at + HEAD_DIM)]
        ref[...] = jnp.concatenate(both, axis=0).astype(f32).T
    @pl.when(step < 4)
    def _():
        for k in range(4):
            wo_ref[48 * k : 48 * k + 48, :] = span(4 * step + k, 192, 240).astype(f32)

    @pl.when(step == 0)
    def _():
        tails = [rows(c, 15).astype(f32) for c in range(16)]
        total = tails[0]
        for part in tails[1:]:
            total = total + part
        gain_one_ref[...] = total[0:1]
        gain_two_ref[...] = total[1:2]
        router_ref[...] = total[8:16]
        table_ref[...] = jnp.concatenate(
            [part[2:3, 0 : table_ref.shape[1]] for part in tails[:HEADS]], axis=0
        )


def ring(axis, stride, size, block, distance):
    def to(i):
        place = (i // stride) % 4
        return i + ((place + distance) % 4 - place) * stride

    return lax.ppermute(block, axis, [(i, to(i)) for i in range(size)])


def gather_ring(axis, stride, size, block):
    half = block.shape[0] // 2
    ahead = ring(axis, stride, size, block, 1)
    behind = ring(axis, stride, size, block, -1)
    far_one = ring(axis, stride, size, ahead[:half], 1)
    far_two = ring(axis, stride, size, behind[half:], -1)
    return [block, ahead, far_one, far_two, behind]


def gather_near(axis, stride, size, block):
    return [block] + [ring(axis, stride, size, block, d) for d in (1, 2, 3)]


def split_kernel(*refs):
    pieces, outs = refs[:4], refs[4:]
    for half, out in enumerate(outs):
        for d, ref in enumerate(pieces):
            block = ref[...]
            out[16 * d : 16 * d + 16, :] = block[16 * half : 16 * half + 16]


def join_kernel(*refs):
    for k in range(2):
        for d, ref in enumerate(refs[4 * k : 4 * k + 4]):
            size = ref.shape[0]
            refs[8 + k][d * size : (d + 1) * size, :] = ref[...]


def gather_near_all(share, n_ctx, n_exp):
    width = share.shape[1]
    along_z = gather_near("exp", 2, n_exp, share)
    quarter = sds((64, width), bf16)
    first, second = call(split_kernel, 8, (quarter, quarter))(*along_z)
    plane = gather_near("ctx", 1, n_ctx, first) + gather_near("ctx", 4, n_ctx, second)
    side = sds((256, width), bf16)
    return call(join_kernel, 8, (side, side))(*plane)


def far_kernel(*refs):
    size = refs[0].shape[0]
    for k, ref in enumerate(refs[:4]):
        refs[4][k * size : (k + 1) * size, :] = ref[...]


def gather_far(first, second, n_ctx, n_exp):
    a = gather_ring("ctx", 4, n_ctx, first)
    b = gather_ring("ctx", 1, n_ctx, second)
    far = call(far_kernel, 8, sds((2 * first.shape[0], first.shape[1]), bf16))(a[2], a[3], b[2], b[3])
    own = [a[0], a[1], a[4], b[0], b[1], b[4], far]
    pairs = [(i, i ^ 1) for i in range(n_exp)]
    return own + [lax.ppermute(piece, "exp", pairs) for piece in own]


def on_device(
    tokens, segment_ids, buckets, routes, attention_gain, query_weight, key_weight, value_weight,
    output_weight, bias_table, expert_gain, router_weight, expert_up, expert_down, out_grad,
):
    n_ctx, n_exp = lax.axis_size("ctx"), lax.axis_size("exp")
    rows, width = tokens.shape[1:]
    length = buckets.shape[0]
    experts = router_weight.shape[1]
    capacity = 5 * rows // (2 * experts)
    slots = experts * capacity
    hidden_units = expert_up.shape[2]
    head = lax.axis_index("ctx")
    gain_one = attention_gain.reshape(1, width)
    gain_two = expert_gain.reshape(1, width)
    bucket_row = buckets.reshape(1, length)
    table = jnp.pad(bias_table, ((0, 0), (0, n_ctx - HEADS)))
    tab = lax.dynamic_slice_in_dim(table, head, 1, axis=1)

    up_down = jnp.concatenate([expert_up[:, 0], expert_down[:, 0]], axis=1)
    weights = lax.all_gather(up_down, "ctx", axis=0, tiled=True)

    x = tokens[0]
    qkv, hidden = call(
        project_kernel,
        60,
        (sds((n_ctx, 2 * QA + HEAD_DIM, rows), bf16), sds((rows, width), bf16)),
        flops=6 * rows * width * width,
        moved=4 * MB,
    )(x, gain_one, segment_ids, query_weight, key_weight, value_weight)
    qkv = lax.all_to_all(qkv, "ctx", split_axis=0, concat_axis=0, tiled=True)
    at = jnp.minimum(head, HEADS - 1) * HEAD_DIM
    own_weights = jnp.concatenate(
        [
            lax.dynamic_slice_in_dim(w, at, HEAD_DIM, axis=1).T
            for w in (query_weight, key_weight, value_weight)
        ],
        axis=0,
    )
    qkv, own_weights = lax.optimization_barrier((qkv, own_weights))
    hidden_all = lax.all_gather(hidden, "ctx", axis=0, tiled=True)

    tiles = length // TQ
    ot, otf, lse = call(
        attend_kernel,
        60,
        (
            sds((n_ctx, HEAD_DIM, rows), bf16),
            sds((tiles, HEAD_DIM, TQ), f32),
            sds((tiles, 1, TQ), f32),
        ),
        scratch_shapes=[
            pltpu.VMEM((tiles // 2, 2 * TQ, QA), bf16),
            pltpu.VMEM((tiles + 1, TQ, TQ), f32),
        ],
        flops=8 * 10**9,
        moved=10 * MB,
    )(qkv, bucket_row, tab)
    ot = lax.all_to_all(ot, "ctx", split_axis=0, concat_axis=0, tiled=True)

    routed = routes[0]
    grads_in = out_grad[0]
    send, residual, gates, hidden_two = call(
        route_kernel,
        60,
        (
            sds((slots, 2 * width), bf16),
            sds((rows, width), f32),
            sds((rows, 256), f32),
            sds((rows, width), bf16),
        ),
        flops=10**9,
        moved=4 * MB,
    )(ot, x, output_weight, gain_two, router_weight, routed.T, routed, grads_in)
    received = lax.all_to_all(send, "exp", split_axis=0, concat_axis=0, tiled=True)

    chunk = 512
    steps = hidden_units // chunk
    whole = lambda shape: pl.BlockSpec(shape, lambda i: (0, 0))
    result, pre, act = call(
        expert_kernel,
        60,
        (
            sds((slots, 2 * width), bf16),
            sds((slots, hidden_units), bf16),
            sds((slots, hidden_units), bf16),
        ),
        grid=(steps,),
        in_specs=[
            whole((slots, 2 * width)),
            pl.BlockSpec((width, chunk), lambda i: (0, i)),
            pl.BlockSpec((width, chunk), lambda i: (0, steps + i)),
        ],
        out_specs=[
            whole((slots, 2 * width)),
            pl.BlockSpec((slots, chunk), lambda i: (0, i)),
            pl.BlockSpec((slots, chunk), lambda i: (0, i)),
        ],
        scratch_shapes=[pltpu.VMEM((slots, width), f32), pltpu.VMEM((slots, width), f32)],
        flops=8 * slots * width * hidden_units,
        moved=16 * MB,
    )(received, weights, weights)
    returned = lax.all_to_all(result, "exp", split_axis=0, concat_axis=0, tiled=True)
    weight_grads = call(
        expert_grad_kernel,
        60,
        sds((width, 2 * hidden_units), bf16),
        grid=(2 * steps,),
        in_specs=[
            whole((slots, 2 * width)),
            pl.BlockSpec((slots, chunk), lambda i: (0, jnp.minimum(i, steps - 1))),
            pl.BlockSpec((slots, chunk), lambda i: (0, jnp.maximum(i - steps, 0))),
        ],
        out_specs=pl.BlockSpec((width, chunk), lambda i: (0, i)),
        scratch_shapes=[pltpu.VMEM((width, slots), bf16)],
        flops=4 * slots * width * hidden_units,
        moved=16 * MB,
    )(received, pre, act)
    returned, weight_grads = lax.optimization_barrier((returned, weight_grads))

    layer_out, residual_grad, gt, wo_grad, small = call(
        combine_kernel,
        60,
        (
            sds((rows, width), bf16),
            sds((rows, width), f32),
            sds((n_ctx, HEAD_DIM, rows), bf16),
            sds((width, width), bf16),
            sds((16, width), f32),
        ),
        in_specs=[pl.BlockSpec(memory_space=pltpu.VMEM)] * 8
        + [pl.BlockSpec(memory_space=pl.ANY), pl.BlockSpec(memory_space=pltpu.VMEM)],
        scratch_shapes=[pltpu.VMEM((width, width), bf16), pltpu.SemaphoreType.DMA(())],
        flops=10**9,
        moved=6 * MB,
    )(
        returned, residual, grads_in, gates, hidden_two, routed, gain_two,
        router_weight.astype(f32).T, output_weight, ot,
    )
    gt = lax.all_to_all(gt, "ctx", split_axis=0, concat_axis=0, tiled=True)
    weight_grads, hidden_all, gt = lax.optimization_barrier((weight_grads, hidden_all, gt))
    summed = lax.psum_scatter(weight_grads, "ctx", scatter_dimension=0, tiled=True)
    wo_parts = lax.all_to_all(
        wo_grad.reshape(n_ctx, width // n_ctx, width), "ctx", split_axis=0, concat_axis=0, tiled=True
    )

    dqkv, flat, bias_grad = call(
        attend_back_kernel,
        60,
        (
            sds((n_ctx, 3 * HEAD_DIM, rows), bf16),
            sds((3 * HEAD_DIM, length), bf16),
            sds((8, 128), f32),
        ),
        scratch_shapes=[
            pltpu.VMEM((tiles // 2, 2 * TQ, QA), bf16),
            pltpu.VMEM((tiles // 2, 2 * TQ, HEAD_DIM), bf16),
            pltpu.VMEM((tiles + 1, TQ, TQ), f32),
            pltpu.VMEM((tiles + 1, TQ, TQ), f32),
            pltpu.VMEM((tiles // 2, HEAD_DIM, 2 * TQ), f32),
            pltpu.VMEM((tiles // 2, HEAD_DIM, 2 * TQ), f32),
        ],
        flops=20 * 10**9,
        moved=20 * MB,
    )(qkv, gt, otf, lse, bucket_row, tab)

    packed = call(
        pack_kernel,
        60,
        sds((ROWS, width), bf16),
        flops=6 * length * width * HEAD_DIM,
        moved=6 * MB,
    )(flat, hidden_all, own_weights, gain_one, wo_parts, small, bias_grad)
    parts = lax.all_to_all(
        packed.reshape(n_exp, ROWS // n_exp, width), "exp", split_axis=0, concat_axis=0, tiled=True
    )
    share = jnp.sum(parts.astype(f32), axis=0).astype(bf16)
    first, second = gather_near_all(share, n_ctx, n_exp)
    first, second, dqkv = lax.optimization_barrier((first, second, dqkv))
    back = lax.all_to_all(dqkv, "ctx", split_axis=0, concat_axis=0, tiled=True)
    everything = gather_far(first, second, n_ctx, n_exp)

    full = sds((width, width), f32)
    column = pl.BlockSpec((width, 128), lambda i, w: (0, i))
    exp = lax.axis_index("exp")
    where = jnp.stack([head % 4, head // 4, exp // 2, exp % 2]).astype(jnp.int32)
    once = lambda shape: pl.BlockSpec(shape, lambda i, w: (0, 0))
    query_grad, key_grad, value_grad, output_grad, gain_a, gain_b, router_grad, table_grad = call(
        unpack_kernel,
        60,
        (
            full,
            full,
            full,
            full,
            sds((1, width), f32),
            sds((1, width), f32),
            sds((experts, width), f32),
            sds((HEADS, bias_table.shape[0]), f32),
        ),
        grid_spec=pltpu.PrefetchScalarGridSpec(
            num_scalar_prefetch=1,
            grid=(HEADS // 2,),
            in_specs=[pl.BlockSpec(memory_space=pl.ANY) for _ in everything],
            out_specs=[
                column,
                column,
                column,
                pl.BlockSpec((192, width), lambda i, w: (jnp.minimum(i, 3), 0)),
                once((1, width)),
                once((1, width)),
                once((experts, width)),
                once((HEADS, bias_table.shape[0])),
            ],
            scratch_shapes=[
                pltpu.VMEM((2, 2, 4, 4, 4, 16, width), bf16),
                pltpu.SemaphoreType.DMA((16,)),
            ],
        ),
        moved=16 * MB,
    )(where, *[ring_rows(piece) for piece in everything])
    back, output_grad = lax.optimization_barrier((back, output_grad))
    tokens_grad = call(
        tokens_kernel,
        60,
        sds((rows, width), f32),
        flops=6 * rows * width * width,
        moved=6 * MB,
    )(back, x, gain_one, residual_grad, query_weight, key_weight, value_weight)
    summed, tokens_grad = lax.optimization_barrier((summed, tokens_grad))
    own_rows = sds((summed.shape[0], 1, hidden_units), f32)
    ups, downs = call(
        widen_kernel,
        60,
        (own_rows, own_rows),
        grid=(summed.shape[0] // 16,),
        in_specs=[pl.BlockSpec((16, 2 * hidden_units), lambda i: (i, 0))],
        out_specs=[pl.BlockSpec((16, 1, hidden_units), lambda i: (i, 0, 0))] * 2,
        moved=2 * MB,
    )(summed)
    return (
        layer_out[None],
        tokens_grad[None],
        gain_a[0],
        query_grad,
        key_grad,
        value_grad,
        output_grad,
        table_grad.T,
        gain_b[0],
        router_grad.T,
        ups,
        downs,
    )


def solution(mesh):
    placed = (
        P("exp", "ctx", None),
        P("exp", "ctx"),
        P(),
        P("exp", "ctx", None),
        P(),
        P(),
        P(),
        P(),
        P(),
        P(),
        P(),
        P(),
        P("ctx", "exp", None),
        P("ctx", "exp", None),
        P("exp", "ctx", None),
    )
    return jax.shard_map(
        on_device,
        mesh=mesh,
        in_specs=placed,
        out_specs=(
            P("exp", "ctx", None),
            P("exp", "ctx", None),
            P(),
            P(),
            P(),
            P(),
            P(),
            P(),
            P(),
            P(),
            P("ctx", "exp", None),
            P("ctx", "exp", None),
        ),
        check_vma=False,
    )
```

```python
import jax
import jax.numpy as jnp
from jax import lax
from jax.experimental import pallas as pl
from jax.experimental.pallas import tpu as pltpu
from jax.sharding import PartitionSpec as P

HEADS = 12
HEAD_DIM = 64
EPS = 1e-06
NEG = -1e30
BIG = 2.0**99
SCALE = HEAD_DIM ** (-0.5)
AUG = 16
ROWS = 256
f32 = jnp.float32
bf16 = jnp.bfloat16
MB = 1024 * 1024


def nn(a, b):
    return lax.dot_general(a, b, (((1,), (0,)), ((), ())), preferred_element_type=f32)


def nt(a, b):
    return lax.dot_general(a, b, (((1,), (1,)), ((), ())), preferred_element_type=f32)


def tn(a, b):
    return lax.dot_general(a, b, (((0,), (0,)), ((), ())), preferred_element_type=f32)


def call(kernel, vmem, out_shape, flops=0, moved=0, **kw):
    return pl.pallas_call(
        kernel,
        out_shape=out_shape,
        compiler_params=pltpu.CompilerParams(vmem_limit_bytes=vmem * MB),
        cost_estimate=pl.CostEstimate(flops=flops, bytes_accessed=moved, transcendentals=0),
        **kw,
    )


def sds(shape, dtype):
    return jax.ShapeDtypeStruct(shape, dtype)


def inv_rms(value):
    return lax.rsqrt(jnp.mean(value * value, axis=-1, keepdims=True) + EPS)


def project_kernel(tok_ref, gain_ref, seg_ref, wq_ref, wk_ref, wv_ref, out_ref, hid_ref):
    x = tok_ref[...].astype(f32)
    hidden = (x * inv_rms(x) * gain_ref[...]).astype(bf16)
    hid_ref[...] = hidden
    tokens = x.shape[0]
    heads = out_ref.shape[0]

    def put(weight_ref, at, factor):
        t = (nn(hidden, weight_ref[...]).astype(bf16).astype(f32) * factor).T.astype(bf16)
        out_ref[0:HEADS, at : at + HEAD_DIM, :] = t.reshape(HEADS, HEAD_DIM, tokens)
        out_ref[HEADS:, at : at + HEAD_DIM, :] = jnp.zeros((heads - HEADS, HEAD_DIM, tokens), bf16)

    put(wq_ref, 0, SCALE)
    put(wk_ref, HEAD_DIM + AUG, 1.0)
    put(wv_ref, 2 * (HEAD_DIM + AUG), 1.0)
    s = jnp.broadcast_to(seg_ref[...].astype(f32), (AUG, tokens))
    row = lax.broadcasted_iota(jnp.int32, (AUG, tokens), 0)
    q_rows = jnp.where(row == 0, s * BIG, jnp.where(row == 1, (1.0 - s) * BIG, 0.0)).astype(bf16)
    k_rows = jnp.where(
        row == 0, s - 1.0, jnp.where(row == 1, -s, jnp.where(row < 5, 1.0, 0.0))
    ).astype(bf16)
    full = (heads, AUG, tokens)
    out_ref[:, HEAD_DIM : HEAD_DIM + AUG, :] = jnp.broadcast_to(q_rows[None], full)
    out_ref[:, 2 * HEAD_DIM + AUG : 2 * (HEAD_DIM + AUG), :] = jnp.broadcast_to(k_rows[None], full)


QA = HEAD_DIM + AUG
TQ = 256


def bias_tiles(bucket_ref, tab_ref, tile_ref):
    length = bucket_ref.shape[1]
    buckets = bucket_ref[...]
    nb = tab_ref.shape[0]
    hot = jnp.broadcast_to(buckets, (nb, length)) == lax.broadcasted_iota(
        jnp.int32, (nb, length), 0
    )
    b = jnp.sum(jnp.where(hot, tab_ref[...], 0.0), axis=0, keepdims=True)
    w = jnp.concatenate([jnp.full((1, TQ), NEG, f32), b], axis=1)
    x = jnp.broadcast_to(w, (8, length + TQ))
    row = lax.broadcasted_iota(jnp.int32, x.shape, 0)
    for bit in (1, 2, 4):
        x = jnp.where((row & bit) > 0, pltpu.roll(x, bit, axis=1), x)
    for bit in (8, 16, 32, 64):
        x = jnp.concatenate([x, pltpu.roll(x, bit, axis=1)], axis=0)
    tiles = length // TQ
    for d in range(tiles):
        at = (d + 1) * TQ
        tile_ref[tiles - 1 - d, 0:128, :] = x[:, at : at + TQ]
        tile_ref[tiles - 1 - d, 128:256, :] = x[:, at - 128 : at - 128 + TQ]
    tile_ref[tiles] = jnp.full((TQ, TQ), NEG, f32)


def transposed(block):
    return block.astype(f32).T.astype(bf16)


def pair(ref, index, at, size, count=2):
    return jnp.concatenate(
        [ref[count * index + k, at : at + size, :] for k in range(count)], axis=1
    )


def boundary(recv_ref):
    ones = recv_ref[:, QA + HEAD_DIM : QA + HEAD_DIM + AUG, :].astype(f32)
    row = lax.broadcasted_iota(jnp.int32, ones.shape, 1)
    total = jnp.sum(jnp.where(row == 1, ones, 0.0))
    return recv_ref.shape[0] * recv_ref.shape[2] + total.astype(jnp.int32)


def first_chunk(qb, edge):
    return jnp.where(qb * TQ >= edge, edge // (2 * TQ), 0)


def attend_kernel(recv_ref, bucket_ref, tab_ref, ot_ref, otf_ref, lse_ref, kn_ref, tile_ref):
    blocks = recv_ref.shape[0]
    bias_tiles(bucket_ref, tab_ref, tile_ref)
    for c in range(blocks):
        kn_ref[c // 4, (c % 4) * 128 : (c % 4) * 128 + 128, :] = transposed(
            recv_ref[c, QA : 2 * QA, :]
        )
    edge = boundary(recv_ref)
    last = blocks // 2 - 1

    def one_query_tile(qb, carry):
        qt = pair(recv_ref, qb, 0, QA)

        def one_key_tile(i, state):
            top, total, acc = state
            kc = qb // 2 - i
            bias = tile_ref[pl.ds(last - qb + 2 * kc, 2)].reshape(2 * TQ, TQ)
            s = nn(kn_ref[kc], qt) + bias
            new_top = jnp.maximum(top, jnp.max(s, axis=0, keepdims=True))
            p = jnp.exp(s - new_top)
            factor = jnp.exp(top - new_top)
            total = total * factor + jnp.sum(p, axis=0, keepdims=True)
            acc = acc * factor + nn(pair(recv_ref, kc, 2 * QA, HEAD_DIM, 4), p.astype(bf16))
            return new_top, total, acc

        start = (jnp.full((1, TQ), NEG, f32), jnp.zeros((1, TQ), f32), jnp.zeros((HEAD_DIM, TQ), f32))
        turns = qb // 2 - first_chunk(qb, edge) + 1
        top, total, acc = lax.fori_loop(0, turns, one_key_tile, start)
        o = acc / total
        otf_ref[qb] = o
        lse_ref[qb] = top + jnp.log(total)
        low = o.astype(bf16)
        ot_ref[2 * qb] = low[:, :128]
        ot_ref[2 * qb + 1] = low[:, 128:]
        return carry

    lax.fori_loop(0, blocks // 2, one_query_tile, 0)


def attend_back_kernel(
    recv_ref, gt_ref, otf_ref, lse_ref, bucket_ref, tab_ref,
    out_ref, flat_ref, bias_ref,
    kn_ref, vn_ref, tile_ref, dtile_ref, dk_ref, dv_ref,
):
    blocks = recv_ref.shape[0]
    tiles = blocks // 2
    bias_tiles(bucket_ref, tab_ref, tile_ref)
    for c in range(blocks):
        at = (c % 4) * 128
        kn_ref[c // 4, at : at + 128, :] = transposed(recv_ref[c, QA : 2 * QA, :])
        vn_ref[c // 4, at : at + 128, :] = transposed(recv_ref[c, 2 * QA : 2 * QA + HEAD_DIM, :])
    edge = boundary(recv_ref)
    dtile_ref[...] = jnp.zeros_like(dtile_ref)
    dk_ref[...] = jnp.zeros_like(dk_ref)
    dv_ref[...] = jnp.zeros_like(dv_ref)

    def one_query_tile(qb, carry):
        qt = pair(recv_ref, qb, 0, QA)
        gt = pair(gt_ref, qb, 0, HEAD_DIM)
        lse = lse_ref[qb]
        delta = jnp.sum(gt.astype(f32) * otf_ref[qb], axis=0, keepdims=True)

        def one_key_tile(i, acc):
            kc = qb // 2 - i
            place = pl.ds(tiles - 1 - qb + 2 * kc, 2)
            p = jnp.exp(nn(kn_ref[kc], qt) + tile_ref[place].reshape(2 * TQ, TQ) - lse)
            dp = nn(vn_ref[kc], gt)
            ds = (p * (dp - delta)).astype(bf16)
            dtile_ref[place] += ds.astype(f32).reshape(2, TQ, TQ)
            dv_ref[kc] += nt(gt, p.astype(bf16))
            dk_ref[kc] += nt(qt[:HEAD_DIM], ds)
            return acc + nn(pair(recv_ref, kc, QA, HEAD_DIM, 4), ds)

        acc = lax.fori_loop(
            0, qb // 2 - first_chunk(qb, edge) + 1, one_key_tile, jnp.zeros((HEAD_DIM, TQ), f32)
        )
        low = (acc * SCALE).astype(bf16)
        out_ref[2 * qb, 0:HEAD_DIM, :] = low[:, :128]
        out_ref[2 * qb + 1, 0:HEAD_DIM, :] = low[:, 128:]
        return carry

    lax.fori_loop(0, tiles, one_query_tile, 0)
    for c in range(blocks):
        for ref, at in ((dk_ref, HEAD_DIM), (dv_ref, 2 * HEAD_DIM)):
            lanes = slice((c % 4) * 128, (c % 4) * 128 + 128)
            out_ref[c, at : at + HEAD_DIM, :] = ref[c // 4, :, lanes].astype(bf16)
    for c in range(blocks):
        flat_ref[:, c * 128 : (c + 1) * 128] = out_ref[c]
    upper = jnp.concatenate([dtile_ref[tiles - 1 - d, 0:128, :] for d in range(tiles)], axis=1)
    lower = jnp.concatenate([dtile_ref[tiles - 1 - d, 128:256, :] for d in range(tiles)], axis=1)
    pad = jnp.zeros((128, 128), f32)
    x = jnp.concatenate([pad, pad, upper], axis=1) + jnp.concatenate([pad, lower, pad], axis=1)
    wide = x.shape[1]
    for half in (64, 32, 16, 8, 4, 2, 1):
        x = x[0:half] + pltpu.roll(x[half : 2 * half], wide - half, axis=1)
    g = x[:, TQ:]
    nb, length = tab_ref.shape[0], bucket_ref.shape[1]
    hot = jnp.broadcast_to(bucket_ref[...], (nb, length)) == lax.broadcasted_iota(
        jnp.int32, (nb, length), 0
    )
    sums = jnp.sum(jnp.where(hot, jnp.broadcast_to(g, (nb, length)), 0.0), axis=1, keepdims=True)
    column = jnp.concatenate([jnp.broadcast_to(sums, (nb, 128)), jnp.zeros((128 - nb, 128), f32)], axis=0)
    bias_ref[...] = column.T[0:8, :]


def route_kernel(
    ot_ref, tok_ref, wo_ref, gain_ref, router_ref, rt_ref, rcol_ref, grad_ref,
    send_ref, res_ref, gate_ref, hid_ref,
):
    tokens, width = tok_ref.shape
    experts = router_ref.shape[1]
    slots_all = send_ref.shape[0]
    capacity = slots_all // experts
    att = ot_ref[0:HEADS].reshape(width, tokens)
    residual = tok_ref[...].astype(f32) + tn(att, wo_ref[...])
    res_ref[...] = residual
    hidden = (residual * inv_rms(residual) * gain_ref[...]).astype(bf16)
    hid_ref[...] = hidden
    logits = nn(hidden, router_ref[...])
    expert_lane = lax.broadcasted_iota(jnp.int32, (tokens, experts), 1)
    picked = [
        jnp.sum(jnp.where(expert_lane == rcol_ref[:, c : c + 1], logits, 0.0), axis=1, keepdims=True)
        for c in (0, 1)
    ]
    top = jnp.maximum(picked[0], picked[1])
    e0, e1 = jnp.exp(picked[0] - top), jnp.exp(picked[1] - top)
    gates = [e0 / (e0 + e1), e1 / (e0 + e1)]
    gate_ref[...] = jnp.concatenate(
        [jnp.broadcast_to(g, (tokens, 128)) for g in gates], axis=1
    )
    expert_row = lax.broadcasted_iota(jnp.int32, (experts, tokens), 0)
    before = (
        lax.broadcasted_iota(jnp.int32, (tokens, tokens), 0)
        < lax.broadcasted_iota(jnp.int32, (tokens, tokens), 1)
    ).astype(bf16)
    slot_row = lax.broadcasted_iota(jnp.int32, (slots_all, tokens), 0)
    hots = [(expert_row == rt_ref[c : c + 1, :]).astype(f32) for c in (0, 1)]
    counts = jnp.sum(hots[0], axis=1, keepdims=True)
    taken = [nn(hots[0].astype(bf16), before), nn(hots[1].astype(bf16), before) + counts]
    to_slot = []
    for c in (0, 1):
        slot = jnp.sum(hots[c] * taken[c], axis=0, keepdims=True).astype(jnp.int32)
        place = rt_ref[c : c + 1, :] * capacity + slot
        to_slot.append((slot_row == place).astype(bf16))
    send_ref[:, 0:width] = nn(to_slot[0] + to_slot[1], hidden).astype(bf16)
    upstream = grad_ref[...].astype(f32)
    weighted = jnp.concatenate([(g * upstream).astype(bf16) for g in gates], axis=0)
    send_ref[:, width:] = nn(jnp.concatenate(to_slot, axis=1), weighted).astype(bf16)


def combine_kernel(
    ret_ref, res_ref, grad_ref, gate_ref, hid_ref, rcol_ref, gain_ref, router_t_ref, wo_ref, ot_ref,
    layer_ref, rgrad_ref, gt_ref, wo_grad_ref, small_ref, weight_ref, sem,
):
    weight_copy = pltpu.make_async_copy(wo_ref, weight_ref, sem)
    weight_copy.start()
    tokens, width = res_ref.shape
    experts = router_t_ref.shape[0]
    slots_all = ret_ref.shape[0]
    capacity = slots_all // experts
    lane = lax.broadcasted_iota(jnp.int32, (tokens, 128), 1)
    earlier = (
        lax.broadcasted_iota(jnp.int32, (tokens, tokens), 1)
        < lax.broadcasted_iota(jnp.int32, (tokens, tokens), 0)
    ).astype(bf16)
    hots = [(lane == rcol_ref[:, c : c + 1]).astype(f32) for c in (0, 1)]
    counts = jnp.sum(hots[0], axis=0, keepdims=True)
    taken = [nn(earlier, hots[0].astype(bf16)), nn(earlier, hots[1].astype(bf16)) + counts]
    slot_lane = lax.broadcasted_iota(jnp.int32, (tokens, slots_all), 1)
    from_slot = []
    for c in (0, 1):
        slot = jnp.sum(hots[c] * taken[c], axis=1, keepdims=True).astype(jnp.int32)
        place = rcol_ref[:, c : c + 1] * capacity + slot
        from_slot.append((slot_lane == place).astype(bf16))
    outs = [nn(m, ret_ref[:, 0:width]) for m in from_slot]
    row_sum = nn(from_slot[0] + from_slot[1], ret_ref[:, width:])
    gates = [gate_ref[:, 0:1], gate_ref[:, 128:129]]
    residual = res_ref[...]
    layer_ref[...] = (residual + (gates[0] * outs[0] + gates[1] * outs[1])).astype(bf16)
    upstream = grad_ref[...].astype(f32)
    gate_grads = [jnp.sum(upstream * o, axis=1, keepdims=True) for o in outs]
    mixed = gates[0] * gate_grads[0] + gates[1] * gate_grads[1]
    logit_grad = (
        gates[0] * (gate_grads[0] - mixed) * hots[0] + gates[1] * (gate_grads[1] - mixed) * hots[1]
    )
    h2g = row_sum
    for e in range(experts):
        h2g = h2g + logit_grad[:, e : e + 1] * router_t_ref[e : e + 1, :]
    inverse = inv_rms(residual)
    normed = residual * inverse
    logit_t = logit_grad.T
    high = logit_t.astype(bf16)
    rest = (logit_t - high.astype(f32)).astype(bf16)
    router_grad = nn(high, hid_ref[...]) + nn(rest, hid_ref[...])
    small_ref[0:8, :] = jnp.broadcast_to(jnp.sum(h2g * normed, axis=0, keepdims=True), (8, width))
    small_ref[8:16, :] = router_grad[0:experts]
    scaled = h2g * gain_ref[...]
    average = jnp.mean(scaled * normed, axis=-1, keepdims=True)
    residual_grad = upstream + inverse * (scaled - normed * average)
    rgrad_ref[...] = residual_grad
    branch = residual_grad.astype(bf16)
    weight_copy.wait()
    gt = nt(weight_ref[...], branch).astype(bf16)
    gt_ref[0:HEADS] = gt.reshape(HEADS, HEAD_DIM, tokens)
    gt_ref[HEADS:] = jnp.zeros((gt_ref.shape[0] - HEADS, HEAD_DIM, tokens), bf16)
    att = ot_ref[0:HEADS].reshape(width, tokens)
    wo_grad_ref[...] = nn(att, branch).astype(bf16)


def expert_kernel(rows_ref, up_ref, down_ref, ret_ref, pre_ref, act_ref, out_acc, row_acc):
    step = pl.program_id(0)
    width = up_ref.shape[0]
    rows = rows_ref[:, 0:width]
    grads = rows_ref[:, width:]
    up, down = up_ref[...], down_ref[...]
    x = nn(rows, up)
    c = 0.7978845608028654
    t = jnp.tanh(c * (x + 0.044715 * (x * x * x)))
    hidden = (0.5 * x * (1.0 + t)).astype(bf16)
    slope = 0.5 * (1.0 + t) + 0.5 * x * (1.0 - t * t) * (c * (1.0 + 3 * 0.044715 * (x * x)))
    pre = (nn(grads, down) * slope).astype(bf16)
    act_ref[...] = hidden
    pre_ref[...] = pre
    out_part, row_part = nt(hidden, down), nt(pre, up)

    @pl.when(step == 0)
    def _():
        out_acc[...] = out_part
        row_acc[...] = row_part

    @pl.when(step > 0)
    def _():
        out_acc[...] += out_part
        row_acc[...] += row_part

    @pl.when(step == pl.num_programs(0) - 1)
    def _():
        ret_ref[:, 0:width] = out_acc[...].astype(bf16)
        ret_ref[:, width:] = row_acc[...].astype(bf16)


def expert_grad_kernel(rows_ref, pre_ref, act_ref, out_ref, left_ref):
    step = pl.program_id(0)
    steps = pl.num_programs(0)
    width = out_ref.shape[0]

    @pl.when(step == 0)
    def _():
        left_ref[...] = rows_ref[:, 0:width].astype(f32).T.astype(bf16)

    @pl.when(step == steps // 2)
    def _():
        left_ref[...] = rows_ref[:, width:].astype(f32).T.astype(bf16)

    @pl.when(step < steps // 2)
    def _():
        out_ref[...] = nn(left_ref[...], pre_ref[...]).astype(bf16)

    @pl.when(step >= steps // 2)
    def _():
        out_ref[...] = nn(left_ref[...], act_ref[...]).astype(bf16)


def pack_kernel(flat_ref, hid_ref, wt_ref, gain_ref, wo_ref, small_ref, bias_ref, out_ref):
    width = hid_ref.shape[1]
    grad = nn(flat_ref[...], hid_ref[...])
    part = jnp.sum(grad * wt_ref[...].astype(f32), axis=0, keepdims=True) / gain_ref[...]
    out_ref[0:192, :] = grad.astype(bf16)
    wo = wo_ref[0].astype(f32)
    for c in range(1, wo_ref.shape[0]):
        wo = wo + wo_ref[c].astype(f32)
    out_ref[192:240, :] = wo.astype(bf16)
    bias = jnp.concatenate([bias_ref[...], jnp.zeros((8, width - 128), f32)], axis=1)
    row = lax.broadcasted_iota(jnp.int32, (8, width), 0)
    first = jnp.where(
        row == 0, jnp.broadcast_to(part, (8, width)), jnp.where(row == 1, small_ref[0:8, :], bias)
    )
    out_ref[240:256, :] = jnp.concatenate([first, small_ref[8:16, :]], axis=0).astype(bf16)


def tokens_kernel(
    recv_ref, tok_ref, gain_ref, rgrad_ref, wq_ref, wk_ref, wv_ref, sum_ref, out_ref, up_ref, down_ref
):
    units = up_ref.shape[2]
    up_ref[:, 0, :] = sum_ref[:, 0:units].astype(f32)
    down_ref[:, 0, :] = sum_ref[:, units:].astype(f32)
    tokens, width = tok_ref.shape
    acc = None
    for weight_ref, at in ((wq_ref, 0), (wk_ref, HEAD_DIM), (wv_ref, 2 * HEAD_DIM)):
        grad = recv_ref[0:HEADS, at : at + HEAD_DIM, :].reshape(width, tokens)
        part = nn(weight_ref[...], grad)
        acc = part if acc is None else acc + part
    hidden_grad = acc.T
    x = tok_ref[...].astype(f32)
    inverse = inv_rms(x)
    normed = x * inverse
    scaled = hidden_grad * gain_ref[...]
    average = jnp.mean(scaled * normed, axis=-1, keepdims=True)
    out_ref[...] = rgrad_ref[...] + inverse * (scaled - normed * average)


def ring_rows(piece):
    rows, width = piece.shape
    shape = (4, 4, 16, width) if rows == 256 else (2, 4, 4, 16, width)
    return piece.reshape(shape)


def unpack_kernel(where_ref, *refs):
    pieces, (q_ref, k_ref, v_ref, wo_ref, gain_ref) = refs[:14], refs[14:19]
    router_ref, table_ref, all_ref, sems = refs[19:]
    step = pl.program_id(0)
    x, y, z, core = where_ref[0], where_ref[1], where_ref[2], where_ref[3]
    copies = []
    for k in range(2):
        part = pieces[7 * k : 7 * k + 7]
        moves = [(part[3 * half + j], all_ref.at[k, half, d]) for half in (0, 1) for j, d in enumerate((0, 1, 3))]
        moves += [(part[6].at[half], all_ref.at[k, half, 2]) for half in (0, 1)]
        for j, (source, place) in enumerate(moves):
            copies.append(pltpu.make_async_copy(source, place, sems.at[8 * k + j]))

    @pl.when(step == 0)
    def _():
        for copy in copies:
            copy.start()

    @pl.when(step == 0)
    def _():
        for copy in copies:
            copy.wait()

    def rows(c, group):
        exp, half = group // 2, group % 2
        dx, dy = (x - c % 4 + 4) % 4, (y - c // 4 + 4) % 4
        dz, other = (z - exp // 2 + 4) % 4, (core + exp % 2) % 2
        first, second = (dy, dx) if half == 0 else (dx, dy)
        return all_ref[other, half, first, second, dz]

    def span(c, start, stop):
        return jnp.concatenate([rows(c, g) for g in range(start // 16, stop // 16)], axis=0)

    for ref, at in ((q_ref, 0), (k_ref, HEAD_DIM), (v_ref, 2 * HEAD_DIM)):
        both = [span(2 * step, at, at + HEAD_DIM), span(2 * step + 1, at, at + HEAD_DIM)]
        ref[...] = jnp.concatenate(both, axis=0).astype(f32).T
    @pl.when(step < 4)
    def _():
        for k in range(4):
            wo_ref[48 * k : 48 * k + 48, :] = span(4 * step + k, 192, 240).astype(f32)

    @pl.when(step == 0)
    def _():
        tails = [rows(c, 15).astype(f32) for c in range(16)]
        total = tails[0]
        for part in tails[1:]:
            total = total + part
        gain_ref[...] = total[0:8]
        router_ref[...] = total[8:16]
        table_ref[...] = jnp.concatenate(
            [part[2:3, 0 : table_ref.shape[1]] for part in tails[:HEADS]], axis=0
        )


def ring(axis, stride, size, block, distance):
    def to(i):
        place = (i // stride) % 4
        return i + ((place + distance) % 4 - place) * stride

    return lax.ppermute(block, axis, [(i, to(i)) for i in range(size)])


def gather_ring(axis, stride, size, block):
    half = block.shape[0] // 2
    ahead = ring(axis, stride, size, block, 1)
    behind = ring(axis, stride, size, block, -1)
    far_one = ring(axis, stride, size, ahead[:half], 1)
    far_two = ring(axis, stride, size, behind[half:], -1)
    return [block, ahead, far_one, far_two, behind]


def gather_near(axis, stride, size, block):
    return [block] + [ring(axis, stride, size, block, d) for d in (1, 2, 3)]


def split_kernel(*refs):
    pieces, outs = refs[:4], refs[4:]
    for half, out in enumerate(outs):
        for d, ref in enumerate(pieces):
            block = ref[...]
            out[16 * d : 16 * d + 16, :] = block[16 * half : 16 * half + 16]


def join_kernel(*refs):
    for k in range(2):
        for d, ref in enumerate(refs[4 * k : 4 * k + 4]):
            size = ref.shape[0]
            refs[8 + k][d * size : (d + 1) * size, :] = ref[...]


def gather_near_all(share, n_ctx, n_exp):
    width = share.shape[1]
    along_z = gather_near("exp", 2, n_exp, share)
    quarter = sds((64, width), bf16)
    first, second = call(split_kernel, 8, (quarter, quarter))(*along_z)
    plane = gather_near("ctx", 1, n_ctx, first) + gather_near("ctx", 4, n_ctx, second)
    side = sds((256, width), bf16)
    return call(join_kernel, 8, (side, side))(*plane)


def far_kernel(*refs):
    size = refs[0].shape[0]
    for k, ref in enumerate(refs[:4]):
        refs[4][k * size : (k + 1) * size, :] = ref[...]


def gather_far(first, second, n_ctx, n_exp):
    a = gather_ring("ctx", 4, n_ctx, first)
    b = gather_ring("ctx", 1, n_ctx, second)
    far = call(far_kernel, 8, sds((2 * first.shape[0], first.shape[1]), bf16))(a[2], a[3], b[2], b[3])
    own = [a[0], a[1], a[4], b[0], b[1], b[4], far]
    pairs = [(i, i ^ 1) for i in range(n_exp)]
    return own + [lax.ppermute(piece, "exp", pairs) for piece in own]


def on_device(
    tokens, segment_ids, buckets, routes, attention_gain, query_weight, key_weight, value_weight,
    output_weight, bias_table, expert_gain, router_weight, expert_up, expert_down, out_grad,
):
    n_ctx, n_exp = lax.axis_size("ctx"), lax.axis_size("exp")
    rows, width = tokens.shape[1:]
    length = buckets.shape[0]
    experts = router_weight.shape[1]
    capacity = 5 * rows // (2 * experts)
    slots = experts * capacity
    hidden_units = expert_up.shape[2]
    head = lax.axis_index("ctx")
    gain_one = attention_gain.reshape(1, width)
    gain_two = expert_gain.reshape(1, width)
    bucket_row = buckets.reshape(1, length)
    table = jnp.pad(bias_table, ((0, 0), (0, n_ctx - HEADS)))
    tab = lax.dynamic_slice_in_dim(table, head, 1, axis=1)

    up_down = jnp.concatenate([expert_up[:, 0], expert_down[:, 0]], axis=1)
    weights = lax.all_gather(up_down, "ctx", axis=0, tiled=True)

    x = tokens[0]
    qkv, hidden = call(
        project_kernel,
        60,
        (sds((n_ctx, 2 * QA + HEAD_DIM, rows), bf16), sds((rows, width), bf16)),
        flops=6 * rows * width * width,
        moved=4 * MB,
    )(x, gain_one, segment_ids, query_weight, key_weight, value_weight)
    qkv = lax.all_to_all(qkv, "ctx", split_axis=0, concat_axis=0, tiled=True)
    at = jnp.minimum(head, HEADS - 1) * HEAD_DIM
    own_weights = jnp.concatenate(
        [
            lax.dynamic_slice_in_dim(w, at, HEAD_DIM, axis=1).T
            for w in (query_weight, key_weight, value_weight)
        ],
        axis=0,
    )
    qkv, own_weights = lax.optimization_barrier((qkv, own_weights))
    hidden_all = lax.all_gather(hidden, "ctx", axis=0, tiled=True)

    tiles = length // TQ
    ot, otf, lse = call(
        attend_kernel,
        60,
        (
            sds((n_ctx, HEAD_DIM, rows), bf16),
            sds((tiles, HEAD_DIM, TQ), f32),
            sds((tiles, 1, TQ), f32),
        ),
        scratch_shapes=[
            pltpu.VMEM((tiles // 2, 2 * TQ, QA), bf16),
            pltpu.VMEM((tiles + 1, TQ, TQ), f32),
        ],
        flops=8 * 10**9,
        moved=10 * MB,
    )(qkv, bucket_row, tab)
    ot = lax.all_to_all(ot, "ctx", split_axis=0, concat_axis=0, tiled=True)

    routed = routes[0]
    grads_in = out_grad[0]
    send, residual, gates, hidden_two = call(
        route_kernel,
        60,
        (
            sds((slots, 2 * width), bf16),
            sds((rows, width), f32),
            sds((rows, 256), f32),
            sds((rows, width), bf16),
        ),
        flops=10**9,
        moved=4 * MB,
    )(ot, x, output_weight, gain_two, router_weight, routed.T, routed, grads_in)
    received = lax.all_to_all(send, "exp", split_axis=0, concat_axis=0, tiled=True)

    chunk = 512
    steps = hidden_units // chunk
    whole = lambda shape: pl.BlockSpec(shape, lambda i: (0, 0))
    result, pre, act = call(
        expert_kernel,
        60,
        (
            sds((slots, 2 * width), bf16),
            sds((slots, hidden_units), bf16),
            sds((slots, hidden_units), bf16),
        ),
        grid=(steps,),
        in_specs=[
            whole((slots, 2 * width)),
            pl.BlockSpec((width, chunk), lambda i: (0, i)),
            pl.BlockSpec((width, chunk), lambda i: (0, steps + i)),
        ],
        out_specs=[
            whole((slots, 2 * width)),
            pl.BlockSpec((slots, chunk), lambda i: (0, i)),
            pl.BlockSpec((slots, chunk), lambda i: (0, i)),
        ],
        scratch_shapes=[pltpu.VMEM((slots, width), f32), pltpu.VMEM((slots, width), f32)],
        flops=8 * slots * width * hidden_units,
        moved=16 * MB,
    )(received, weights, weights)
    returned = lax.all_to_all(result, "exp", split_axis=0, concat_axis=0, tiled=True)
    weight_grads = call(
        expert_grad_kernel,
        60,
        sds((width, 2 * hidden_units), bf16),
        grid=(2 * steps,),
        in_specs=[
            whole((slots, 2 * width)),
            pl.BlockSpec((slots, chunk), lambda i: (0, jnp.minimum(i, steps - 1))),
            pl.BlockSpec((slots, chunk), lambda i: (0, jnp.maximum(i - steps, 0))),
        ],
        out_specs=pl.BlockSpec((width, chunk), lambda i: (0, i)),
        scratch_shapes=[pltpu.VMEM((width, slots), bf16)],
        flops=4 * slots * width * hidden_units,
        moved=16 * MB,
    )(received, pre, act)
    returned, weight_grads = lax.optimization_barrier((returned, weight_grads))

    layer_out, residual_grad, gt, wo_grad, small = call(
        combine_kernel,
        60,
        (
            sds((rows, width), bf16),
            sds((rows, width), f32),
            sds((n_ctx, HEAD_DIM, rows), bf16),
            sds((width, width), bf16),
            sds((16, width), f32),
        ),
        in_specs=[pl.BlockSpec(memory_space=pltpu.VMEM)] * 8
        + [pl.BlockSpec(memory_space=pl.ANY), pl.BlockSpec(memory_space=pltpu.VMEM)],
        scratch_shapes=[pltpu.VMEM((width, width), bf16), pltpu.SemaphoreType.DMA(())],
        flops=10**9,
        moved=6 * MB,
    )(
        returned, residual, grads_in, gates, hidden_two, routed, gain_two,
        router_weight.astype(f32).T, output_weight, ot,
    )
    gt = lax.all_to_all(gt, "ctx", split_axis=0, concat_axis=0, tiled=True)
    weight_grads, hidden_all, gt = lax.optimization_barrier((weight_grads, hidden_all, gt))
    summed = lax.psum_scatter(weight_grads, "ctx", scatter_dimension=0, tiled=True)
    wo_parts = lax.all_to_all(
        wo_grad.reshape(n_ctx, width // n_ctx, width), "ctx", split_axis=0, concat_axis=0, tiled=True
    )

    dqkv, flat, bias_grad = call(
        attend_back_kernel,
        60,
        (
            sds((n_ctx, 3 * HEAD_DIM, rows), bf16),
            sds((3 * HEAD_DIM, length), bf16),
            sds((8, 128), f32),
        ),
        scratch_shapes=[
            pltpu.VMEM((tiles // 2, 2 * TQ, QA), bf16),
            pltpu.VMEM((tiles // 2, 2 * TQ, HEAD_DIM), bf16),
            pltpu.VMEM((tiles + 1, TQ, TQ), f32),
            pltpu.VMEM((tiles + 1, TQ, TQ), f32),
            pltpu.VMEM((tiles // 2, HEAD_DIM, 2 * TQ), f32),
            pltpu.VMEM((tiles // 2, HEAD_DIM, 2 * TQ), f32),
        ],
        flops=20 * 10**9,
        moved=20 * MB,
    )(qkv, gt, otf, lse, bucket_row, tab)

    packed = call(
        pack_kernel,
        60,
        sds((ROWS, width), bf16),
        flops=6 * length * width * HEAD_DIM,
        moved=6 * MB,
    )(flat, hidden_all, own_weights, gain_one, wo_parts, small, bias_grad)
    parts = lax.all_to_all(
        packed.reshape(n_exp, ROWS // n_exp, width), "exp", split_axis=0, concat_axis=0, tiled=True
    )
    share = jnp.sum(parts.astype(f32), axis=0).astype(bf16)
    first, second = gather_near_all(share, n_ctx, n_exp)
    first, second, dqkv = lax.optimization_barrier((first, second, dqkv))
    back = lax.all_to_all(dqkv, "ctx", split_axis=0, concat_axis=0, tiled=True)
    everything = gather_far(first, second, n_ctx, n_exp)

    full = sds((width, width), f32)
    column = pl.BlockSpec((width, 128), lambda i, w: (0, i))
    exp = lax.axis_index("exp")
    where = jnp.stack([head % 4, head // 4, exp // 2, exp % 2]).astype(jnp.int32)
    once = lambda shape: pl.BlockSpec(shape, lambda i, w: (0, 0))
    query_grad, key_grad, value_grad, output_grad, gains, router_grad, table_grad = call(
        unpack_kernel,
        60,
        (
            full,
            full,
            full,
            full,
            sds((8, width), f32),
            sds((experts, width), f32),
            sds((HEADS, bias_table.shape[0]), f32),
        ),
        grid_spec=pltpu.PrefetchScalarGridSpec(
            num_scalar_prefetch=1,
            grid=(HEADS // 2,),
            in_specs=[pl.BlockSpec(memory_space=pl.ANY) for _ in everything],
            out_specs=[
                column,
                column,
                column,
                pl.BlockSpec((192, width), lambda i, w: (jnp.minimum(i, 3), 0)),
                once((8, width)),
                once((experts, width)),
                once((HEADS, bias_table.shape[0])),
            ],
            scratch_shapes=[
                pltpu.VMEM((2, 2, 4, 4, 4, 16, width), bf16),
                pltpu.SemaphoreType.DMA((16,)),
            ],
        ),
        moved=16 * MB,
    )(where, *[ring_rows(piece) for piece in everything])
    back, output_grad = lax.optimization_barrier((back, output_grad))
    own_rows = sds((summed.shape[0], 1, hidden_units), f32)
    tokens_grad, ups, downs = call(
        tokens_kernel,
        60,
        (sds((rows, width), f32), own_rows, own_rows),
        flops=6 * rows * width * width,
        moved=8 * MB,
    )(back, x, gain_one, residual_grad, query_weight, key_weight, value_weight, summed)
    return (
        layer_out[None],
        tokens_grad[None],
        gains[0],
        query_grad,
        key_grad,
        value_grad,
        output_grad,
        table_grad.T,
        gains[1],
        router_grad.T,
        ups,
        downs,
    )


def solution(mesh):
    placed = (
        P("exp", "ctx", None),
        P("exp", "ctx"),
        P(),
        P("exp", "ctx", None),
        P(),
        P(),
        P(),
        P(),
        P(),
        P(),
        P(),
        P(),
        P("ctx", "exp", None),
        P("ctx", "exp", None),
        P("exp", "ctx", None),
    )
    return jax.shard_map(
        on_device,
        mesh=mesh,
        in_specs=placed,
        out_specs=(
            P("exp", "ctx", None),
            P("exp", "ctx", None),
            P(),
            P(),
            P(),
            P(),
            P(),
            P(),
            P(),
            P(),
            P("ctx", "exp", None),
            P("ctx", "exp", None),
        ),
        check_vma=False,
    )
```
